256 devices in a mesh: seq: 32 (over x, y, z_lo), chan: 8 (over z_hi, core).
Axes of the slice: x: 4, y: 4, z: 8 (z_hi: 4, z_lo: 2; z = z_hi * 2 + z_lo), core: 2. Of those that a mesh axis runs over, the one named last changes fastest.
Arguments:
- gate_feat: bfloat16 [8192, 4096], P('seq', 'chan'), may hold values from -30 to 30
- key_feat: bfloat16 [8192, 4096], P('seq', 'chan'), may hold values from -5 to 5
- value_feat: bfloat16 [8192, 4096], P('seq', 'chan'), may hold values from -5 to 5
- filter_taps: bfloat16 [8192, 4096], P('seq', 'chan'), may hold values from -0.0625 to 0.0625
- skip_bias: float32 [4096], P('chan'), may hold values from 0.5 to 1.5
- norm_gain: float32 [4096], P('chan'), may hold values from 0.25 to 1.75
- cotangent: bfloat16 [8192, 4096], P('seq', 'chan'), may hold values from -5 to 5
Outputs:
- normed_out: bfloat16 [8192, 4096], P('seq', 'chan')
- grad_gate: bfloat16 [8192, 4096], P('seq', 'chan')
- grad_key: bfloat16 [8192, 4096], P('seq', 'chan')
- grad_value: bfloat16 [8192, 4096], P('seq', 'chan')
- grad_filter: bfloat16 [8192, 4096], P('seq', 'chan')
- grad_bias: float32 [4096], P('chan')
The draws below stay inside these ranges and needn't reach their ends.
All inputs are finite; a program needn't handle non-finite values.
Results may differ from the reference program's by a relative error of at most 0.015.
Values may be sent and summed in bfloat16 or wider, within the bound.
No kernel may reach another device: no remote copies, remote signals or barrier semaphores. Data moves between devices by JAX's collectives and lax.ppermute only.
A program may use at most 64 MiB of HBM per device.

```python
import jax
import jax.numpy as jnp
from jax import lax

D = 4096
LENGTH = 8192


def draw_gate_feat(key, part):
    key = jax.random.fold_in(key, 7)
    column = jnp.arange(D, dtype=jnp.float32) / D
    key_noise = jax.random.fold_in(key, 0)
    noise_base = jnp.clip(jax.random.normal(key_noise, (LENGTH, D), jnp.float32), -5.0, 5.0)
    values = noise_base * (0.6 * 3.0 ** column)[None, :]
    return values.astype(jnp.bfloat16)


def block_levels(rng, shape, cuts, least, top_value):
    level, own = 1.0, jax.random.fold_in(rng, 6)
    for axis_at, parts in cuts:
        draws = jnp.exp(jax.random.uniform(jax.random.fold_in(own, axis_at), (parts,), jnp.float32, least / len(cuts), top_value / len(cuts)))
        level = level * jnp.repeat(draws, shape[axis_at] // parts).reshape([-1 if axis == axis_at else 1 for axis in range(len(shape))])
    return level


def centred(own_key, shape, scale, reach, cuts=(), kind=jnp.bfloat16):
    loudness = block_levels(own_key, shape, cuts, -0.22, 0.18) if cuts else 1.0
    drawn = jax.random.normal(own_key, shape, jnp.float32) * scale * loudness
    return jnp.minimum(jnp.maximum(drawn, -reach), reach).astype(kind)


def setup_inputs(seed: int = 0) -> dict:
    seeds = jax.random.split(jax.random.key(seed), 8)
    gate_feat = draw_gate_feat(jax.random.fold_in(seeds[7], 71), 0)
    key_feat = centred(seeds[1], (LENGTH, D), 1.0, 5.0, ((0, 32), (1, 8)))
    value_feat = centred(seeds[2], (LENGTH, D), 1.0, 5.0, ((0, 32), (1, 8)))
    filter_taps = centred(seeds[3], (LENGTH, D), LENGTH ** -0.5, 0.0625, ((0, 32), (1, 8)))
    skip_bias = jnp.clip(0.5 + 1.0 * jax.random.uniform(seeds[4], (D,), jnp.float32) ** block_levels(seeds[4], (D,), ((0, 8),), -0.2, 0.2), 0.5, 1.5)
    norm_gain = jnp.clip(1.0 + 0.15 * jax.random.normal(seeds[5], (D,), jnp.float32), 0.25, 1.75)
    cotangent = centred(seeds[6], (LENGTH, D), 1.0, 5.0, ((0, 32), (1, 8)))
    return dict(gate_feat=gate_feat, key_feat=key_feat, value_feat=value_feat, filter_taps=filter_taps, skip_bias=skip_bias, norm_gain=norm_gain, cotangent=cotangent)


epsilon = 1e-05

def reference(gate_feat, key_feat, value_feat, filter_taps, skip_bias, norm_gain, cotangent):
    full_count = 2 * LENGTH
    mixed = (key_feat.astype(jnp.float32) * value_feat.astype(jnp.float32)).astype(jnp.bfloat16)
    mixed_wide = mixed.astype(jnp.float32)
    spec_mixed = jnp.fft.rfft(mixed_wide, n=full_count, axis=0)
    spec_filter = jnp.fft.rfft(filter_taps.astype(jnp.float32), n=full_count, axis=0)
    conv_out = jnp.fft.irfft(spec_mixed * spec_filter, n=full_count, axis=0)[:LENGTH].astype(jnp.bfloat16)
    full = conv_out.astype(jnp.float32) + skip_bias[None, :] * mixed_wide
    gated = gate_feat.astype(jnp.float32) * full
    inv_rms = lax.rsqrt(lax.optimization_barrier(jnp.mean(gated * gated, axis=1, keepdims=True)) + epsilon)
    normed_out = (gated * inv_rms * norm_gain[None, :]).astype(jnp.bfloat16)
    scaled_grad = cotangent.astype(jnp.float32) * norm_gain[None, :]
    row_inner = lax.optimization_barrier(jnp.sum(scaled_grad * gated, axis=1, keepdims=True))
    grad_gated = inv_rms * scaled_grad - gated * inv_rms ** 3 * row_inner / D
    grad_gate = (grad_gated * full).astype(jnp.bfloat16)
    grad_conv = (grad_gated * gate_feat.astype(jnp.float32)).astype(jnp.bfloat16)
    grad_wide = grad_conv.astype(jnp.float32)
    grad_bias = lax.optimization_barrier(jnp.sum(grad_wide * mixed_wide, axis=0))
    spec_grad = jnp.fft.rfft(grad_wide, n=full_count, axis=0)
    grad_mixed_conv = jnp.fft.irfft(jnp.conj(spec_filter) * spec_grad, n=full_count, axis=0)[:LENGTH].astype(jnp.bfloat16)
    grad_filter = jnp.fft.irfft(jnp.conj(spec_mixed) * spec_grad, n=full_count, axis=0)[:LENGTH].astype(jnp.bfloat16)
    grad_mixed = grad_mixed_conv.astype(jnp.float32) + skip_bias[None, :] * grad_wide
    grad_key = (grad_mixed * value_feat.astype(jnp.float32)).astype(jnp.bfloat16)
    grad_value = (grad_mixed * key_feat.astype(jnp.float32)).astype(jnp.bfloat16)
    return (normed_out, grad_gate, grad_key, grad_value, grad_filter, grad_bias)
```

```python
import functools

import jax
import jax.numpy as jnp
import numpy as np
from jax import lax
from jax.experimental import pallas as pl
from jax.experimental.pallas import tpu as pltpu
from jax.sharding import PartitionSpec as P

D = 4096
LENGTH = 8192
epsilon = 1e-05

f32, bf16 = jnp.float32, jnp.bfloat16

PARTS = 32
GROUP = 8
BLOCK = LENGTH // PARTS
WIDTH = D // GROUP
PIECE = WIDTH // PARTS
HALF = PIECE // 2
FULL = 2 * LENGTH
SPAN = 2 * PARTS
BINS = PARTS + 1
ROWS = BINS * PIECE
TAIL = 16


def tables():
    low = np.array(list(range(1, PARTS)) + [0, PARTS])
    block, inside = np.arange(PARTS), np.arange(BLOCK)
    outer = 2 * np.pi * (low[:, None] * block[None, :] % SPAN) / SPAN
    cosine, sine = np.cos(outer), np.sin(outer)
    eye = np.eye(HALF)
    enter = np.kron(np.concatenate([cosine, -sine[: PARTS - 1]], 0), eye)
    weight = np.where((low == 0) | (low == PARTS), 1.0, 2.0)[:, None] / 4
    leave = np.kron(np.concatenate([cosine * weight, (sine * weight)[: PARTS - 1]], 0).T, eye)
    turn = 2 * np.pi * (low[:, None] * inside[None, :] % FULL) / FULL
    turn = np.stack([np.repeat(np.cos(turn), HALF, 0), np.repeat(-np.sin(turn), HALF, 0)])
    inner = 2 * np.pi * (inside[:, None] * inside[None, :] % BLOCK) / BLOCK
    cosine, sine = np.cos(inner) / 16, -np.sin(inner) / 16
    inner = np.block([[cosine, sine], [-sine, cosine]])
    return (
        enter.astype(np.float32).astype(bf16),
        leave.astype(np.float32).astype(bf16),
        inner.astype(np.float32).astype(bf16),
        turn.astype(np.float32),
    )


def dot(first, second):
    return jnp.dot(first, second, preferred_element_type=f32)


def rotate(real, imag, turn):
    cosine, sine = turn[0], turn[1]
    own = imag.shape[0]
    turned_re = jnp.concatenate(
        [real[:own] * cosine[:own] - imag * sine[:own], real[own:] * cosine[own:]], 0
    )
    turned_im = jnp.concatenate(
        [real[:own] * sine[:own] + imag * cosine[:own], real[own:] * sine[own:]], 0
    )
    return turned_re, turned_im


def join(halves):
    parts = [half.reshape(BINS, HALF, BLOCK) for half in halves]
    return jnp.concatenate(parts, 1).reshape(ROWS, BLOCK)


def spectrum(signal, enter, inner, turn):
    wide = signal.astype(f32)
    reals, imags = [], []
    for half in range(2):
        rows = wide[:, half * HALF : (half + 1) * HALF].reshape(PARTS * HALF, BLOCK)
        mixed = dot(enter, rows.astype(bf16))
        real, imag = rotate(mixed[: BINS * HALF], mixed[BINS * HALF :], turn)
        reals.append(real)
        imags.append(imag)
    both = jnp.concatenate([join(reals).astype(bf16), join(imags).astype(bf16)], 1)
    return dot(both, inner)


def invert(real, imag, leave, inner, turn):
    back = dot(jnp.concatenate([real.astype(bf16), imag.astype(bf16)], 1), inner)
    back = back.reshape(BINS, PIECE, 2 * BLOCK)
    outs = []
    for half in range(2):
        rows = back[:, half * HALF : (half + 1) * HALF].reshape(BINS * HALF, 2 * BLOCK)
        real, imag = rows[:, :BLOCK], rows[:, BLOCK:]
        own = (BINS - 2) * HALF
        turned_re = real * turn[0] - imag * turn[1]
        turned_im = real[:own] * turn[1][:own] + imag[:own] * turn[0][:own]
        turned = jnp.concatenate([turned_re, turned_im], 0).astype(bf16)
        outs.append(dot(leave, turned).reshape(PARTS, HALF, BLOCK))
    return jnp.concatenate(outs, 1)


def flat(pieces):
    return pieces.reshape(WIDTH, BLOCK)


def cut(rows):
    return rows.reshape(PARTS, PIECE, BLOCK)


def pack_kernel(key_ref, value_ref, taps_ref, out_ref):
    mixed = (key_ref[...].astype(f32) * value_ref[...].astype(f32)).astype(bf16)
    out_ref[:, :PIECE, :] = cut(mixed.T)
    out_ref[:, PIECE:, :] = cut(taps_ref[...].T)


def side_kernel(gate_ref, cot_ref, skip_ref, gain_ref, gate_out, cot_out, skip_out, gain_out):
    gate_out[...] = gate_ref[...].T
    cot_out[...] = cot_ref[...].T
    skip_out[...] = jnp.broadcast_to(skip_ref[...], (128, WIDTH)).T
    gain_out[...] = jnp.broadcast_to(gain_ref[...], (128, WIDTH)).T


def forward_kernel(in_ref, enter_ref, leave_ref, inner_ref, turn_ref, out_ref, spec_ref):
    enter, leave, inner = enter_ref[...], leave_ref[...], inner_ref[...]
    turn = (turn_ref[0], turn_ref[1])
    first = spectrum(in_ref[:, :PIECE, :], enter, inner, turn)
    spec_ref[0] = first.astype(bf16)
    second = spectrum(in_ref[:, PIECE:, :], enter, inner, turn)
    spec_ref[1] = second.astype(bf16)
    first_re, first_im = first[:, :BLOCK], first[:, BLOCK:]
    second_re, second_im = second[:, :BLOCK], second[:, BLOCK:]
    real = first_re * second_re - first_im * second_im
    imag = -(first_re * second_im + first_im * second_re)
    out_ref[...] = invert(real, imag, leave, inner, turn).astype(bf16)


def wide_twice(column):
    return jnp.concatenate([column, column], 1)


def gate_parts(conv_ref, pack_ref, gate_ref, skip_ref):
    mixed = flat(pack_ref[:, :PIECE, :]).astype(f32)
    full = flat(conv_ref[...]).astype(f32) + wide_twice(skip_ref[...]) * mixed
    gate = gate_ref[...].astype(f32)
    return full, gate, gate * full


def sums_kernel(conv_ref, pack_ref, gate_ref, cot_ref, skip_ref, gain_ref, out_ref):
    _, _, gated = gate_parts(conv_ref, pack_ref, gate_ref, skip_ref)
    scaled = cot_ref[...].astype(f32) * wide_twice(gain_ref[...])
    squares = jnp.sum(gated * gated, axis=0, keepdims=True)
    inner = jnp.sum(scaled * gated, axis=0, keepdims=True)
    both = jnp.concatenate([squares, inner], 0)
    out_ref[...] = jnp.broadcast_to(both[None], (GROUP, 2, BLOCK))


def norm_parts(sums_ref):
    sums = jnp.sum(sums_ref[...], axis=0)
    inv_rms = lax.rsqrt(sums[0:1] / D + epsilon)
    return inv_rms, inv_rms * inv_rms * inv_rms * sums[1:2] / D


def grad_kernel(sums_ref, conv_ref, pack_ref, gate_ref, cot_ref, skip_ref, gain_ref, out_ref):
    inv_rms, pull = norm_parts(sums_ref)
    _, gate, gated = gate_parts(conv_ref, pack_ref, gate_ref, skip_ref)
    scaled = cot_ref[...].astype(f32) * wide_twice(gain_ref[...])
    grad_gated = inv_rms * scaled - gated * pull
    out_ref[...] = cut((grad_gated * gate).astype(bf16))


def norm_kernel(
    sums_ref, conv_ref, pack_ref, gate_ref, cot_ref, skip_ref, gain_ref, grad_ref, normed_out, gate_out, grad_out
):
    inv_rms, pull = norm_parts(sums_ref)
    full, _, gated = gate_parts(conv_ref, pack_ref, gate_ref, skip_ref)
    gain = wide_twice(gain_ref[...])
    normed_out[...] = (gated * inv_rms * gain).astype(bf16).T
    grad_gated = inv_rms * (cot_ref[...].astype(f32) * gain) - gated * pull
    gate_out[...] = (grad_gated * full).astype(bf16).T
    grad_out[...] = flat(grad_ref[...]).T


def backward_kernel(in_ref, pack_ref, spec_ref, enter_ref, leave_ref, inner_ref, turn_ref, out_ref):
    enter, leave, inner = enter_ref[...], leave_ref[...], inner_ref[...]
    turn = (turn_ref[0], turn_ref[1])
    grad = in_ref[...]
    bias = jnp.sum(grad.astype(f32) * pack_ref[:, :PIECE, :].astype(f32), axis=0)
    bias = jnp.sum(bias, axis=1, keepdims=True)
    high = bias.astype(bf16).astype(f32)
    lane = lax.broadcasted_iota(jnp.int32, (PIECE, 128), 1)
    bias = jnp.where(lane == 0, high, jnp.where(lane == 1, bias - high, 0.0)).astype(bf16)
    out_ref[:, 4 * PIECE :, :] = jnp.broadcast_to(bias[None], (PARTS, TAIL, 128))
    grad = spectrum(grad, enter, inner, turn)
    grad_re, grad_im = grad[:, :BLOCK], grad[:, BLOCK:]
    for place, other in ((0, 1), (1, 0)):
        real, imag = spec_ref[other, :, :BLOCK].astype(f32), spec_ref[other, :, BLOCK:].astype(f32)
        result = invert(
            real * grad_re + imag * grad_im, imag * grad_re - real * grad_im, leave, inner, turn
        ).astype(bf16)
        out_ref[:, 2 * place * PIECE : (2 * place + 1) * PIECE, :] = result[:, :, :128]
        out_ref[:, (2 * place + 1) * PIECE : (2 * place + 2) * PIECE, :] = result[:, :, 128:]


def last_kernel(in_ref, grad_ref, key_ref, value_ref, skip_ref, key_out, value_out, taps_out, bias_out):
    def whole(place):
        at = 2 * place * PIECE
        left, right = in_ref[:, at : at + PIECE, :], in_ref[:, at + PIECE : at + 2 * PIECE, :]
        return jnp.concatenate([left.reshape(WIDTH, 128).T, right.reshape(WIDTH, 128).T], 0)

    grad_mixed = whole(0).astype(f32) + skip_ref[...] * grad_ref[...].astype(f32)
    key_out[...] = (grad_mixed * value_ref[...].astype(f32)).astype(bf16)
    value_out[...] = (grad_mixed * key_ref[...].astype(f32)).astype(bf16)
    taps_out[...] = whole(1)
    bias = in_ref[:, 4 * PIECE :, :].reshape(WIDTH, 128).astype(f32).T
    bias_out[...] = bias[0:1] + bias[1:2]


def call(kernel, name, outs, *operands):
    return pl.pallas_call(
        kernel,
        name=name,
        out_shape=[jax.ShapeDtypeStruct(shape, kind) for shape, kind in outs],
        compiler_params=pltpu.CompilerParams(vmem_limit_bytes=40 * 1024 * 1024),
    )(*operands)


def on_device(gate_feat, key_feat, value_feat, filter_taps, skip_bias, norm_gain, cotangent):
    enter, leave, inner, turn = (jnp.asarray(table) for table in tables())
    skip_row, gain_row = skip_bias[None, :], norm_gain[None, :]
    natural = ((BLOCK, WIDTH), bf16)
    turned = ((WIDTH, BLOCK), bf16)
    column = ((WIDTH, 128), f32)
    pieces = ((PARTS, PIECE, BLOCK), bf16)

    (packed,) = call(pack_kernel, "pack", [((PARTS, 2 * PIECE, BLOCK), bf16)], key_feat, value_feat, filter_taps)
    arrived = lax.all_to_all(packed, "seq", 0, 0, tiled=True)
    gate_t, cot_t, skip_t, gain_t = call(
        side_kernel, "side", [turned, turned, column, column], gate_feat, cotangent, skip_row, gain_row
    )
    conv, spec = call(
        forward_kernel, "forward", [pieces, ((2, ROWS, 2 * BLOCK), bf16)], arrived, enter, leave, inner, turn
    )
    conv = lax.all_to_all(conv, "seq", 0, 0, tiled=True)
    sides = (conv, packed, gate_t, cot_t, skip_t, gain_t)
    (sums,) = call(sums_kernel, "sums", [((GROUP, 2, BLOCK), f32)], *sides)
    sums = lax.all_to_all(sums, "chan", 0, 0, tiled=True)
    (grad,) = call(grad_kernel, "grad", [pieces], sums, *sides)
    grad_arrived = lax.all_to_all(grad, "seq", 0, 0, tiled=True)
    normed_out, grad_gate, grad_conv = call(norm_kernel, "norm", [natural] * 3, sums, *sides, grad)
    (result,) = call(
        backward_kernel,
        "backward",
        [((PARTS, 4 * PIECE + TAIL, 128), bf16)],
        grad_arrived,
        arrived,
        spec,
        enter,
        leave,
        inner,
        turn,
    )
    result = lax.all_to_all(result, "seq", 0, 0, tiled=True)
    grad_key, grad_value, grad_filter, grad_bias = call(
        last_kernel,
        "last",
        [natural] * 3 + [((1, WIDTH), f32)],
        result,
        grad_conv,
        key_feat,
        value_feat,
        skip_row,
    )
    return normed_out, grad_gate, grad_key, grad_value, grad_filter, grad_bias[0]


def solution(mesh):
    wide, row = P("seq", "chan"), P("chan")
    return jax.shard_map(
        on_device,
        mesh=mesh,
        in_specs=(wide, wide, wide, wide, row, row, wide),
        out_specs=(wide, wide, wide, wide, wide, row),
        check_vma=False,
    )
```

```python
import jax
import jax.numpy as jnp
import numpy as np
from jax import lax
from jax.experimental import pallas as pl
from jax.experimental.pallas import tpu as pltpu
from jax.sharding import PartitionSpec as P

D = 4096
LENGTH = 8192
epsilon = 1e-05

f32, bf16 = jnp.float32, jnp.bfloat16

PARTS = 32
GROUP = 8
BLOCK = LENGTH // PARTS
WIDTH = D // GROUP
PIECE = WIDTH // PARTS
HALF = PIECE // 2
FULL = 2 * LENGTH
SPAN = 2 * PARTS
BINS = PARTS + 1
ROWS = BINS * PIECE
TAIL = 8
CHIPS = GROUP // 2


def tables():
    low = np.array(list(range(1, PARTS)) + [0, PARTS])
    block, inside = np.arange(PARTS), np.arange(BLOCK)
    outer = 2 * np.pi * (low[:, None] * block[None, :] % SPAN) / SPAN
    cosine, sine = np.cos(outer), np.sin(outer)
    eye = np.eye(HALF)
    enter = np.kron(np.concatenate([cosine, -sine[: PARTS - 1]], 0), eye)
    weight = np.where((low == 0) | (low == PARTS), 1.0, 2.0)[:, None] / 4
    leave = np.kron(np.concatenate([cosine * weight, (sine * weight)[: PARTS - 1]], 0).T, eye)
    turn = 2 * np.pi * (low[:, None] * inside[None, :] % FULL) / FULL
    turn = np.stack([np.repeat(np.cos(turn), HALF, 0), np.repeat(-np.sin(turn), HALF, 0)])
    inner = 2 * np.pi * (inside[:, None] * inside[None, :] % BLOCK) / BLOCK
    cosine, sine = np.cos(inner) / 16, -np.sin(inner) / 16
    inner = np.block([[cosine, sine], [-sine, cosine]])
    return (
        enter.astype(np.float32).astype(bf16),
        leave.astype(np.float32).astype(bf16),
        inner.astype(np.float32).astype(bf16),
        turn.astype(np.float32),
    )


def dot(first, second):
    return jnp.dot(first, second, preferred_element_type=f32)


def rotate(real, imag, turn):
    cosine, sine = turn[0], turn[1]
    own = imag.shape[0]
    turned_re = jnp.concatenate(
        [real[:own] * cosine[:own] - imag * sine[:own], real[own:] * cosine[own:]], 0
    )
    turned_im = jnp.concatenate(
        [real[:own] * sine[:own] + imag * cosine[:own], real[own:] * sine[own:]], 0
    )
    return turned_re, turned_im


def join(halves):
    parts = [half.reshape(BINS, HALF, BLOCK) for half in halves]
    return jnp.concatenate(parts, 1).reshape(ROWS, BLOCK)


def spectrum(signal, enter, inner, turn):
    wide = signal.astype(f32)
    reals, imags = [], []
    for half in range(2):
        rows = wide[:, half * HALF : (half + 1) * HALF].reshape(PARTS * HALF, BLOCK)
        mixed = dot(enter, rows.astype(bf16))
        real, imag = rotate(mixed[: BINS * HALF], mixed[BINS * HALF :], turn)
        reals.append(real)
        imags.append(imag)
    both = jnp.concatenate([join(reals).astype(bf16), join(imags).astype(bf16)], 1)
    return dot(both, inner)


def invert(real, imag, leave, inner, turn):
    back = dot(jnp.concatenate([real.astype(bf16), imag.astype(bf16)], 1), inner)
    back = back.reshape(BINS, PIECE, 2 * BLOCK)
    outs = []
    for half in range(2):
        rows = back[:, half * HALF : (half + 1) * HALF].reshape(BINS * HALF, 2 * BLOCK)
        real, imag = rows[:, :BLOCK], rows[:, BLOCK:]
        own = (BINS - 2) * HALF
        turned_re = real * turn[0] - imag * turn[1]
        turned_im = real[:own] * turn[1][:own] + imag[:own] * turn[0][:own]
        turned = jnp.concatenate([turned_re, turned_im], 0).astype(bf16)
        outs.append(dot(leave, turned).reshape(PARTS, HALF, BLOCK))
    return jnp.concatenate(outs, 1)


def flat(pieces):
    return pieces.reshape(WIDTH, BLOCK)


def cut(rows):
    return rows.reshape(PARTS, PIECE, BLOCK)


def pack_kernel(key_hbm, value_hbm, taps_hbm, out_ref, key_ref, value_ref, taps_ref, sems):
    copies = [
        pltpu.make_async_copy(source, target, sems.at[place])
        for place, (source, target) in enumerate(
            ((key_hbm, key_ref), (value_hbm, value_ref), (taps_hbm, taps_ref))
        )
    ]
    for copy in copies:
        copy.start()
    copies[0].wait()
    copies[1].wait()
    mixed = (key_ref[...].astype(f32) * value_ref[...].astype(f32)).astype(bf16)
    out_ref[:, :PIECE, :] = cut(mixed.T)
    copies[2].wait()
    out_ref[:, PIECE:, :] = cut(taps_ref[...].T)


def side_kernel(gate_ref, cot_ref, skip_ref, gain_ref, gate_out, cot_out, skip_out, gain_out):
    gate_out[...] = gate_ref[...].T
    cot_out[...] = cot_ref[...].T
    skip_out[...] = jnp.broadcast_to(skip_ref[...], (128, WIDTH)).T
    gain_out[...] = jnp.broadcast_to(gain_ref[...], (128, WIDTH)).T


def forward_kernel(in_ref, enter_ref, leave_ref, inner_ref, turn_ref, out_ref, spec_hbm, spec_ref, sems):
    enter, leave, inner = enter_ref[...], leave_ref[...], inner_ref[...]
    turn = (turn_ref[0], turn_ref[1])
    spectra, copies = [], []
    for place in range(2):
        signal = in_ref[:, place * PIECE : (place + 1) * PIECE, :]
        spectra.append(spectrum(signal, enter, inner, turn))
        spec_ref[place] = spectra[place].astype(bf16)
        copies.append(pltpu.make_async_copy(spec_ref.at[place], spec_hbm.at[place], sems.at[place]))
        copies[place].start()
    first_re, first_im = spectra[0][:, :BLOCK], spectra[0][:, BLOCK:]
    second_re, second_im = spectra[1][:, :BLOCK], spectra[1][:, BLOCK:]
    real = first_re * second_re - first_im * second_im
    imag = -(first_re * second_im + first_im * second_re)
    out_ref[...] = invert(real, imag, leave, inner, turn).astype(bf16)
    for copy in copies:
        copy.wait()


def wide_twice(column):
    return jnp.concatenate([column, column], 1)


def gate_parts(conv_ref, pack_ref, gate_ref, skip_ref):
    mixed = flat(pack_ref[:, :PIECE, :]).astype(f32)
    full = flat(conv_ref[...]).astype(f32) + wide_twice(skip_ref[...]) * mixed
    gate = gate_ref[...].astype(f32)
    return full, gate, gate * full


def sums_kernel(conv_ref, pack_ref, gate_ref, cot_ref, skip_ref, gain_ref, out_ref):
    _, _, gated = gate_parts(conv_ref, pack_ref, gate_ref, skip_ref)
    scaled = cot_ref[...].astype(f32) * wide_twice(gain_ref[...])
    squares = jnp.sum(gated * gated, axis=0, keepdims=True)
    inner = jnp.sum(scaled * gated, axis=0, keepdims=True)
    out_ref[...] = jnp.concatenate([squares, inner], 0)


def norm_parts(sums_ref):
    sums = sums_ref[...]
    inv_rms = lax.rsqrt(sums[0:1] / D + epsilon)
    return inv_rms, inv_rms * inv_rms * inv_rms * sums[1:2] / D


def grad_kernel(sums_ref, conv_ref, pack_ref, gate_ref, cot_ref, skip_ref, gain_ref, out_ref):
    inv_rms, pull = norm_parts(sums_ref)
    _, gate, gated = gate_parts(conv_ref, pack_ref, gate_ref, skip_ref)
    scaled = cot_ref[...].astype(f32) * wide_twice(gain_ref[...])
    grad_gated = inv_rms * scaled - gated * pull
    out_ref[...] = cut((grad_gated * gate).astype(bf16))


def norm_kernel(
    sums_ref, conv_ref, pack_ref, gate_ref, cot_ref, skip_ref, gain_ref, grad_ref, row_ref,
    normed_out, gate_out, grad_out, row_out,
):
    inv_rms, pull = norm_parts(sums_ref)
    full, _, gated = gate_parts(conv_ref, pack_ref, gate_ref, skip_ref)
    gain = wide_twice(gain_ref[...])
    normed_out[...] = (gated * inv_rms * gain).astype(bf16).T
    grad_gated = inv_rms * (cot_ref[...].astype(f32) * gain) - gated * pull
    gate_out[...] = (grad_gated * full).astype(bf16).T
    grad_out[...] = flat(grad_ref[...]).T
    row_out[...] = row_ref[...]


def backward_kernel(in_ref, pack_ref, spec_ref, enter_ref, leave_ref, inner_ref, turn_ref, out_ref):
    enter, leave, inner = enter_ref[...], leave_ref[...], inner_ref[...]
    turn = (turn_ref[0], turn_ref[1])
    grad = in_ref[...]
    bias = jnp.sum(grad.astype(f32) * pack_ref[:, :PIECE, :].astype(f32), axis=0)
    bias = jnp.sum(bias, axis=1, keepdims=True)
    high = bias.astype(bf16).astype(f32)
    lane = lax.broadcasted_iota(jnp.int32, (TAIL, 128), 1)
    tail = jnp.zeros((TAIL, 128), f32)
    for at, part in enumerate((high[:HALF], (bias - high)[:HALF], high[HALF:], (bias - high)[HALF:])):
        tail = jnp.where(lane == at, part, tail)
    out_ref[:, 4 * PIECE :, :] = jnp.broadcast_to(tail.astype(bf16)[None], (PARTS, TAIL, 128))
    grad = spectrum(grad, enter, inner, turn)
    grad_re, grad_im = grad[:, :BLOCK], grad[:, BLOCK:]
    for place, other in ((0, 1), (1, 0)):
        real, imag = spec_ref[other, :, :BLOCK].astype(f32), spec_ref[other, :, BLOCK:].astype(f32)
        result = invert(
            real * grad_re + imag * grad_im, imag * grad_re - real * grad_im, leave, inner, turn
        ).astype(bf16)
        out_ref[:, 2 * place * PIECE : (2 * place + 1) * PIECE, :] = result[:, :, :128]
        out_ref[:, (2 * place + 1) * PIECE : (2 * place + 2) * PIECE, :] = result[:, :, 128:]


def last_kernel(
    in_ref, grad_ref, key_ref, value_ref, skip_ref,
    key_hbm, value_hbm, taps_hbm, bias_out, key_out, value_out, taps_out, sems,
):
    copies = []

    def send(source, target, half):
        rows = pl.ds(half * 128, 128)
        copies.append(pltpu.make_async_copy(source.at[rows], target.at[rows], sems.at[len(copies)]))
        copies[-1].start()

    for half in range(2):
        rows = pl.ds(half * 128, 128)
        at = half * PIECE
        taps_out[rows, :] = in_ref[:, 2 * PIECE + at : 3 * PIECE + at, :].reshape(WIDTH, 128).T
        send(taps_out, taps_hbm, half)
        mixed = in_ref[:, at : at + PIECE, :].reshape(WIDTH, 128).T.astype(f32)
        mixed = mixed + skip_ref[...] * grad_ref[rows, :].astype(f32)
        key_out[rows, :] = (mixed * value_ref[rows, :].astype(f32)).astype(bf16)
        send(key_out, key_hbm, half)
        value_out[rows, :] = (mixed * key_ref[rows, :].astype(f32)).astype(bf16)
        send(value_out, value_hbm, half)
    tail = in_ref[:, 4 * PIECE :, :].astype(f32)
    tail = jnp.concatenate([tail, pltpu.roll(tail, 126, 2)], 1).reshape(WIDTH, 128).T
    bias_out[...] = tail[0:1] + tail[1:2]
    for copy in copies:
        copy.wait()


def call(kernel, name, outs, *operands, hbm_in=(), hbm_out=(), scratch=()):
    vmem, hbm = pl.BlockSpec(memory_space=pltpu.VMEM), pl.BlockSpec(memory_space=pltpu.HBM)
    return pl.pallas_call(
        kernel,
        name=name,
        out_shape=[jax.ShapeDtypeStruct(shape, kind) for shape, kind in outs],
        in_specs=[hbm if place in hbm_in else vmem for place in range(len(operands))],
        out_specs=[hbm if place in hbm_out else vmem for place in range(len(outs))],
        scratch_shapes=list(scratch),
        compiler_params=pltpu.CompilerParams(vmem_limit_bytes=32 * 1024 * 1024),
    )(*operands)


def add_over_chan(sums):
    sums = sums + lax.ppermute(sums, "chan", [(at, at ^ 1) for at in range(GROUP)])
    sums = sums + lax.ppermute(sums, "chan", [(at, at ^ 2) for at in range(GROUP)])
    mirror = [(at, (CHIPS - 1 - at // 2) * 2 + at % 2) for at in range(GROUP)]
    return sums + lax.ppermute(sums, "chan", mirror)


def on_device(gate_feat, key_feat, value_feat, filter_taps, skip_bias, norm_gain, cotangent):
    enter, leave, inner, turn = (jnp.asarray(table) for table in tables())
    skip_row, gain_row = skip_bias[None, :], norm_gain[None, :]
    natural = ((BLOCK, WIDTH), bf16)
    turned = ((WIDTH, BLOCK), bf16)
    column = ((WIDTH, 128), f32)
    pieces = ((PARTS, PIECE, BLOCK), bf16)
    spectra = ((2, ROWS, 2 * BLOCK), bf16)
    whole = pltpu.VMEM(*natural)

    (packed,) = call(
        pack_kernel,
        "pack",
        [((PARTS, 2 * PIECE, BLOCK), bf16)],
        key_feat,
        value_feat,
        filter_taps,
        hbm_in=(0, 1, 2),
        scratch=[whole, whole, whole, pltpu.SemaphoreType.DMA((3,))],
    )
    arrived = lax.all_to_all(packed, "seq", 0, 0, tiled=True)
    gate_t, cot_t, skip_t, gain_t = call(
        side_kernel, "side", [turned, turned, column, column], gate_feat, cotangent, skip_row, gain_row
    )
    conv, spec = call(
        forward_kernel,
        "forward",
        [pieces, spectra],
        arrived,
        enter,
        leave,
        inner,
        turn,
        hbm_out=(1,),
        scratch=[pltpu.VMEM(*spectra), pltpu.SemaphoreType.DMA((2,))],
    )
    conv = lax.all_to_all(conv, "seq", 0, 0, tiled=True)
    sides = (conv, packed, gate_t, cot_t, skip_t, gain_t)
    (sums,) = call(sums_kernel, "sums", [((2, BLOCK), f32)], *sides)
    sums = add_over_chan(sums)
    (grad,) = call(grad_kernel, "grad", [pieces], sums, *sides)
    grad_arrived = lax.all_to_all(grad, "seq", 0, 0, tiled=True)
    normed_out, grad_gate, grad_conv, skip_row = call(
        norm_kernel, "norm", [natural] * 3 + [((1, WIDTH), f32)], sums, *sides, grad, skip_row
    )
    (result,) = call(
        backward_kernel,
        "backward",
        [((PARTS, 4 * PIECE + TAIL, 128), bf16)],
        grad_arrived,
        arrived,
        spec,
        enter,
        leave,
        inner,
        turn,
    )
    result = lax.all_to_all(result, "seq", 0, 0, tiled=True)
    grad_key, grad_value, grad_filter, grad_bias = call(
        last_kernel,
        "last",
        [natural] * 3 + [((1, WIDTH), f32)],
        result,
        grad_conv,
        key_feat,
        value_feat,
        skip_row,
        hbm_out=(0, 1, 2),
        scratch=[whole, whole, whole, pltpu.SemaphoreType.DMA((6,))],
    )
    return normed_out, grad_gate, grad_key, grad_value, grad_filter, grad_bias[0]


def solution(mesh):
    wide, row = P("seq", "chan"), P("chan")
    return jax.shard_map(
        on_device,
        mesh=mesh,
        in_specs=(wide, wide, wide, wide, row, row, wide),
        out_specs=(wide, wide, wide, wide, wide, row),
        check_vma=False,
    )
```

```python
import jax
import jax.numpy as jnp
import numpy as np
from jax import lax
from jax.experimental import pallas as pl
from jax.experimental.pallas import tpu as pltpu
from jax.sharding import PartitionSpec as P

D = 4096
LENGTH = 8192
epsilon = 1e-05

f32, bf16 = jnp.float32, jnp.bfloat16

PARTS = 32
GROUP = 8
BLOCK = LENGTH // PARTS
WIDTH = D // GROUP
PIECE = WIDTH // PARTS
HALF = PIECE // 2
FULL = 2 * LENGTH
SPAN = 2 * PARTS
BINS = PARTS + 1
ROWS = BINS * PIECE
TAIL = 8
CHIPS = GROUP // 2


def tables():
    low = np.array(list(range(1, PARTS)) + [0, PARTS])
    block, inside = np.arange(PARTS), np.arange(BLOCK)
    outer = 2 * np.pi * (low[:, None] * block[None, :] % SPAN) / SPAN
    cosine, sine = np.cos(outer), np.sin(outer)
    eye = np.eye(HALF)
    enter = np.kron(np.concatenate([cosine, -sine[: PARTS - 1]], 0), eye)
    weight = np.where((low == 0) | (low == PARTS), 1.0, 2.0)[:, None] / 4
    leave = np.kron(np.concatenate([cosine * weight, (sine * weight)[: PARTS - 1]], 0).T, eye)
    turn = 2 * np.pi * (low[:, None] * inside[None, :] % FULL) / FULL
    turn = np.stack([np.cos(turn), -np.sin(turn)])
    inner = 2 * np.pi * (inside[:, None] * inside[None, :] % BLOCK) / BLOCK
    cosine, sine = np.cos(inner) / 16, -np.sin(inner) / 16
    inner = np.block([[cosine, sine], [-sine, cosine]])
    half = SPAN * HALF // 2
    steps = np.concatenate([inner, leave, np.concatenate([enter[:half], enter[half:]], 1)], 0)
    return steps.astype(np.float32).astype(bf16), turn.astype(np.float32)


def open_tables(steps_ref, turn_ref):
    inner, leave, last = 2 * BLOCK, 3 * BLOCK, 4 * BLOCK
    enter = jnp.concatenate([steps_ref[leave:last, :BLOCK], steps_ref[leave:last, BLOCK:]], 0)
    turn = [
        jnp.broadcast_to(turn_ref[part][:, None, :], (BINS, HALF, BLOCK)).reshape(BINS * HALF, BLOCK)
        for part in range(2)
    ]
    return enter, steps_ref[inner:leave, :], steps_ref[:inner, :], turn


def dot(first, second):
    return jnp.dot(first, second, preferred_element_type=f32)


def rotate(real, imag, turn):
    cosine, sine = turn[0], turn[1]
    own = imag.shape[0]
    turned_re = jnp.concatenate(
        [real[:own] * cosine[:own] - imag * sine[:own], real[own:] * cosine[own:]], 0
    )
    turned_im = jnp.concatenate(
        [real[:own] * sine[:own] + imag * cosine[:own], real[own:] * sine[own:]], 0
    )
    return turned_re, turned_im


def join(halves):
    parts = [half.reshape(BINS, HALF, BLOCK) for half in halves]
    return jnp.concatenate(parts, 1).reshape(ROWS, BLOCK)


def spectrum(signal, enter, inner, turn):
    wide = signal.astype(f32)
    reals, imags = [], []
    for half in range(2):
        rows = wide[:, half * HALF : (half + 1) * HALF].reshape(PARTS * HALF, BLOCK)
        mixed = dot(enter, rows.astype(bf16))
        real, imag = rotate(mixed[: BINS * HALF], mixed[BINS * HALF :], turn)
        reals.append(real)
        imags.append(imag)
    both = jnp.concatenate([join(reals).astype(bf16), join(imags).astype(bf16)], 1)
    return dot(both, inner)


def invert(real, imag, leave, inner, turn):
    back = dot(jnp.concatenate([real.astype(bf16), imag.astype(bf16)], 1), inner)
    back = back.reshape(BINS, PIECE, 2 * BLOCK)
    outs = []
    for half in range(2):
        rows = back[:, half * HALF : (half + 1) * HALF].reshape(BINS * HALF, 2 * BLOCK)
        real, imag = rows[:, :BLOCK], rows[:, BLOCK:]
        own = (BINS - 2) * HALF
        turned_re = real * turn[0] - imag * turn[1]
        turned_im = real[:own] * turn[1][:own] + imag[:own] * turn[0][:own]
        turned = jnp.concatenate([turned_re, turned_im], 0).astype(bf16)
        outs.append(dot(leave, turned).reshape(PARTS, HALF, BLOCK))
    return jnp.concatenate(outs, 1)


def flat(pieces):
    return pieces.reshape(WIDTH, BLOCK)


def cut(rows):
    return rows.reshape(PARTS, PIECE, BLOCK)


def pack_kernel(key_hbm, value_hbm, taps_hbm, out_hbm, key_ref, value_ref, taps_ref, out_ref, sems):
    width, parts = WIDTH // 2, PARTS // 2
    loads, stores = [], []
    for half in range(2):
        columns = pl.ds(half * width, width)
        for source, target in ((key_hbm, key_ref), (value_hbm, value_ref), (taps_hbm, taps_ref)):
            loads.append(pltpu.make_async_copy(source.at[:, columns], target.at[:, columns], sems.at[len(loads)]))
            loads[-1].start()
    for half in range(2):
        columns, owners = pl.ds(half * width, width), pl.ds(half * parts, parts)
        loads[3 * half].wait()
        loads[3 * half + 1].wait()
        mixed = key_ref[:, columns].astype(f32) * value_ref[:, columns].astype(f32)
        out_ref[owners, :PIECE, :] = mixed.astype(bf16).T.reshape(parts, PIECE, BLOCK)
        loads[3 * half + 2].wait()
        out_ref[owners, PIECE:, :] = taps_ref[:, columns].T.reshape(parts, PIECE, BLOCK)
        stores.append(pltpu.make_async_copy(out_ref.at[owners], out_hbm.at[owners], sems.at[6 + half]))
        stores[-1].start()
    for store in stores:
        store.wait()


def forward_kernel(
    in_ref, steps_ref, turn_ref, gate_ref, cot_ref, out_ref, gate_out, cot_out
):
    gate_out[...] = gate_ref[...].T
    cot_out[...] = cot_ref[...].T
    enter, leave, inner, turn = open_tables(steps_ref, turn_ref)
    first = spectrum(in_ref[:, :PIECE, :], enter, inner, turn)
    second = spectrum(in_ref[:, PIECE:, :], enter, inner, turn)
    first_re, first_im = first[:, :BLOCK], first[:, BLOCK:]
    second_re, second_im = second[:, :BLOCK], second[:, BLOCK:]
    real = first_re * second_re - first_im * second_im
    imag = -(first_re * second_im + first_im * second_re)
    out_ref[...] = invert(real, imag, leave, inner, turn).astype(bf16)


def spectra_kernel(in_ref, steps_ref, turn_ref, after_ref, spec_ref):
    enter, _, inner, turn = open_tables(steps_ref, turn_ref)
    for place in range(2):
        signal = in_ref[:, place * PIECE : (place + 1) * PIECE, :]
        spec_ref[place] = spectrum(signal, enter, inner, turn).astype(bf16)


def column(row_ref):
    turned = jnp.broadcast_to(row_ref[...], (128, WIDTH)).T
    return jnp.concatenate([turned, turned], 1)


def gate_parts(conv_ref, pack_ref, gate_ref, skip_ref):
    mixed = flat(pack_ref[:, :PIECE, :]).astype(f32)
    full = flat(conv_ref[...]).astype(f32) + column(skip_ref) * mixed
    gate = gate_ref[...].astype(f32)
    return full, gate, gate * full


def sums_kernel(conv_ref, pack_ref, gate_ref, cot_ref, skip_ref, gain_ref, out_ref):
    _, _, gated = gate_parts(conv_ref, pack_ref, gate_ref, skip_ref)
    scaled = cot_ref[...].astype(f32) * column(gain_ref)
    squares = jnp.sum(gated * gated, axis=0, keepdims=True)
    inner = jnp.sum(scaled * gated, axis=0, keepdims=True)
    out_ref[...] = jnp.concatenate([squares, inner], 0)


def norm_parts(sums_ref):
    sums = sums_ref[...]
    inv_rms = lax.rsqrt(sums[0:1] / D + epsilon)
    return inv_rms, inv_rms * inv_rms * inv_rms * sums[1:2] / D


def grad_kernel(sums_ref, conv_ref, pack_ref, gate_ref, cot_ref, skip_ref, gain_ref, out_ref):
    inv_rms, pull = norm_parts(sums_ref)
    _, gate, gated = gate_parts(conv_ref, pack_ref, gate_ref, skip_ref)
    scaled = cot_ref[...].astype(f32) * column(gain_ref)
    grad_gated = inv_rms * scaled - gated * pull
    out_ref[...] = cut((grad_gated * gate).astype(bf16))


def norm_kernel(
    sums_ref, conv_ref, pack_ref, gate_ref, cot_ref, skip_ref, gain_ref,
    normed_out, gate_out, grad_out, skip_out,
):
    inv_rms, pull = norm_parts(sums_ref)
    full, gate, gated = gate_parts(conv_ref, pack_ref, gate_ref, skip_ref)
    gain = column(gain_ref)
    normed_out[...] = (gated * inv_rms * gain).astype(bf16).T
    grad_gated = inv_rms * (cot_ref[...].astype(f32) * gain) - gated * pull
    gate_out[...] = (grad_gated * full).astype(bf16).T
    grad_out[...] = (grad_gated * gate).astype(bf16).T
    skip_out[...] = skip_ref[...]


def backward_kernel(
    in_ref, pack_ref, spec_ref, steps_ref, turn_ref, after_ref, out_ref
):
    enter, leave, inner, turn = open_tables(steps_ref, turn_ref)
    grad = in_ref[...]
    bias = jnp.sum(grad.astype(f32) * pack_ref[:, :PIECE, :].astype(f32), axis=0)
    bias = jnp.sum(bias, axis=1, keepdims=True)
    high = bias.astype(bf16).astype(f32)
    lane = lax.broadcasted_iota(jnp.int32, (TAIL, 128), 1)
    tail = jnp.zeros((TAIL, 128), f32)
    for at, part in enumerate((high[:HALF], (bias - high)[:HALF], high[HALF:], (bias - high)[HALF:])):
        tail = jnp.where(lane == at, part, tail)
    out_ref[:, 4 * PIECE :, :] = jnp.broadcast_to(tail.astype(bf16)[None], (PARTS, TAIL, 128))
    grad = spectrum(grad, enter, inner, turn)
    grad_re, grad_im = grad[:, :BLOCK], grad[:, BLOCK:]
    for place, other in ((0, 1), (1, 0)):
        real, imag = spec_ref[other, :, :BLOCK].astype(f32), spec_ref[other, :, BLOCK:].astype(f32)
        result = invert(
            real * grad_re + imag * grad_im, imag * grad_re - real * grad_im, leave, inner, turn
        ).astype(bf16)
        out_ref[:, 2 * place * PIECE : (2 * place + 1) * PIECE, :] = result[:, :, :128]
        out_ref[:, (2 * place + 1) * PIECE : (2 * place + 2) * PIECE, :] = result[:, :, 128:]


def last_kernel(in_ref, grad_ref, key_ref, value_ref, skip_ref, key_out, value_out, taps_out, bias_out):
    def whole(place):
        at = 2 * place * PIECE
        left, right = in_ref[:, at : at + PIECE, :], in_ref[:, at + PIECE : at + 2 * PIECE, :]
        return jnp.concatenate([left.reshape(WIDTH, 128).T, right.reshape(WIDTH, 128).T], 0)

    grad_mixed = whole(0).astype(f32) + skip_ref[...] * grad_ref[...].astype(f32)
    key_out[...] = (grad_mixed * value_ref[...].astype(f32)).astype(bf16)
    value_out[...] = (grad_mixed * key_ref[...].astype(f32)).astype(bf16)
    taps_out[...] = whole(1)
    tail = in_ref[:, 4 * PIECE :, :].astype(f32)
    tail = jnp.concatenate([tail, pltpu.roll(tail, 126, 2)], 1).reshape(WIDTH, 128).T
    bias_out[...] = tail[0:1] + tail[1:2]


def call(kernel, name, outs, *operands, hbm_in=(), hbm_out=(), scratch=(), grant=32):
    vmem, hbm = pl.BlockSpec(memory_space=pltpu.VMEM), pl.BlockSpec(memory_space=pltpu.HBM)
    return pl.pallas_call(
        kernel,
        name=name,
        out_shape=[jax.ShapeDtypeStruct(shape, kind) for shape, kind in outs],
        in_specs=[hbm if place in hbm_in else vmem for place in range(len(operands))],
        out_specs=[hbm if place in hbm_out else vmem for place in range(len(outs))],
        scratch_shapes=list(scratch),
        compiler_params=pltpu.CompilerParams(vmem_limit_bytes=grant * 1024 * 1024),
    )(*operands)


def add_over_chan(sums):
    sums = sums + lax.ppermute(sums, "chan", [(at, at ^ 1) for at in range(GROUP)])
    sums = sums + lax.ppermute(sums, "chan", [(at, at ^ 2) for at in range(GROUP)])
    mirror = [(at, (CHIPS - 1 - at // 2) * 2 + at % 2) for at in range(GROUP)]
    return sums + lax.ppermute(sums, "chan", mirror)


def on_device(gate_feat, key_feat, value_feat, filter_taps, skip_bias, norm_gain, cotangent):
    steps, turn = (jnp.asarray(table) for table in tables())
    skip_row, gain_row = skip_bias[None, :], norm_gain[None, :]
    natural = ((BLOCK, WIDTH), bf16)
    turned = ((WIDTH, BLOCK), bf16)
    pieces = ((PARTS, PIECE, BLOCK), bf16)
    spectra = ((2, ROWS, 2 * BLOCK), bf16)
    whole = pltpu.VMEM(*natural)

    (packed,) = call(
        pack_kernel,
        "pack",
        [((PARTS, 2 * PIECE, BLOCK), bf16)],
        key_feat,
        value_feat,
        filter_taps,
        hbm_in=(0, 1, 2),
        hbm_out=(0,),
        scratch=[whole, whole, whole, pltpu.VMEM((PARTS, 2 * PIECE, BLOCK), bf16), pltpu.SemaphoreType.DMA((8,))],
        grant=63,
    )
    arrived = lax.all_to_all(packed, "seq", 0, 0, tiled=True)
    conv, gate_t, cot_t = call(
        forward_kernel,
        "forward",
        [pieces, turned, turned],
        arrived,
        steps,
        turn,
        gate_feat,
        cotangent,
    )
    conv = lax.all_to_all(conv, "seq", 0, 0, tiled=True)
    sides = (conv, packed, gate_t, cot_t, skip_row, gain_row)
    (sums,) = call(sums_kernel, "sums", [((2, BLOCK), f32)], *sides)
    sums = add_over_chan(sums)
    (grad,) = call(grad_kernel, "grad", [pieces], sums, *sides)
    grad_arrived = lax.all_to_all(grad, "seq", 0, 0, tiled=True)
    normed_out, grad_gate, grad_conv, skip_row = call(
        norm_kernel, "norm", [natural] * 3 + [((1, WIDTH), f32)], sums, *sides
    )
    (spec,) = call(spectra_kernel, "spectra", [spectra], arrived, steps, turn, skip_row)
    (result,) = call(
        backward_kernel,
        "backward",
        [((PARTS, 4 * PIECE + TAIL, 128), bf16)],
        grad_arrived,
        arrived,
        spec,
        steps,
        turn,
        skip_row,
    )
    result = lax.all_to_all(result, "seq", 0, 0, tiled=True)
    grad_key, grad_value, grad_filter, grad_bias = call(
        last_kernel,
        "last",
        [natural] * 3 + [((1, WIDTH), f32)],
        result,
        grad_conv,
        key_feat,
        value_feat,
        skip_row,
    )
    return normed_out, grad_gate, grad_key, grad_value, grad_filter, grad_bias[0]


def solution(mesh):
    wide, row = P("seq", "chan"), P("chan")
    return jax.shard_map(
        on_device,
        mesh=mesh,
        in_specs=(wide, wide, wide, wide, row, row, wide),
        out_specs=(wide, wide, wide, wide, wide, row),
        check_vma=False,
    )
```

```python
import jax
import jax.numpy as jnp
import numpy as np
from jax import lax
from jax.experimental import pallas as pl
from jax.experimental.pallas import tpu as pltpu
from jax.sharding import PartitionSpec as P

D = 4096
LENGTH = 8192
epsilon = 1e-05

f32, bf16 = jnp.float32, jnp.bfloat16

PARTS = 32
GROUP = 8
BLOCK = LENGTH // PARTS
WIDTH = D // GROUP
PIECE = WIDTH // PARTS
HALF = PIECE // 2
NEAR = BLOCK // 2
FULL = 2 * LENGTH
SPAN = 2 * PARTS
BINS = PARTS + 1
ROWS = BINS * PIECE
TAIL = 8
CHIPS = GROUP // 2


def tables():
    low = np.array(list(range(1, PARTS)) + [0, PARTS])
    block, inside, near = np.arange(PARTS), np.arange(BLOCK), np.arange(NEAR)
    outer = 2 * np.pi * (low[:, None] * block[None, :] % SPAN) / SPAN
    cosine, sine = np.cos(outer), np.sin(outer)
    eye = np.eye(HALF)
    enter = np.kron(np.concatenate([cosine, -sine[: PARTS - 1]], 0), eye)
    weight = np.where((low == 0) | (low == PARTS), 1.0, 2.0)[:, None] / 4
    leave = np.kron(np.concatenate([cosine * weight, (sine * weight)[: PARTS - 1]], 0).T, eye)
    inner = 2 * np.pi * (near[:, None] * near[None, :] % NEAR) / NEAR
    cosine, sine = np.cos(inner) / 16, -np.sin(inner) / 16
    inner = np.block([[cosine, sine], [-sine, cosine]])
    half = SPAN * HALF // 2
    steps = np.concatenate([inner, leave, enter[:half], enter[half:]], 1)
    turn = 2 * np.pi * (low[:, None] * inside[None, :] % FULL) / FULL
    pair = 2 * np.pi * inside[None, :] / BLOCK
    turn = np.concatenate([turn, pair], 0)
    turn = np.stack([np.cos(turn), -np.sin(turn)])
    return steps.astype(np.float32).astype(bf16), turn.astype(np.float32)


def open_tables(steps_ref, turn_ref):
    cuts = (BLOCK, BLOCK + SPAN * HALF, 2 * BLOCK + SPAN * HALF)
    enter = jnp.concatenate([steps_ref[:, cuts[1] : cuts[2]], steps_ref[:, cuts[2] :]], 0)
    turn = [
        jnp.broadcast_to(turn_ref[part, :BINS][:, None, :], (BINS, HALF, BLOCK)).reshape(BINS * HALF, BLOCK)
        for part in range(2)
    ]
    pair = [turn_ref[part, BINS:, :NEAR] for part in range(2)]
    return enter, steps_ref[:, cuts[0] : cuts[1]], steps_ref[:, : cuts[0]], turn, pair


def dot(first, second):
    return jnp.dot(first, second, preferred_element_type=f32)


def rotate(real, imag, turn):
    return real * turn[0] - imag * turn[1], real * turn[1] + imag * turn[0]


def rotate_first(real, imag, turn):
    cosine, sine = turn
    own = imag.shape[0]
    turned_re, turned_im = rotate(real[:own], imag, (cosine[:own], sine[:own]))
    turned_re = jnp.concatenate([turned_re, real[own:] * cosine[own:]], 0)
    turned_im = jnp.concatenate([turned_im, real[own:] * sine[own:]], 0)
    return turned_re, turned_im


def join(halves):
    parts = [half.reshape(BINS, HALF, NEAR) for half in halves]
    return jnp.concatenate(parts, 1).reshape(ROWS, NEAR).astype(bf16)


def spectrum(signal, enter, inner, turn, pair):
    wide = signal.astype(f32)
    pieces = ([], [], [], [])
    for half in range(2):
        rows = wide[:, half * HALF : (half + 1) * HALF].reshape(PARTS * HALF, BLOCK)
        mixed = dot(enter, rows.astype(bf16))
        real, imag = rotate_first(mixed[: BINS * HALF], mixed[BINS * HALF :], turn)
        pieces[0].append(real[:, :NEAR] + real[:, NEAR:])
        pieces[1].append(imag[:, :NEAR] + imag[:, NEAR:])
        real, imag = rotate(real[:, :NEAR] - real[:, NEAR:], imag[:, :NEAR] - imag[:, NEAR:], pair)
        pieces[2].append(real)
        pieces[3].append(imag)
    pieces = [join(piece) for piece in pieces]
    return [dot(jnp.concatenate(pieces[at : at + 2], 1), inner) for at in (0, 2)]


def invert(even, odd, leave, inner, turn, pair):
    even, odd = [
        dot(jnp.concatenate([real.astype(bf16), imag.astype(bf16)], 1), inner).reshape(BINS, PIECE, BLOCK)
        for real, imag in (even, odd)
    ]
    outs = []
    for half in range(2):
        rows = slice(half * HALF, (half + 1) * HALF)
        first, second = [part[:, rows].reshape(BINS * HALF, BLOCK) for part in (even, odd)]
        first_re, first_im = first[:, :NEAR], first[:, NEAR:]
        second_re, second_im = rotate(second[:, :NEAR], second[:, NEAR:], pair)
        real = jnp.concatenate([first_re + second_re, first_re - second_re], 1)
        imag = jnp.concatenate([first_im + second_im, first_im - second_im], 1)
        own = (BINS - 2) * HALF
        turned_re = real * turn[0] - imag * turn[1]
        turned_im = real[:own] * turn[1][:own] + imag[:own] * turn[0][:own]
        turned = jnp.concatenate([turned_re, turned_im], 0).astype(bf16)
        outs.append(dot(leave, turned).reshape(PARTS, HALF, BLOCK))
    return jnp.concatenate(outs, 1)


def parts_of(values):
    return values[:, :NEAR].astype(f32), values[:, NEAR:].astype(f32)


def flat(pieces):
    return pieces.reshape(WIDTH, BLOCK)


def cut(rows):
    return rows.reshape(PARTS, PIECE, BLOCK)


def pack_kernel(key_hbm, value_hbm, taps_hbm, out_hbm, key_ref, value_ref, taps_ref, out_ref, sems):
    width, parts = WIDTH // 2, PARTS // 2
    loads, stores = [], []
    for half in range(2):
        columns = pl.ds(half * width, width)
        for source, target in ((key_hbm, key_ref), (value_hbm, value_ref), (taps_hbm, taps_ref)):
            loads.append(pltpu.make_async_copy(source.at[:, columns], target.at[:, columns], sems.at[len(loads)]))
            loads[-1].start()
    for half in range(2):
        columns, owners = pl.ds(half * width, width), pl.ds(half * parts, parts)
        loads[3 * half].wait()
        loads[3 * half + 1].wait()
        mixed = key_ref[:, columns].astype(f32) * value_ref[:, columns].astype(f32)
        out_ref[owners, :PIECE, :] = mixed.astype(bf16).T.reshape(parts, PIECE, BLOCK)
        loads[3 * half + 2].wait()
        out_ref[owners, PIECE:, :] = taps_ref[:, columns].T.reshape(parts, PIECE, BLOCK)
        stores.append(pltpu.make_async_copy(out_ref.at[owners], out_hbm.at[owners], sems.at[6 + half]))
        stores[-1].start()
    for store in stores:
        store.wait()


def forward_kernel(in_ref, steps_ref, turn_ref, gate_ref, cot_ref, out_ref, gate_out, cot_out):
    gate_out[...] = gate_ref[...].T
    cot_out[...] = cot_ref[...].T
    enter, leave, inner, turn, pair = open_tables(steps_ref, turn_ref)
    first = spectrum(in_ref[:, :PIECE, :], enter, inner, turn, pair)
    second = spectrum(in_ref[:, PIECE:, :], enter, inner, turn, pair)
    products = []
    for one, other in zip(first, second, strict=True):
        one_re, one_im = parts_of(one)
        other_re, other_im = parts_of(other)
        products.append((one_re * other_re - one_im * other_im, -(one_re * other_im + one_im * other_re)))
    out_ref[...] = invert(*products, leave, inner, turn, pair).astype(bf16)


def between_kernel(
    in_ref, steps_ref, turn_ref, conv_ref, key_ref, value_ref, skip_ref, after_ref, spec_ref, full_ref
):
    enter, _, inner, turn, pair = open_tables(steps_ref, turn_ref)
    for place in range(2):
        signal = in_ref[:, place * PIECE : (place + 1) * PIECE, :]
        even, odd = spectrum(signal, enter, inner, turn, pair)
        spec_ref[2 * place] = even.astype(bf16)
        spec_ref[2 * place + 1] = odd.astype(bf16)
    mixed = (key_ref[...].astype(f32) * value_ref[...].astype(f32)).astype(bf16)
    full_ref[...] = flat(conv_ref[...]).T.astype(f32) + skip_ref[...] * mixed.astype(f32)


def column(row_ref):
    turned = jnp.broadcast_to(row_ref[...], (128, WIDTH)).T
    return jnp.concatenate([turned, turned], 1)


def gate_parts(conv_ref, pack_ref, gate_ref, skip_ref):
    mixed = flat(pack_ref[:, :PIECE, :]).astype(f32)
    full = flat(conv_ref[...]).astype(f32) + column(skip_ref) * mixed
    gate = gate_ref[...].astype(f32)
    return full, gate, gate * full


def sums_kernel(conv_ref, pack_ref, gate_ref, cot_ref, skip_ref, gain_ref, out_ref):
    _, _, gated = gate_parts(conv_ref, pack_ref, gate_ref, skip_ref)
    scaled = cot_ref[...].astype(f32) * column(gain_ref)
    squares = jnp.sum(gated * gated, axis=0, keepdims=True)
    inner = jnp.sum(scaled * gated, axis=0, keepdims=True)
    out_ref[...] = jnp.concatenate([squares, inner], 0)


def norm_parts(sums_ref):
    sums = sums_ref[...]
    inv_rms = lax.rsqrt(sums[0:1] / D + epsilon)
    return inv_rms, inv_rms * inv_rms * inv_rms * sums[1:2] / D


def grad_kernel(
    sums_ref, conv_ref, pack_ref, gate_ref, cot_ref, skip_ref, gain_ref, after_ref, out_ref
):
    inv_rms, pull = norm_parts(sums_ref)
    _, gate, gated = gate_parts(conv_ref, pack_ref, gate_ref, skip_ref)
    scaled = cot_ref[...].astype(f32) * column(gain_ref)
    grad_gated = inv_rms * scaled - gated * pull
    out_ref[...] = cut((grad_gated * gate).astype(bf16))


def wide_column(row):
    turned = jnp.broadcast_to(row, (128, BLOCK)).T
    return jnp.concatenate([turned] * (WIDTH // 128), 1)


def backward_kernel(
    in_ref, pack_ref, spec_ref, steps_ref, turn_ref, sums_ref, full_ref, gate_ref, cot_ref, gain_ref,
    out_ref, grad_out, normed_hbm, gate_hbm, normed_ref, gate_out, sems,
):
    inv_rms, pull = (wide_column(row) for row in norm_parts(sums_ref))
    full, gate, gain = full_ref[...], gate_ref[...].astype(f32), gain_ref[...]
    gated = gate * full
    normed_ref[...] = (gated * inv_rms * gain).astype(bf16)
    grad_gated = inv_rms * (cot_ref[...].astype(f32) * gain) - gated * pull
    gate_out[...] = (grad_gated * full).astype(bf16)
    grad_out[...] = (grad_gated * gate).astype(bf16)
    copies = [
        pltpu.make_async_copy(normed_ref, normed_hbm, sems.at[0]),
        pltpu.make_async_copy(gate_out, gate_hbm, sems.at[1]),
    ]
    for copy in copies:
        copy.start()
    enter, leave, inner, turn, pair = open_tables(steps_ref, turn_ref)
    grad = in_ref[...]
    bias = jnp.sum(grad.astype(f32) * pack_ref[:, :PIECE, :].astype(f32), axis=0)
    bias = jnp.sum(bias, axis=1, keepdims=True)
    high = bias.astype(bf16).astype(f32)
    lane = lax.broadcasted_iota(jnp.int32, (TAIL, 128), 1)
    tail = jnp.zeros((TAIL, 128), f32)
    for at, part in enumerate((high[:HALF], (bias - high)[:HALF], high[HALF:], (bias - high)[HALF:])):
        tail = jnp.where(lane == at, part, tail)
    out_ref[:, 4 * PIECE :, :] = jnp.broadcast_to(tail.astype(bf16)[None], (PARTS, TAIL, 128))
    spectra = spectrum(grad, enter, inner, turn, pair)
    for place, other in ((0, 1), (1, 0)):
        products = []
        for parity, mine in enumerate(spectra):
            real, imag = parts_of(spec_ref[2 * other + parity])
            mine_re, mine_im = parts_of(mine)
            products.append((real * mine_re + imag * mine_im, imag * mine_re - real * mine_im))
        result = invert(*products, leave, inner, turn, pair).astype(bf16)
        out_ref[:, 2 * place * PIECE : (2 * place + 1) * PIECE, :] = result[:, :, :128]
        out_ref[:, (2 * place + 1) * PIECE : (2 * place + 2) * PIECE, :] = result[:, :, 128:]
    for copy in copies:
        copy.wait()


def last_kernel(in_ref, grad_ref, key_ref, value_ref, skip_ref, key_out, value_out, taps_out, bias_out):
    def whole(place):
        at = 2 * place * PIECE
        left, right = in_ref[:, at : at + PIECE, :], in_ref[:, at + PIECE : at + 2 * PIECE, :]
        return jnp.concatenate([left.reshape(WIDTH, 128).T, right.reshape(WIDTH, 128).T], 0)

    grad_mixed = whole(0).astype(f32) + skip_ref[...] * grad_ref[...].astype(f32)
    key_out[...] = (grad_mixed * value_ref[...].astype(f32)).astype(bf16)
    value_out[...] = (grad_mixed * key_ref[...].astype(f32)).astype(bf16)
    taps_out[...] = whole(1)
    tail = in_ref[:, 4 * PIECE :, :].astype(f32)
    tail = jnp.concatenate([tail, pltpu.roll(tail, 126, 2)], 1).reshape(WIDTH, 128).T
    bias_out[...] = tail[0:1] + tail[1:2]


def call(kernel, name, outs, *operands, hbm_in=(), hbm_out=(), scratch=(), grant=32 * 1024):
    vmem, hbm = pl.BlockSpec(memory_space=pltpu.VMEM), pl.BlockSpec(memory_space=pltpu.HBM)
    return pl.pallas_call(
        kernel,
        name=name,
        out_shape=[jax.ShapeDtypeStruct(shape, kind) for shape, kind in outs],
        in_specs=[hbm if place in hbm_in else vmem for place in range(len(operands))],
        out_specs=[hbm if place in hbm_out else vmem for place in range(len(outs))],
        scratch_shapes=list(scratch),
        compiler_params=pltpu.CompilerParams(vmem_limit_bytes=grant * 1024),
    )(*operands)


def add_over_pairs(sums):
    sums = sums + lax.ppermute(sums, "chan", [(at, at ^ 1) for at in range(GROUP)])
    return sums + lax.ppermute(sums, "chan", [(at, at ^ 2) for at in range(GROUP)])


def add_over_mirror(sums):
    mirror = [(at, (CHIPS - 1 - at // 2) * 2 + at % 2) for at in range(GROUP)]
    return sums + lax.ppermute(sums, "chan", mirror)


def on_device(gate_feat, key_feat, value_feat, filter_taps, skip_bias, norm_gain, cotangent):
    steps, turn = (jnp.asarray(table) for table in tables())
    skip_row, gain_row = skip_bias[None, :], norm_gain[None, :]
    natural = ((BLOCK, WIDTH), bf16)
    turned = ((WIDTH, BLOCK), bf16)
    pieces = ((PARTS, PIECE, BLOCK), bf16)
    spectra = ((4, ROWS, BLOCK), bf16)
    whole = pltpu.VMEM(*natural)

    (packed,) = call(
        pack_kernel,
        "pack",
        [((PARTS, 2 * PIECE, BLOCK), bf16)],
        key_feat,
        value_feat,
        filter_taps,
        hbm_in=(0, 1, 2),
        hbm_out=(0,),
        scratch=[whole, whole, whole, pltpu.VMEM((PARTS, 2 * PIECE, BLOCK), bf16), pltpu.SemaphoreType.DMA((8,))],
        grant=63 * 1024,
    )
    arrived = lax.all_to_all(packed, "seq", 0, 0, tiled=True)
    conv, gate_t, cot_t = call(
        forward_kernel,
        "forward",
        [pieces, turned, turned],
        arrived,
        steps,
        turn,
        gate_feat,
        cotangent,
    )
    conv = lax.all_to_all(conv, "seq", 0, 0, tiled=True)
    sides = (conv, packed, gate_t, cot_t, skip_row, gain_row)
    (sums,) = call(sums_kernel, "sums", [((2, BLOCK), f32)], *sides)
    sums = add_over_pairs(sums)
    spec, full = call(
        between_kernel,
        "between",
        [spectra, ((BLOCK, WIDTH), f32)],
        arrived,
        steps,
        turn,
        conv,
        key_feat,
        value_feat,
        skip_row,
        sums,
    )
    sums = add_over_mirror(sums)
    (grad,) = call(grad_kernel, "grad", [pieces], sums, *sides, full)
    grad_arrived = lax.all_to_all(grad, "seq", 0, 0, tiled=True)
    result, grad_conv, normed_out, grad_gate = call(
        backward_kernel,
        "backward",
        [((PARTS, 4 * PIECE + TAIL, 128), bf16), natural, natural, natural],
        grad_arrived,
        arrived,
        spec,
        steps,
        turn,
        sums,
        full,
        gate_feat,
        cotangent,
        gain_row,
        hbm_out=(2, 3),
        scratch=[whole, whole, pltpu.SemaphoreType.DMA((2,))],
    )
    result = lax.all_to_all(result, "seq", 0, 0, tiled=True)
    grad_key, grad_value, grad_filter, grad_bias = call(
        last_kernel,
        "last",
        [natural] * 3 + [((1, WIDTH), f32)],
        result,
        grad_conv,
        key_feat,
        value_feat,
        skip_row,
    )
    return normed_out, grad_gate, grad_key, grad_value, grad_filter, grad_bias[0]


def solution(mesh):
    wide, row = P("seq", "chan"), P("chan")
    return jax.shard_map(
        on_device,
        mesh=mesh,
        in_specs=(wide, wide, wide, wide, row, row, wide),
        out_specs=(wide, wide, wide, wide, wide, row),
        check_vma=False,
    )
```

```python
import jax
import jax.numpy as jnp
import numpy as np
from jax import lax
from jax.experimental import pallas as pl
from jax.experimental.pallas import tpu as pltpu
from jax.sharding import PartitionSpec as P

D = 4096
LENGTH = 8192
epsilon = 1e-05

f32, bf16 = jnp.float32, jnp.bfloat16

PARTS = 32
GROUP = 8
BLOCK = LENGTH // PARTS
WIDTH = D // GROUP
PIECE = WIDTH // PARTS
HALF = PIECE // 2
NEAR = BLOCK // 2
FULL = 2 * LENGTH
SPAN = 2 * PARTS
BINS = PARTS + 1
ROWS = BINS * PIECE
TAIL = 8
CHIPS = GROUP // 2


def tables():
    low = np.array(list(range(1, PARTS)) + [0, PARTS])
    block, inside, near = np.arange(PARTS), np.arange(BLOCK), np.arange(NEAR)
    outer = 2 * np.pi * (low[:, None] * block[None, :] % SPAN) / SPAN
    cosine, sine = np.cos(outer), np.sin(outer)
    eye = np.eye(HALF)
    enter = np.kron(np.concatenate([cosine, -sine[: PARTS - 1]], 0), eye)
    weight = np.where((low == 0) | (low == PARTS), 1.0, 2.0)[:, None] / 4
    leave = np.kron(np.concatenate([cosine * weight, (sine * weight)[: PARTS - 1]], 0).T, eye)
    inner = 2 * np.pi * (near[:, None] * near[None, :] % NEAR) / NEAR
    cosine, sine = np.cos(inner) / 16, -np.sin(inner) / 16
    inner = np.block([[cosine, sine], [-sine, cosine]])
    half = SPAN * HALF // 2
    steps = np.concatenate([inner, leave, enter[:half], enter[half:]], 1)
    turn = 2 * np.pi * (low[:, None] * inside[None, :] % FULL) / FULL
    pair = 2 * np.pi * inside[None, :] / BLOCK
    turn = np.concatenate([turn, pair], 0)
    turn = np.stack([np.cos(turn), -np.sin(turn)])
    return steps.astype(np.float32).astype(bf16), turn.astype(np.float32)


def open_tables(steps_ref, turn_ref):
    cuts = (BLOCK, BLOCK + SPAN * HALF, 2 * BLOCK + SPAN * HALF)
    enter = jnp.concatenate([steps_ref[:, cuts[1] : cuts[2]], steps_ref[:, cuts[2] :]], 0)
    turn = [
        jnp.broadcast_to(turn_ref[part, :BINS][:, None, :], (BINS, HALF, BLOCK)).reshape(BINS * HALF, BLOCK)
        for part in range(2)
    ]
    pair = [turn_ref[part, BINS:, :NEAR] for part in range(2)]
    return enter, steps_ref[:, cuts[0] : cuts[1]], steps_ref[:, : cuts[0]], turn, pair


def dot(first, second):
    return jnp.dot(first, second, preferred_element_type=f32)


def rotate(real, imag, turn):
    return real * turn[0] - imag * turn[1], real * turn[1] + imag * turn[0]


def rotate_first(real, imag, turn):
    cosine, sine = turn
    own = imag.shape[0]
    turned_re, turned_im = rotate(real[:own], imag, (cosine[:own], sine[:own]))
    turned_re = jnp.concatenate([turned_re, real[own:] * cosine[own:]], 0)
    turned_im = jnp.concatenate([turned_im, real[own:] * sine[own:]], 0)
    return turned_re, turned_im


def join(halves):
    parts = [half.reshape(BINS, HALF, NEAR) for half in halves]
    return jnp.concatenate(parts, 1).reshape(ROWS, NEAR).astype(bf16)


def spectrum(signal, enter, inner, turn, pair):
    wide = signal.astype(f32)
    pieces = ([], [], [], [])
    for half in range(2):
        rows = wide[:, half * HALF : (half + 1) * HALF].reshape(PARTS * HALF, BLOCK)
        mixed = dot(enter, rows.astype(bf16))
        real, imag = rotate_first(mixed[: BINS * HALF], mixed[BINS * HALF :], turn)
        pieces[0].append(real[:, :NEAR] + real[:, NEAR:])
        pieces[1].append(imag[:, :NEAR] + imag[:, NEAR:])
        real, imag = rotate(real[:, :NEAR] - real[:, NEAR:], imag[:, :NEAR] - imag[:, NEAR:], pair)
        pieces[2].append(real)
        pieces[3].append(imag)
    pieces = [join(piece) for piece in pieces]
    return [dot(jnp.concatenate(pieces[at : at + 2], 1), inner) for at in (0, 2)]


def invert(even, odd, leave, inner, turn, pair):
    even, odd = [
        dot(jnp.concatenate([real.astype(bf16), imag.astype(bf16)], 1), inner).reshape(BINS, PIECE, BLOCK)
        for real, imag in (even, odd)
    ]
    outs = []
    for half in range(2):
        rows = slice(half * HALF, (half + 1) * HALF)
        first, second = [part[:, rows].reshape(BINS * HALF, BLOCK) for part in (even, odd)]
        first_re, first_im = first[:, :NEAR], first[:, NEAR:]
        second_re, second_im = rotate(second[:, :NEAR], second[:, NEAR:], pair)
        real = jnp.concatenate([first_re + second_re, first_re - second_re], 1)
        imag = jnp.concatenate([first_im + second_im, first_im - second_im], 1)
        own = (BINS - 2) * HALF
        turned_re = real * turn[0] - imag * turn[1]
        turned_im = real[:own] * turn[1][:own] + imag[:own] * turn[0][:own]
        turned = jnp.concatenate([turned_re, turned_im], 0).astype(bf16)
        outs.append(dot(leave, turned).reshape(PARTS, HALF, BLOCK))
    return jnp.concatenate(outs, 1)


def parts_of(values):
    return values[:, :NEAR].astype(f32), values[:, NEAR:].astype(f32)


def flat(pieces):
    return pieces.reshape(WIDTH, BLOCK)


def cut(rows):
    return rows.reshape(PARTS, PIECE, BLOCK)


def pack_kernel(mixed_ref, taps_ref, out_ref):
    out_ref[:, :PIECE, :] = cut(mixed_ref[...].T)
    out_ref[:, PIECE:, :] = cut(taps_ref[...].T)


def forward_kernel(in_ref, steps_ref, turn_ref, gate_ref, cot_ref, out_ref, gate_out, cot_out):
    gate_out[...] = gate_ref[...].T
    cot_out[...] = cot_ref[...].T
    enter, leave, inner, turn, pair = open_tables(steps_ref, turn_ref)
    first = spectrum(in_ref[:, :PIECE, :], enter, inner, turn, pair)
    second = spectrum(in_ref[:, PIECE:, :], enter, inner, turn, pair)
    products = []
    for one, other in zip(first, second, strict=True):
        one_re, one_im = parts_of(one)
        other_re, other_im = parts_of(other)
        products.append((one_re * other_re - one_im * other_im, -(one_re * other_im + one_im * other_re)))
    out_ref[...] = invert(*products, leave, inner, turn, pair).astype(bf16)


def between_kernel(
    in_ref, steps_ref, turn_ref, conv_ref, key_ref, value_ref, skip_ref, after_ref, spec_ref, full_ref
):
    enter, _, inner, turn, pair = open_tables(steps_ref, turn_ref)
    for place in range(2):
        signal = in_ref[:, place * PIECE : (place + 1) * PIECE, :]
        even, odd = spectrum(signal, enter, inner, turn, pair)
        spec_ref[2 * place] = even.astype(bf16)
        spec_ref[2 * place + 1] = odd.astype(bf16)
    mixed = (key_ref[...].astype(f32) * value_ref[...].astype(f32)).astype(bf16)
    full_ref[...] = flat(conv_ref[...]).T.astype(f32) + skip_ref[...] * mixed.astype(f32)


def column(row_ref):
    turned = jnp.broadcast_to(row_ref[...], (128, WIDTH)).T
    return jnp.concatenate([turned, turned], 1)


def gate_parts(conv_ref, pack_ref, gate_ref, skip_ref):
    mixed = flat(pack_ref[:, :PIECE, :]).astype(f32)
    full = flat(conv_ref[...]).astype(f32) + column(skip_ref) * mixed
    gate = gate_ref[...].astype(f32)
    return full, gate, gate * full


def sums_kernel(conv_ref, pack_ref, gate_ref, cot_ref, skip_ref, gain_ref, out_ref):
    _, _, gated = gate_parts(conv_ref, pack_ref, gate_ref, skip_ref)
    scaled = cot_ref[...].astype(f32) * column(gain_ref)
    squares = jnp.sum(gated * gated, axis=0, keepdims=True)
    inner = jnp.sum(scaled * gated, axis=0, keepdims=True)
    out_ref[...] = jnp.concatenate([squares, inner], 0)


def norm_parts(sums_ref):
    sums = sums_ref[...]
    inv_rms = lax.rsqrt(sums[0:1] / D + epsilon)
    return inv_rms, inv_rms * inv_rms * inv_rms * sums[1:2] / D


def grad_kernel(
    sums_ref, conv_ref, pack_ref, gate_ref, cot_ref, skip_ref, gain_ref, after_ref, out_ref
):
    inv_rms, pull = norm_parts(sums_ref)
    _, gate, gated = gate_parts(conv_ref, pack_ref, gate_ref, skip_ref)
    scaled = cot_ref[...].astype(f32) * column(gain_ref)
    grad_gated = inv_rms * scaled - gated * pull
    out_ref[...] = cut((grad_gated * gate).astype(bf16))


def wide_column(row):
    turned = jnp.broadcast_to(row, (128, BLOCK)).T
    return jnp.concatenate([turned] * (WIDTH // 128), 1)


def backward_kernel(
    in_ref, pack_ref, spec_ref, steps_ref, turn_ref, sums_ref, full_ref, gate_ref, cot_ref, gain_ref,
    out_ref, grad_out, normed_out, gate_out,
):
    inv_rms, pull = (wide_column(row) for row in norm_parts(sums_ref))
    full, gate, gain = full_ref[...], gate_ref[...].astype(f32), gain_ref[...]
    gated = gate * full
    normed_out[...] = (gated * inv_rms * gain).astype(bf16)
    grad_gated = inv_rms * (cot_ref[...].astype(f32) * gain) - gated * pull
    gate_out[...] = (grad_gated * full).astype(bf16)
    grad_out[...] = (grad_gated * gate).astype(bf16)
    enter, leave, inner, turn, pair = open_tables(steps_ref, turn_ref)
    grad = in_ref[...]
    bias = jnp.sum(grad.astype(f32) * pack_ref[:, :PIECE, :].astype(f32), axis=0)
    bias = jnp.sum(bias, axis=1, keepdims=True)
    high = bias.astype(bf16).astype(f32)
    lane = lax.broadcasted_iota(jnp.int32, (TAIL, 128), 1)
    tail = jnp.zeros((TAIL, 128), f32)
    for at, part in enumerate((high[:HALF], (bias - high)[:HALF], high[HALF:], (bias - high)[HALF:])):
        tail = jnp.where(lane == at, part, tail)
    out_ref[:, 4 * PIECE :, :] = jnp.broadcast_to(tail.astype(bf16)[None], (PARTS, TAIL, 128))
    spectra = spectrum(grad, enter, inner, turn, pair)
    for place, other in ((0, 1), (1, 0)):
        products = []
        for parity, mine in enumerate(spectra):
            real, imag = parts_of(spec_ref[2 * other + parity])
            mine_re, mine_im = parts_of(mine)
            products.append((real * mine_re + imag * mine_im, imag * mine_re - real * mine_im))
        result = invert(*products, leave, inner, turn, pair).astype(bf16)
        out_ref[:, 2 * place * PIECE : (2 * place + 1) * PIECE, :] = result[:, :, :128]
        out_ref[:, (2 * place + 1) * PIECE : (2 * place + 2) * PIECE, :] = result[:, :, 128:]


def last_kernel(
    in_ref, grad_ref, key_ref, value_ref, skip_ref, normed_ref, gate_ref,
    key_out, value_out, taps_out, bias_out, normed_hbm, gate_hbm, sems,
):
    copies = [
        pltpu.make_async_copy(normed_ref, normed_hbm, sems.at[0]),
        pltpu.make_async_copy(gate_ref, gate_hbm, sems.at[1]),
    ]
    for copy in copies:
        copy.start()

    def whole(place):
        at = 2 * place * PIECE
        left, right = in_ref[:, at : at + PIECE, :], in_ref[:, at + PIECE : at + 2 * PIECE, :]
        return jnp.concatenate([left.reshape(WIDTH, 128).T, right.reshape(WIDTH, 128).T], 0)

    grad_mixed = whole(0).astype(f32) + skip_ref[...] * grad_ref[...].astype(f32)
    key_out[...] = (grad_mixed * value_ref[...].astype(f32)).astype(bf16)
    value_out[...] = (grad_mixed * key_ref[...].astype(f32)).astype(bf16)
    taps_out[...] = whole(1)
    tail = in_ref[:, 4 * PIECE :, :].astype(f32)
    tail = jnp.concatenate([tail, pltpu.roll(tail, 126, 2)], 1).reshape(WIDTH, 128).T
    bias_out[...] = tail[0:1] + tail[1:2]
    for copy in copies:
        copy.wait()


def call(kernel, name, outs, *operands, hbm_out=(), scratch=()):
    vmem, hbm = pl.BlockSpec(memory_space=pltpu.VMEM), pl.BlockSpec(memory_space=pltpu.HBM)
    return pl.pallas_call(
        kernel,
        name=name,
        out_shape=[jax.ShapeDtypeStruct(shape, kind) for shape, kind in outs],
        in_specs=[vmem] * len(operands),
        out_specs=[hbm if place in hbm_out else vmem for place in range(len(outs))],
        scratch_shapes=list(scratch),
        compiler_params=pltpu.CompilerParams(vmem_limit_bytes=32 * 1024 * 1024),
    )(*operands)


def add_over_pairs(sums):
    sums = sums + lax.ppermute(sums, "chan", [(at, at ^ 1) for at in range(GROUP)])
    return sums + lax.ppermute(sums, "chan", [(at, at ^ 2) for at in range(GROUP)])


def add_over_mirror(sums):
    mirror = [(at, (CHIPS - 1 - at // 2) * 2 + at % 2) for at in range(GROUP)]
    return sums + lax.ppermute(sums, "chan", mirror)


def on_device(gate_feat, key_feat, value_feat, filter_taps, skip_bias, norm_gain, cotangent):
    steps, turn = (jnp.asarray(table) for table in tables())
    skip_row, gain_row = skip_bias[None, :], norm_gain[None, :]
    natural = ((BLOCK, WIDTH), bf16)
    turned = ((WIDTH, BLOCK), bf16)
    pieces = ((PARTS, PIECE, BLOCK), bf16)
    spectra = ((4, ROWS, BLOCK), bf16)

    mixed = (key_feat.astype(f32) * value_feat.astype(f32)).astype(bf16)
    taps = jnp.where(key_feat == key_feat, filter_taps, mixed)
    (packed,) = call(pack_kernel, "pack", [((PARTS, 2 * PIECE, BLOCK), bf16)], mixed, taps)
    arrived = lax.all_to_all(packed, "seq", 0, 0, tiled=True)
    conv, gate_t, cot_t = call(
        forward_kernel,
        "forward",
        [pieces, turned, turned],
        arrived,
        steps,
        turn,
        gate_feat,
        cotangent,
    )
    conv = lax.all_to_all(conv, "seq", 0, 0, tiled=True)
    sides = (conv, packed, gate_t, cot_t, skip_row, gain_row)
    (sums,) = call(sums_kernel, "sums", [((2, BLOCK), f32)], *sides)
    sums = add_over_pairs(sums)
    spec, full = call(
        between_kernel,
        "between",
        [spectra, ((BLOCK, WIDTH), f32)],
        arrived,
        steps,
        turn,
        conv,
        key_feat,
        value_feat,
        skip_row,
        sums,
    )
    sums = add_over_mirror(sums)
    (grad,) = call(grad_kernel, "grad", [pieces], sums, *sides, full)
    grad_arrived = lax.all_to_all(grad, "seq", 0, 0, tiled=True)
    result, grad_conv, normed, gate = call(
        backward_kernel,
        "backward",
        [((PARTS, 4 * PIECE + TAIL, 128), bf16), natural, natural, natural],
        grad_arrived,
        arrived,
        spec,
        steps,
        turn,
        sums,
        full,
        gate_feat,
        cotangent,
        gain_row,
    )
    result = lax.all_to_all(result, "seq", 0, 0, tiled=True)
    grad_key, grad_value, grad_filter, grad_bias, normed_out, grad_gate = call(
        last_kernel,
        "last",
        [natural] * 3 + [((1, WIDTH), f32)] + [natural] * 2,
        result,
        grad_conv,
        key_feat,
        value_feat,
        skip_row,
        normed,
        gate,
        hbm_out=(4, 5),
        scratch=[pltpu.SemaphoreType.DMA((2,))],
    )
    return normed_out, grad_gate, grad_key, grad_value, grad_filter, grad_bias[0]


def solution(mesh):
    wide, row = P("seq", "chan"), P("chan")
    return jax.shard_map(
        on_device,
        mesh=mesh,
        in_specs=(wide, wide, wide, wide, row, row, wide),
        out_specs=(wide, wide, wide, wide, wide, row),
        check_vma=False,
    )
```

```python
import jax
import jax.numpy as jnp
import numpy as np
from jax import lax
from jax.experimental import pallas as pl
from jax.experimental.pallas import tpu as pltpu
from jax.sharding import PartitionSpec as P

D = 4096
LENGTH = 8192
epsilon = 1e-05

f32, bf16 = jnp.float32, jnp.bfloat16

PARTS = 32
GROUP = 8
BLOCK = LENGTH // PARTS
WIDTH = D // GROUP
PIECE = WIDTH // PARTS
HALF = PIECE // 2
NEAR = BLOCK // 2
FULL = 2 * LENGTH
SPAN = 2 * PARTS
BINS = PARTS + 1
ROWS = BINS * PIECE
TAIL = 8
CHIPS = GROUP // 2


def tables():
    low = np.array(list(range(1, PARTS)) + [0, PARTS])
    block, inside, near = np.arange(PARTS), np.arange(BLOCK), np.arange(NEAR)
    outer = 2 * np.pi * (low[:, None] * block[None, :] % SPAN) / SPAN
    cosine, sine = np.cos(outer), np.sin(outer)
    eye = np.eye(HALF)
    enter = np.kron(np.concatenate([cosine, -sine[: PARTS - 1]], 0), eye)
    weight = np.where((low == 0) | (low == PARTS), 1.0, 2.0)[:, None] / 4
    leave = np.kron(np.concatenate([cosine * weight, (sine * weight)[: PARTS - 1]], 0).T, eye)
    inner = 2 * np.pi * (near[:, None] * near[None, :] % NEAR) / NEAR
    cosine, sine = np.cos(inner) / 16, -np.sin(inner) / 16
    inner = np.block([[cosine, sine], [-sine, cosine]])
    half = SPAN * HALF // 2
    steps = np.concatenate([inner, leave, enter[:half], enter[half:]], 1)
    turn = 2 * np.pi * (low[:, None] * inside[None, :] % FULL) / FULL
    pair = 2 * np.pi * inside[None, :] / BLOCK
    turn = np.concatenate([turn, pair], 0)
    turn = np.stack([np.cos(turn), -np.sin(turn)])
    return steps.astype(np.float32).astype(bf16), turn.astype(np.float32)


def open_tables(steps_ref, turn_ref):
    cuts = (BLOCK, BLOCK + SPAN * HALF, 2 * BLOCK + SPAN * HALF)
    enter = jnp.concatenate([steps_ref[:, cuts[1] : cuts[2]], steps_ref[:, cuts[2] :]], 0)
    turn = [
        jnp.broadcast_to(turn_ref[part, :BINS][:, None, :], (BINS, HALF, BLOCK)).reshape(BINS * HALF, BLOCK)
        for part in range(2)
    ]
    pair = [turn_ref[part, BINS:, :NEAR] for part in range(2)]
    return enter, steps_ref[:, cuts[0] : cuts[1]], steps_ref[:, : cuts[0]], turn, pair


def dot(first, second):
    return jnp.dot(first, second, preferred_element_type=f32)


def rotate(real, imag, turn):
    return real * turn[0] - imag * turn[1], real * turn[1] + imag * turn[0]


def rotate_first(real, imag, turn):
    cosine, sine = turn
    own = imag.shape[0]
    turned_re, turned_im = rotate(real[:own], imag, (cosine[:own], sine[:own]))
    turned_re = jnp.concatenate([turned_re, real[own:] * cosine[own:]], 0)
    turned_im = jnp.concatenate([turned_im, real[own:] * sine[own:]], 0)
    return turned_re, turned_im


def join(halves):
    parts = [half.reshape(BINS, HALF, NEAR) for half in halves]
    return jnp.concatenate(parts, 1).reshape(ROWS, NEAR).astype(bf16)


def enter_blocks(signal, enter):
    wide = signal.astype(f32)
    halves = [wide[:, half * HALF : (half + 1) * HALF].reshape(PARTS * HALF, BLOCK) for half in range(2)]
    return [dot(enter, half.astype(bf16)) for half in halves]


def finish_spectrum(halves, inner, turn, pair):
    pieces = ([], [], [], [])
    for mixed in halves:
        real, imag = rotate_first(mixed[: BINS * HALF], mixed[BINS * HALF :], turn)
        pieces[0].append(real[:, :NEAR] + real[:, NEAR:])
        pieces[1].append(imag[:, :NEAR] + imag[:, NEAR:])
        real, imag = rotate(real[:, :NEAR] - real[:, NEAR:], imag[:, :NEAR] - imag[:, NEAR:], pair)
        pieces[2].append(real)
        pieces[3].append(imag)
    pieces = [join(piece) for piece in pieces]
    return [dot(jnp.concatenate(pieces[at : at + 2], 1), inner) for at in (0, 2)]


def invert_inner(products, inner):
    return [
        dot(jnp.concatenate([real.astype(bf16), imag.astype(bf16)], 1), inner).reshape(BINS, PIECE, BLOCK)
        for real, imag in products
    ]


def finish_inverse(parts, leave, turn, pair):
    outs = []
    for half in range(2):
        rows = slice(half * HALF, (half + 1) * HALF)
        first, second = [part[:, rows].reshape(BINS * HALF, BLOCK) for part in parts]
        first_re, first_im = first[:, :NEAR], first[:, NEAR:]
        second_re, second_im = rotate(second[:, :NEAR], second[:, NEAR:], pair)
        real = jnp.concatenate([first_re + second_re, first_re - second_re], 1)
        imag = jnp.concatenate([first_im + second_im, first_im - second_im], 1)
        own = (BINS - 2) * HALF
        turned_re = real * turn[0] - imag * turn[1]
        turned_im = real[:own] * turn[1][:own] + imag[:own] * turn[0][:own]
        turned = jnp.concatenate([turned_re, turned_im], 0).astype(bf16)
        outs.append(dot(leave, turned).reshape(PARTS, HALF, BLOCK))
    return jnp.concatenate(outs, 1)


def parts_of(values):
    return values[:, :NEAR].astype(f32), values[:, NEAR:].astype(f32)


def flat(pieces):
    return pieces.reshape(WIDTH, BLOCK)


def cut(rows):
    return rows.reshape(PARTS, PIECE, BLOCK)


def pack_kernel(mixed_ref, taps_ref, out_ref):
    out_ref[:, :PIECE, :] = cut(mixed_ref[...].T)
    out_ref[:, PIECE:, :] = cut(taps_ref[...].T)


def forward_kernel(in_ref, steps_ref, turn_ref, gate_ref, cot_ref, out_ref, gate_out, cot_out):
    gate_out[...] = gate_ref[...].T
    cot_out[...] = cot_ref[...].T
    enter, leave, inner, turn, pair = open_tables(steps_ref, turn_ref)
    first = enter_blocks(in_ref[:, :PIECE, :], enter)
    second = enter_blocks(in_ref[:, PIECE:, :], enter)
    first, second = [finish_spectrum(halves, inner, turn, pair) for halves in (first, second)]
    products = []
    for one, other in zip(first, second, strict=True):
        one_re, one_im = parts_of(one)
        other_re, other_im = parts_of(other)
        products.append((one_re * other_re - one_im * other_im, -(one_re * other_im + one_im * other_re)))
    out_ref[...] = finish_inverse(invert_inner(products, inner), leave, turn, pair).astype(bf16)


def between_kernel(
    in_ref, steps_ref, turn_ref, conv_ref, key_ref, value_ref, skip_ref, after_ref, spec_ref, full_ref
):
    enter, _, inner, turn, pair = open_tables(steps_ref, turn_ref)
    for place in range(2):
        signal = in_ref[:, place * PIECE : (place + 1) * PIECE, :]
        even, odd = finish_spectrum(enter_blocks(signal, enter), inner, turn, pair)
        spec_ref[2 * place] = even.astype(bf16)
        spec_ref[2 * place + 1] = odd.astype(bf16)
    mixed = (key_ref[...].astype(f32) * value_ref[...].astype(f32)).astype(bf16)
    full_ref[...] = flat(conv_ref[...]).T.astype(f32) + skip_ref[...] * mixed.astype(f32)


def column(row_ref):
    turned = jnp.broadcast_to(row_ref[...], (128, WIDTH)).T
    return jnp.concatenate([turned, turned], 1)


def gate_parts(conv_ref, pack_ref, gate_ref, skip_ref):
    mixed = flat(pack_ref[:, :PIECE, :]).astype(f32)
    full = flat(conv_ref[...]).astype(f32) + column(skip_ref) * mixed
    gate = gate_ref[...].astype(f32)
    return full, gate, gate * full


def sums_kernel(conv_ref, pack_ref, gate_ref, cot_ref, skip_ref, gain_ref, out_ref):
    _, _, gated = gate_parts(conv_ref, pack_ref, gate_ref, skip_ref)
    scaled = cot_ref[...].astype(f32) * column(gain_ref)
    squares = jnp.sum(gated * gated, axis=0, keepdims=True)
    inner = jnp.sum(scaled * gated, axis=0, keepdims=True)
    out_ref[...] = jnp.concatenate([squares, inner], 0)


def norm_parts(sums_ref):
    sums = sums_ref[...]
    inv_rms = lax.rsqrt(sums[0:1] / D + epsilon)
    return inv_rms, inv_rms * inv_rms * inv_rms * sums[1:2] / D


def grad_kernel(
    sums_ref, conv_ref, pack_ref, gate_ref, cot_ref, skip_ref, gain_ref, after_ref, out_ref
):
    inv_rms, pull = norm_parts(sums_ref)
    _, gate, gated = gate_parts(conv_ref, pack_ref, gate_ref, skip_ref)
    scaled = cot_ref[...].astype(f32) * column(gain_ref)
    grad_gated = inv_rms * scaled - gated * pull
    out_ref[...] = cut((grad_gated * gate).astype(bf16))


def wide_column(row):
    turned = jnp.broadcast_to(row, (128, BLOCK)).T
    return jnp.concatenate([turned] * (WIDTH // 128), 1)


def backward_kernel(
    in_ref, pack_ref, spec_ref, steps_ref, turn_ref, sums_ref, full_ref, gate_ref, cot_ref, gain_ref,
    out_ref, grad_out, normed_out, gate_out,
):
    inv_rms, pull = (wide_column(row) for row in norm_parts(sums_ref))
    full, gate, gain = full_ref[...], gate_ref[...].astype(f32), gain_ref[...]
    gated = gate * full
    normed_out[...] = (gated * inv_rms * gain).astype(bf16)
    grad_gated = inv_rms * (cot_ref[...].astype(f32) * gain) - gated * pull
    gate_out[...] = (grad_gated * full).astype(bf16)
    grad_out[...] = (grad_gated * gate).astype(bf16)
    enter, leave, inner, turn, pair = open_tables(steps_ref, turn_ref)
    grad = in_ref[...]
    bias = jnp.sum(grad.astype(f32) * pack_ref[:, :PIECE, :].astype(f32), axis=0)
    bias = jnp.sum(bias, axis=1, keepdims=True)
    high = bias.astype(bf16).astype(f32)
    lane = lax.broadcasted_iota(jnp.int32, (TAIL, 128), 1)
    tail = jnp.zeros((TAIL, 128), f32)
    for at, part in enumerate((high[:HALF], (bias - high)[:HALF], high[HALF:], (bias - high)[HALF:])):
        tail = jnp.where(lane == at, part, tail)
    out_ref[:, 4 * PIECE :, :] = jnp.broadcast_to(tail.astype(bf16)[None], (PARTS, TAIL, 128))
    spectra = finish_spectrum(enter_blocks(grad, enter), inner, turn, pair)
    inverses = []
    for other in (1, 0):
        products = []
        for parity, mine in enumerate(spectra):
            real, imag = parts_of(spec_ref[2 * other + parity])
            mine_re, mine_im = parts_of(mine)
            products.append((real * mine_re + imag * mine_im, imag * mine_re - real * mine_im))
        inverses.append(invert_inner(products, inner))
    for place, parts in enumerate(inverses):
        result = finish_inverse(parts, leave, turn, pair).astype(bf16)
        out_ref[:, 2 * place * PIECE : (2 * place + 1) * PIECE, :] = result[:, :, :128]
        out_ref[:, (2 * place + 1) * PIECE : (2 * place + 2) * PIECE, :] = result[:, :, 128:]


def last_kernel(
    in_ref, grad_ref, key_ref, value_ref, skip_ref, normed_ref, gate_ref,
    key_out, value_out, taps_out, bias_out, normed_out, gate_out,
):
    normed_out[...] = normed_ref[...]
    gate_out[...] = gate_ref[...]

    def whole(place):
        at = 2 * place * PIECE
        left, right = in_ref[:, at : at + PIECE, :], in_ref[:, at + PIECE : at + 2 * PIECE, :]
        return jnp.concatenate([left.reshape(WIDTH, 128).T, right.reshape(WIDTH, 128).T], 0)

    grad_mixed = whole(0).astype(f32) + skip_ref[...] * grad_ref[...].astype(f32)
    key_out[...] = (grad_mixed * value_ref[...].astype(f32)).astype(bf16)
    value_out[...] = (grad_mixed * key_ref[...].astype(f32)).astype(bf16)
    taps_out[...] = whole(1)
    tail = in_ref[:, 4 * PIECE :, :].astype(f32)
    tail = jnp.concatenate([tail, pltpu.roll(tail, 126, 2)], 1).reshape(WIDTH, 128).T
    bias_out[...] = tail[0:1] + tail[1:2]


def call(kernel, name, outs, *operands):
    vmem = pl.BlockSpec(memory_space=pltpu.VMEM)
    return pl.pallas_call(
        kernel,
        name=name,
        out_shape=[jax.ShapeDtypeStruct(shape, kind) for shape, kind in outs],
        in_specs=[vmem] * len(operands),
        out_specs=[vmem] * len(outs),
        compiler_params=pltpu.CompilerParams(vmem_limit_bytes=32 * 1024 * 1024),
    )(*operands)


def add_over_pairs(sums):
    sums = sums + lax.ppermute(sums, "chan", [(at, at ^ 1) for at in range(GROUP)])
    return sums + lax.ppermute(sums, "chan", [(at, at ^ 2) for at in range(GROUP)])


def add_over_mirror(sums):
    mirror = [(at, (CHIPS - 1 - at // 2) * 2 + at % 2) for at in range(GROUP)]
    return sums + lax.ppermute(sums, "chan", mirror)


def on_device(gate_feat, key_feat, value_feat, filter_taps, skip_bias, norm_gain, cotangent):
    steps, turn = (jnp.asarray(table) for table in tables())
    skip_row, gain_row = skip_bias[None, :], norm_gain[None, :]
    natural = ((BLOCK, WIDTH), bf16)
    turned = ((WIDTH, BLOCK), bf16)
    pieces = ((PARTS, PIECE, BLOCK), bf16)
    spectra = ((4, ROWS, BLOCK), bf16)

    mixed = (key_feat.astype(f32) * value_feat.astype(f32)).astype(bf16)
    taps = jnp.where(key_feat == key_feat, filter_taps, mixed)
    (packed,) = call(pack_kernel, "pack", [((PARTS, 2 * PIECE, BLOCK), bf16)], mixed, taps)
    arrived = lax.all_to_all(packed, "seq", 0, 0, tiled=True)
    conv, gate_t, cot_t = call(
        forward_kernel,
        "forward",
        [pieces, turned, turned],
        arrived,
        steps,
        turn,
        gate_feat,
        cotangent,
    )
    conv = lax.all_to_all(conv, "seq", 0, 0, tiled=True)
    sides = (conv, packed, gate_t, cot_t, skip_row, gain_row)
    (sums,) = call(sums_kernel, "sums", [((2, BLOCK), f32)], *sides)
    sums = add_over_pairs(sums)
    spec, full = call(
        between_kernel,
        "between",
        [spectra, ((BLOCK, WIDTH), f32)],
        arrived,
        steps,
        turn,
        conv,
        key_feat,
        value_feat,
        skip_row,
        sums,
    )
    sums = add_over_mirror(sums)
    (grad,) = call(grad_kernel, "grad", [pieces], sums, *sides, full)
    grad_arrived = lax.all_to_all(grad, "seq", 0, 0, tiled=True)
    result, grad_conv, normed, gate = call(
        backward_kernel,
        "backward",
        [((PARTS, 4 * PIECE + TAIL, 128), bf16), natural, natural, natural],
        grad_arrived,
        arrived,
        spec,
        steps,
        turn,
        sums,
        full,
        gate_feat,
        cotangent,
        gain_row,
    )
    result = lax.all_to_all(result, "seq", 0, 0, tiled=True)
    grad_key, grad_value, grad_filter, grad_bias, normed_out, grad_gate = call(
        last_kernel,
        "last",
        [natural] * 3 + [((1, WIDTH), f32)] + [natural] * 2,
        result,
        grad_conv,
        key_feat,
        value_feat,
        skip_row,
        normed,
        gate,
    )
    return normed_out, grad_gate, grad_key, grad_value, grad_filter, grad_bias[0]


def solution(mesh):
    wide, row = P("seq", "chan"), P("chan")
    return jax.shard_map(
        on_device,
        mesh=mesh,
        in_specs=(wide, wide, wide, wide, row, row, wide),
        out_specs=(wide, wide, wide, wide, wide, row),
        check_vma=False,
    )
```

```python
import jax
import jax.numpy as jnp
import numpy as np
from jax import lax
from jax.experimental import pallas as pl
from jax.experimental.pallas import tpu as pltpu
from jax.sharding import PartitionSpec as P

D = 4096
LENGTH = 8192
epsilon = 1e-05

f32, bf16 = jnp.float32, jnp.bfloat16

PARTS = 32
GROUP = 8
BLOCK = LENGTH // PARTS
WIDTH = D // GROUP
PIECE = WIDTH // PARTS
HALF = PIECE // 2
NEAR = BLOCK // 2
FULL = 2 * LENGTH
SPAN = 2 * PARTS
BINS = PARTS + 1
ROWS = BINS * PIECE
TAIL = 8
CHIPS = GROUP // 2


def tables():
    low = np.array(list(range(1, PARTS)) + [0, PARTS])
    block, inside, near = np.arange(PARTS), np.arange(BLOCK), np.arange(NEAR)
    outer = 2 * np.pi * (low[:, None] * block[None, :] % SPAN) / SPAN
    cosine, sine = np.cos(outer), np.sin(outer)
    eye = np.eye(HALF)
    enter = np.kron(np.concatenate([cosine, -sine[: PARTS - 1]], 0), eye)
    weight = np.where((low == 0) | (low == PARTS), 1.0, 2.0)[:, None] / 4
    leave = np.kron(np.concatenate([cosine * weight, (sine * weight)[: PARTS - 1]], 0).T, eye)
    inner = 2 * np.pi * (near[:, None] * near[None, :] % NEAR) / NEAR
    cosine, sine = np.cos(inner) / 16, -np.sin(inner) / 16
    inner = np.block([[cosine, sine], [-sine, cosine]])
    half = SPAN * HALF // 2
    steps = np.concatenate([inner, leave, enter[:half], enter[half:]], 1)
    turn = 2 * np.pi * (low[:, None] * inside[None, :] % FULL) / FULL
    pair = 2 * np.pi * inside[None, :] / BLOCK
    turn = np.concatenate([turn, pair], 0)
    turn = np.stack([np.cos(turn), -np.sin(turn)])
    return steps.astype(np.float32).astype(bf16), turn.astype(np.float32)


def open_tables(steps_ref, turn_ref):
    cuts = (BLOCK, BLOCK + SPAN * HALF, 2 * BLOCK + SPAN * HALF)
    enter = jnp.concatenate([steps_ref[:, cuts[1] : cuts[2]], steps_ref[:, cuts[2] :]], 0)
    turn = [
        jnp.broadcast_to(turn_ref[part, :BINS][:, None, :], (BINS, HALF, BLOCK)).reshape(BINS * HALF, BLOCK)
        for part in range(2)
    ]
    pair = [turn_ref[part, BINS:, :NEAR] for part in range(2)]
    return enter, steps_ref[:, cuts[0] : cuts[1]], steps_ref[:, : cuts[0]], turn, pair


def dot(first, second):
    return jnp.dot(first, second, preferred_element_type=f32)


def rotate(real, imag, turn):
    return real * turn[0] - imag * turn[1], real * turn[1] + imag * turn[0]


def rotate_first(real, imag, turn):
    cosine, sine = turn
    own = imag.shape[0]
    turned_re, turned_im = rotate(real[:own], imag, (cosine[:own], sine[:own]))
    turned_re = jnp.concatenate([turned_re, real[own:] * cosine[own:]], 0)
    turned_im = jnp.concatenate([turned_im, real[own:] * sine[own:]], 0)
    return turned_re, turned_im


def join(halves):
    parts = [half.reshape(BINS, HALF, NEAR) for half in halves]
    return jnp.concatenate(parts, 1).reshape(ROWS, NEAR).astype(bf16)


def enter_blocks(signal, enter):
    wide = signal.astype(f32)
    halves = [wide[:, half * HALF : (half + 1) * HALF].reshape(PARTS * HALF, BLOCK) for half in range(2)]
    return [dot(enter, half.astype(bf16)) for half in halves]


def finish_spectrum(halves, inner, turn, pair):
    pieces = ([], [], [], [])
    for mixed in halves:
        real, imag = rotate_first(mixed[: BINS * HALF], mixed[BINS * HALF :], turn)
        pieces[0].append(real[:, :NEAR] + real[:, NEAR:])
        pieces[1].append(imag[:, :NEAR] + imag[:, NEAR:])
        real, imag = rotate(real[:, :NEAR] - real[:, NEAR:], imag[:, :NEAR] - imag[:, NEAR:], pair)
        pieces[2].append(real)
        pieces[3].append(imag)
    pieces = [join(piece) for piece in pieces]
    return [dot(jnp.concatenate(pieces[at : at + 2], 1), inner) for at in (0, 2)]


def invert_inner(products, inner):
    return [
        dot(jnp.concatenate([real.astype(bf16), imag.astype(bf16)], 1), inner).reshape(BINS, PIECE, BLOCK)
        for real, imag in products
    ]


def finish_inverse(parts, leave, turn, pair):
    outs = []
    for half in range(2):
        rows = slice(half * HALF, (half + 1) * HALF)
        first, second = [part[:, rows].reshape(BINS * HALF, BLOCK) for part in parts]
        first_re, first_im = first[:, :NEAR], first[:, NEAR:]
        second_re, second_im = rotate(second[:, :NEAR], second[:, NEAR:], pair)
        real = jnp.concatenate([first_re + second_re, first_re - second_re], 1)
        imag = jnp.concatenate([first_im + second_im, first_im - second_im], 1)
        own = (BINS - 2) * HALF
        turned_re = real * turn[0] - imag * turn[1]
        turned_im = real[:own] * turn[1][:own] + imag[:own] * turn[0][:own]
        turned = jnp.concatenate([turned_re, turned_im], 0).astype(bf16)
        outs.append(dot(leave, turned).reshape(PARTS, HALF, BLOCK))
    return jnp.concatenate(outs, 1)


def parts_of(values):
    return values[:, :NEAR], values[:, NEAR:]


def flat(pieces):
    return pieces.reshape(WIDTH, BLOCK)


def cut(rows):
    return rows.reshape(PARTS, PIECE, BLOCK)


def pack_kernel(mixed_ref, taps_ref, out_ref):
    out_ref[:, :PIECE, :] = cut(mixed_ref[...].T)
    out_ref[:, PIECE:, :] = cut(taps_ref[...].T)


def forward_kernel(in_ref, steps_ref, turn_ref, gate_ref, cot_ref, out_ref, gate_out, cot_out):
    gate_out[...] = gate_ref[...].T
    cot_out[...] = cot_ref[...].T
    enter, leave, inner, turn, pair = open_tables(steps_ref, turn_ref)
    first = enter_blocks(in_ref[:, :PIECE, :], enter)
    second = enter_blocks(in_ref[:, PIECE:, :], enter)
    first, second = [finish_spectrum(halves, inner, turn, pair) for halves in (first, second)]
    products = []
    for one, other in zip(first, second, strict=True):
        one_re, one_im = parts_of(one)
        other_re, other_im = parts_of(other)
        products.append((one_re * other_re - one_im * other_im, -(one_re * other_im + one_im * other_re)))
    out_ref[...] = finish_inverse(invert_inner(products, inner), leave, turn, pair).astype(bf16)


def between_kernel(
    in_ref, steps_ref, turn_ref, key_ref, value_ref, conv_ref, pack_ref, gate_ref, cot_ref, skip_ref, gain_ref,
    after_ref, spec_ref, full_ref, push_ref, hold_ref,
):
    _, gate, gated = gate_parts(conv_ref, pack_ref, gate_ref, skip_ref)
    push_ref[...] = cot_ref[...].astype(f32) * column(gain_ref) * gate
    hold_ref[...] = gated * gate
    enter, _, inner, turn, pair = open_tables(steps_ref, turn_ref)
    for place in range(2):
        signal = in_ref[:, place * PIECE : (place + 1) * PIECE, :]
        even, odd = finish_spectrum(enter_blocks(signal, enter), inner, turn, pair)
        spec_ref[2 * place] = even
        spec_ref[2 * place + 1] = odd
    mixed = (key_ref[...].astype(f32) * value_ref[...].astype(f32)).astype(bf16)
    full_ref[...] = flat(conv_ref[...]).T.astype(f32) + skip_ref[...] * mixed.astype(f32)


def column(row_ref):
    turned = jnp.broadcast_to(row_ref[...], (128, WIDTH)).T
    return jnp.concatenate([turned, turned], 1)


def gate_parts(conv_ref, pack_ref, gate_ref, skip_ref):
    mixed = flat(pack_ref[:, :PIECE, :]).astype(f32)
    full = flat(conv_ref[...]).astype(f32) + column(skip_ref) * mixed
    gate = gate_ref[...].astype(f32)
    return full, gate, gate * full


def sums_kernel(conv_ref, pack_ref, gate_ref, cot_ref, skip_ref, gain_ref, out_ref):
    _, _, gated = gate_parts(conv_ref, pack_ref, gate_ref, skip_ref)
    scaled = cot_ref[...].astype(f32) * column(gain_ref)
    squares = jnp.sum(gated * gated, axis=0, keepdims=True)
    inner = jnp.sum(scaled * gated, axis=0, keepdims=True)
    out_ref[...] = jnp.concatenate([squares, inner], 0)


def norm_parts(sums_ref):
    sums = sums_ref[...]
    inv_rms = lax.rsqrt(sums[0:1] / D + epsilon)
    return inv_rms, inv_rms * inv_rms * inv_rms * sums[1:2] / D


def grad_kernel(sums_ref, push_ref, hold_ref, out_ref):
    inv_rms, pull = norm_parts(sums_ref)
    out_ref[...] = cut((inv_rms * push_ref[...] - pull * hold_ref[...]).astype(bf16))


def wide_column(row):
    turned = jnp.broadcast_to(row, (128, BLOCK)).T
    return jnp.concatenate([turned] * (WIDTH // 128), 1)


def backward_kernel(
    in_ref, pack_ref, spec_ref, steps_ref, turn_ref, sums_ref, full_ref, gate_ref, cot_ref, gain_ref,
    out_ref, grad_out, normed_out, gate_out,
):
    inv_rms, pull = (wide_column(row) for row in norm_parts(sums_ref))
    full, gate, gain = full_ref[...], gate_ref[...].astype(f32), gain_ref[...]
    gated = gate * full
    normed_out[...] = (gated * inv_rms * gain).astype(bf16)
    grad_gated = inv_rms * (cot_ref[...].astype(f32) * gain) - gated * pull
    gate_out[...] = (grad_gated * full).astype(bf16)
    grad_out[...] = (grad_gated * gate).astype(bf16)
    enter, leave, inner, turn, pair = open_tables(steps_ref, turn_ref)
    grad = in_ref[...]
    bias = jnp.sum(grad.astype(f32) * pack_ref[:, :PIECE, :].astype(f32), axis=0)
    bias = jnp.sum(bias, axis=1, keepdims=True)
    high = bias.astype(bf16).astype(f32)
    lane = lax.broadcasted_iota(jnp.int32, (TAIL, 128), 1)
    tail = jnp.zeros((TAIL, 128), f32)
    for at, part in enumerate((high[:HALF], (bias - high)[:HALF], high[HALF:], (bias - high)[HALF:])):
        tail = jnp.where(lane == at, part, tail)
    out_ref[:, 4 * PIECE :, :] = jnp.broadcast_to(tail.astype(bf16)[None], (PARTS, TAIL, 128))
    spectra = finish_spectrum(enter_blocks(grad, enter), inner, turn, pair)
    inverses = []
    for other in (1, 0):
        products = []
        for parity, mine in enumerate(spectra):
            real, imag = parts_of(spec_ref[2 * other + parity])
            mine_re, mine_im = parts_of(mine)
            products.append((real * mine_re + imag * mine_im, imag * mine_re - real * mine_im))
        inverses.append(invert_inner(products, inner))
    for place, parts in enumerate(inverses):
        result = finish_inverse(parts, leave, turn, pair).astype(bf16)
        out_ref[:, 2 * place * PIECE : (2 * place + 1) * PIECE, :] = result[:, :, :128]
        out_ref[:, (2 * place + 1) * PIECE : (2 * place + 2) * PIECE, :] = result[:, :, 128:]


def last_kernel(
    in_ref, grad_ref, key_ref, value_ref, skip_ref, normed_ref, gate_ref,
    key_out, value_out, taps_out, bias_out, normed_out, gate_out,
):
    normed_out[...] = normed_ref[...]
    gate_out[...] = gate_ref[...]

    def whole(place):
        at = 2 * place * PIECE
        left, right = in_ref[:, at : at + PIECE, :], in_ref[:, at + PIECE : at + 2 * PIECE, :]
        return jnp.concatenate([left.reshape(WIDTH, 128).T, right.reshape(WIDTH, 128).T], 0)

    grad_mixed = whole(0).astype(f32) + skip_ref[...] * grad_ref[...].astype(f32)
    key_out[...] = (grad_mixed * value_ref[...].astype(f32)).astype(bf16)
    value_out[...] = (grad_mixed * key_ref[...].astype(f32)).astype(bf16)
    taps_out[...] = whole(1)
    tail = in_ref[:, 4 * PIECE :, :].astype(f32)
    tail = jnp.concatenate([tail, pltpu.roll(tail, 126, 2)], 1).reshape(WIDTH, 128).T
    bias_out[...] = tail[0:1] + tail[1:2]


def call(kernel, name, outs, *operands):
    vmem = pl.BlockSpec(memory_space=pltpu.VMEM)
    return pl.pallas_call(
        kernel,
        name=name,
        out_shape=[jax.ShapeDtypeStruct(shape, kind) for shape, kind in outs],
        in_specs=[vmem] * len(operands),
        out_specs=[vmem] * len(outs),
        compiler_params=pltpu.CompilerParams(vmem_limit_bytes=32 * 1024 * 1024),
    )(*operands)


def add_over_pairs(sums):
    sums = sums + lax.ppermute(sums, "chan", [(at, at ^ 1) for at in range(GROUP)])
    return sums + lax.ppermute(sums, "chan", [(at, at ^ 2) for at in range(GROUP)])


def add_over_mirror(sums):
    mirror = [(at, (CHIPS - 1 - at // 2) * 2 + at % 2) for at in range(GROUP)]
    return sums + lax.ppermute(sums, "chan", mirror)


def on_device(gate_feat, key_feat, value_feat, filter_taps, skip_bias, norm_gain, cotangent):
    steps, turn = (jnp.asarray(table) for table in tables())
    skip_row, gain_row = skip_bias[None, :], norm_gain[None, :]
    natural = ((BLOCK, WIDTH), bf16)
    turned = ((WIDTH, BLOCK), bf16)
    pieces = ((PARTS, PIECE, BLOCK), bf16)
    spectra = ((4, ROWS, BLOCK), f32)

    mixed = (key_feat.astype(f32) * value_feat.astype(f32)).astype(bf16)
    taps = jnp.where(key_feat == key_feat, filter_taps, mixed)
    (packed,) = call(pack_kernel, "pack", [((PARTS, 2 * PIECE, BLOCK), bf16)], mixed, taps)
    arrived = lax.all_to_all(packed, "seq", 0, 0, tiled=True)
    conv, gate_t, cot_t = call(
        forward_kernel,
        "forward",
        [pieces, turned, turned],
        arrived,
        steps,
        turn,
        gate_feat,
        cotangent,
    )
    conv = lax.all_to_all(conv, "seq", 0, 0, tiled=True)
    sides = (conv, packed, gate_t, cot_t, skip_row, gain_row)
    (sums,) = call(sums_kernel, "sums", [((2, BLOCK), f32)], *sides)
    sums = add_over_pairs(sums)
    spec, full, push, hold = call(
        between_kernel,
        "between",
        [spectra, ((BLOCK, WIDTH), f32), ((WIDTH, BLOCK), f32), ((WIDTH, BLOCK), f32)],
        arrived,
        steps,
        turn,
        key_feat,
        value_feat,
        *sides,
        sums,
    )
    sums = add_over_mirror(sums)
    (grad,) = call(grad_kernel, "grad", [pieces], sums, push, hold)
    grad_arrived = lax.all_to_all(grad, "seq", 0, 0, tiled=True)
    result, grad_conv, normed, gate = call(
        backward_kernel,
        "backward",
        [((PARTS, 4 * PIECE + TAIL, 128), bf16), natural, natural, natural],
        grad_arrived,
        arrived,
        spec,
        steps,
        turn,
        sums,
        full,
        gate_feat,
        cotangent,
        gain_row,
    )
    result = lax.all_to_all(result, "seq", 0, 0, tiled=True)
    grad_key, grad_value, grad_filter, grad_bias, normed_out, grad_gate = call(
        last_kernel,
        "last",
        [natural] * 3 + [((1, WIDTH), f32)] + [natural] * 2,
        result,
        grad_conv,
        key_feat,
        value_feat,
        skip_row,
        normed,
        gate,
    )
    return normed_out, grad_gate, grad_key, grad_value, grad_filter, grad_bias[0]


def solution(mesh):
    wide, row = P("seq", "chan"), P("chan")
    return jax.shard_map(
        on_device,
        mesh=mesh,
        in_specs=(wide, wide, wide, wide, row, row, wide),
        out_specs=(wide, wide, wide, wide, wide, row),
        check_vma=False,
    )
```

```python
import jax
import jax.numpy as jnp
import numpy as np
from jax import lax
from jax.experimental import pallas as pl
from jax.experimental.pallas import tpu as pltpu
from jax.sharding import PartitionSpec as P

D = 4096
LENGTH = 8192
epsilon = 1e-05

f32, bf16 = jnp.float32, jnp.bfloat16

PARTS = 32
GROUP = 8
BLOCK = LENGTH // PARTS
WIDTH = D // GROUP
PIECE = WIDTH // PARTS
HALF = PIECE // 2
NEAR = BLOCK // 2
FULL = 2 * LENGTH
SPAN = 2 * PARTS
BINS = PARTS + 1
ROWS = BINS * PIECE
TAIL = 8
CHIPS = GROUP // 2


def tables():
    low = np.array(list(range(1, PARTS)) + [0, PARTS])
    block, inside, near = np.arange(PARTS), np.arange(BLOCK), np.arange(NEAR)
    outer = 2 * np.pi * (low[:, None] * block[None, :] % SPAN) / SPAN
    cosine, sine = np.cos(outer), np.sin(outer)
    eye = np.eye(HALF)
    enter = np.kron(np.concatenate([cosine, -sine[: PARTS - 1]], 0), eye)
    weight = np.where((low == 0) | (low == PARTS), 1.0, 2.0)[:, None] / 4
    leave = np.kron(np.concatenate([cosine * weight, (sine * weight)[: PARTS - 1]], 0).T, eye)
    into, back = [], []
    for odd in range(2):
        inner = 2 * np.pi * (near[:, None] * (2 * near[None, :] + odd) % BLOCK) / BLOCK
        cosine, sine = np.cos(inner) / 16, -np.sin(inner) / 16
        into.append(np.block([[cosine, sine], [-sine, cosine]]))
        back.append(np.block([[cosine.T, sine.T], [sine.T, -cosine.T]]))
    half = SPAN * HALF // 2
    steps = np.concatenate([*into, *back, leave, enter[:half], enter[half:]], 1)
    turn = 2 * np.pi * (low[:, None] * inside[None, :] % FULL) / FULL
    turn = np.stack([np.cos(turn), -np.sin(turn)])
    return steps.astype(np.float32).astype(bf16), turn.astype(np.float32)


def open_tables(steps_ref, turn_ref):
    blocks = [steps_ref[:, at * BLOCK : (at + 1) * BLOCK] for at in range(8)]
    turn = [
        jnp.broadcast_to(turn_ref[part][:, None, :], (BINS, HALF, BLOCK)).reshape(BINS * HALF, BLOCK)
        for part in range(2)
    ]
    enter, leave = jnp.concatenate(blocks[6:], 0), jnp.concatenate(blocks[4:6], 1)
    return enter, leave, blocks[:2], blocks[2:4], turn


def dot(first, second):
    return jnp.dot(first, second, preferred_element_type=f32)


def rotate(real, imag, turn):
    cosine, sine = turn
    own = imag.shape[0]
    turned_re = real[:own] * cosine[:own] - imag * sine[:own]
    turned_im = real[:own] * sine[:own] + imag * cosine[:own]
    turned_re = jnp.concatenate([turned_re, real[own:] * cosine[own:]], 0)
    turned_im = jnp.concatenate([turned_im, real[own:] * sine[own:]], 0)
    return turned_re, turned_im


def join(halves):
    parts = [half.reshape(BINS, HALF, NEAR) for half in halves]
    return jnp.concatenate(parts, 1).reshape(ROWS, NEAR).astype(bf16)


def enter_blocks(signal, enter):
    wide = signal.astype(f32)
    halves = [wide[:, half * HALF : (half + 1) * HALF].reshape(PARTS * HALF, BLOCK) for half in range(2)]
    return [dot(enter, half.astype(bf16)) for half in halves]


def finish_spectrum(halves, into, turn):
    pieces = ([], [], [], [])
    for mixed in halves:
        real, imag = rotate(mixed[: BINS * HALF], mixed[BINS * HALF :], turn)
        pieces[0].append(real[:, :NEAR] + real[:, NEAR:])
        pieces[1].append(imag[:, :NEAR] + imag[:, NEAR:])
        pieces[2].append(real[:, :NEAR] - real[:, NEAR:])
        pieces[3].append(imag[:, :NEAR] - imag[:, NEAR:])
    pieces = [join(piece) for piece in pieces]
    return [dot(jnp.concatenate(pieces[2 * odd : 2 * odd + 2], 1), into[odd]) for odd in range(2)]


def invert_inner(products, back):
    return [
        dot(jnp.concatenate([real.astype(bf16), imag.astype(bf16)], 1), matrix).reshape(BINS, PIECE, BLOCK)
        for (real, imag), matrix in zip(products, back, strict=True)
    ]


def finish_inverse(parts, leave, turn):
    outs = []
    for half in range(2):
        rows = slice(half * HALF, (half + 1) * HALF)
        even, odd = [part[:, rows].reshape(BINS * HALF, BLOCK) for part in parts]
        total, rest = even + odd, even - odd
        real = jnp.concatenate([total[:, :NEAR], rest[:, :NEAR]], 1)
        imag = jnp.concatenate([total[:, NEAR:], rest[:, NEAR:]], 1)
        own = (BINS - 2) * HALF
        turned_re = real * turn[0] - imag * turn[1]
        turned_im = real[:own] * turn[1][:own] + imag[:own] * turn[0][:own]
        turned = jnp.concatenate([turned_re, turned_im], 0).astype(bf16)
        outs.append(dot(leave, turned).reshape(PARTS, HALF, BLOCK))
    return jnp.concatenate(outs, 1)


def parts_of(values):
    return values[:, :NEAR], values[:, NEAR:]


def flat(pieces):
    return pieces.reshape(WIDTH, BLOCK)


def cut(rows):
    return rows.reshape(PARTS, PIECE, BLOCK)


def pack_kernel(mixed_ref, taps_ref, out_ref):
    out_ref[:, :PIECE, :] = cut(mixed_ref[...].T)
    out_ref[:, PIECE:, :] = cut(taps_ref[...].T)


def forward_kernel(in_ref, steps_ref, turn_ref, gate_ref, cot_ref, out_ref, gate_out, cot_out):
    gate_out[...] = gate_ref[...].T
    cot_out[...] = cot_ref[...].T
    enter, leave, into, back, turn = open_tables(steps_ref, turn_ref)
    first = enter_blocks(in_ref[:, :PIECE, :], enter)
    second = enter_blocks(in_ref[:, PIECE:, :], enter)
    first, second = [finish_spectrum(halves, into, turn) for halves in (first, second)]
    products = []
    for one, other in zip(first, second, strict=True):
        one_re, one_im = parts_of(one)
        other_re, other_im = parts_of(other)
        products.append((one_re * other_re - one_im * other_im, one_re * other_im + one_im * other_re))
    out_ref[...] = finish_inverse(invert_inner(products, back), leave, turn).astype(bf16)


def between_kernel(
    in_ref, steps_ref, turn_ref, key_ref, value_ref, conv_ref, pack_ref, gate_ref, cot_ref, skip_ref, gain_ref,
    after_ref, spec_ref, full_ref, push_ref, hold_ref,
):
    _, gate, gated = gate_parts(conv_ref, pack_ref, gate_ref, skip_ref)
    push_ref[...] = cot_ref[...].astype(f32) * column(gain_ref) * gate
    hold_ref[...] = gated * gate
    enter, _, into, _, turn = open_tables(steps_ref, turn_ref)
    for place in range(2):
        signal = in_ref[:, place * PIECE : (place + 1) * PIECE, :]
        even, odd = finish_spectrum(enter_blocks(signal, enter), into, turn)
        spec_ref[2 * place] = even
        spec_ref[2 * place + 1] = odd
    mixed = (key_ref[...].astype(f32) * value_ref[...].astype(f32)).astype(bf16)
    full_ref[...] = flat(conv_ref[...]).T.astype(f32) + skip_ref[...] * mixed.astype(f32)


def column(row_ref):
    turned = jnp.broadcast_to(row_ref[...], (128, WIDTH)).T
    return jnp.concatenate([turned, turned], 1)


def gate_parts(conv_ref, pack_ref, gate_ref, skip_ref):
    mixed = flat(pack_ref[:, :PIECE, :]).astype(f32)
    full = flat(conv_ref[...]).astype(f32) + column(skip_ref) * mixed
    gate = gate_ref[...].astype(f32)
    return full, gate, gate * full


def sums_kernel(conv_ref, pack_ref, gate_ref, cot_ref, skip_ref, gain_ref, out_ref):
    _, _, gated = gate_parts(conv_ref, pack_ref, gate_ref, skip_ref)
    scaled = cot_ref[...].astype(f32) * column(gain_ref)
    squares = jnp.sum(gated * gated, axis=0, keepdims=True)
    inner = jnp.sum(scaled * gated, axis=0, keepdims=True)
    out_ref[...] = jnp.concatenate([squares, inner], 0)


def norm_parts(sums_ref):
    sums = sums_ref[...]
    inv_rms = lax.rsqrt(sums[0:1] / D + epsilon)
    return inv_rms, inv_rms * inv_rms * inv_rms * sums[1:2] / D


def grad_kernel(sums_ref, push_ref, hold_ref, out_ref):
    inv_rms, pull = norm_parts(sums_ref)
    out_ref[...] = cut((inv_rms * push_ref[...] - pull * hold_ref[...]).astype(bf16))


def wide_column(row):
    turned = jnp.broadcast_to(row, (128, BLOCK)).T
    return jnp.concatenate([turned] * (WIDTH // 128), 1)


def backward_kernel(
    in_ref, pack_ref, spec_ref, steps_ref, turn_ref, sums_ref, full_ref, gate_ref, cot_ref, gain_ref,
    out_ref, grad_out, normed_out, gate_out,
):
    inv_rms, pull = (wide_column(row) for row in norm_parts(sums_ref))
    full, gate, gain = full_ref[...], gate_ref[...].astype(f32), gain_ref[...]
    gated = gate * full
    normed_out[...] = (gated * inv_rms * gain).astype(bf16)
    grad_gated = inv_rms * (cot_ref[...].astype(f32) * gain) - gated * pull
    gate_out[...] = (grad_gated * full).astype(bf16)
    grad_out[...] = (grad_gated * gate).astype(bf16)
    enter, leave, into, back, turn = open_tables(steps_ref, turn_ref)
    grad = in_ref[...]
    bias = jnp.sum(grad.astype(f32) * pack_ref[:, :PIECE, :].astype(f32), axis=0)
    bias = jnp.sum(bias, axis=1, keepdims=True)
    high = bias.astype(bf16).astype(f32)
    lane = lax.broadcasted_iota(jnp.int32, (TAIL, 128), 1)
    tail = jnp.zeros((TAIL, 128), f32)
    for at, part in enumerate((high[:HALF], (bias - high)[:HALF], high[HALF:], (bias - high)[HALF:])):
        tail = jnp.where(lane == at, part, tail)
    out_ref[:, 4 * PIECE :, :] = jnp.broadcast_to(tail.astype(bf16)[None], (PARTS, TAIL, 128))
    spectra = finish_spectrum(enter_blocks(grad, enter), into, turn)
    inverses = []
    for other in (1, 0):
        products = []
        for parity, mine in enumerate(spectra):
            real, imag = parts_of(spec_ref[2 * other + parity])
            mine_re, mine_im = parts_of(mine)
            products.append((real * mine_re + imag * mine_im, real * mine_im - imag * mine_re))
        inverses.append(invert_inner(products, back))
    for place, parts in enumerate(inverses):
        result = finish_inverse(parts, leave, turn).astype(bf16)
        out_ref[:, 2 * place * PIECE : (2 * place + 1) * PIECE, :] = result[:, :, :128]
        out_ref[:, (2 * place + 1) * PIECE : (2 * place + 2) * PIECE, :] = result[:, :, 128:]


def last_kernel(
    in_ref, grad_ref, key_ref, value_ref, skip_ref, normed_ref, gate_ref,
    key_out, value_out, taps_out, bias_out, normed_out, gate_out,
):
    normed_out[...] = normed_ref[...]
    gate_out[...] = gate_ref[...]

    def whole(place):
        at = 2 * place * PIECE
        left, right = in_ref[:, at : at + PIECE, :], in_ref[:, at + PIECE : at + 2 * PIECE, :]
        return jnp.concatenate([left.reshape(WIDTH, 128).T, right.reshape(WIDTH, 128).T], 0)

    grad_mixed = whole(0).astype(f32) + skip_ref[...] * grad_ref[...].astype(f32)
    key_out[...] = (grad_mixed * value_ref[...].astype(f32)).astype(bf16)
    value_out[...] = (grad_mixed * key_ref[...].astype(f32)).astype(bf16)
    taps_out[...] = whole(1)
    tail = in_ref[:, 4 * PIECE :, :].astype(f32)
    tail = jnp.concatenate([tail, pltpu.roll(tail, 126, 2)], 1).reshape(WIDTH, 128).T
    bias_out[...] = tail[0:1] + tail[1:2]


def call(kernel, name, outs, *operands):
    vmem = pl.BlockSpec(memory_space=pltpu.VMEM)
    return pl.pallas_call(
        kernel,
        name=name,
        out_shape=[jax.ShapeDtypeStruct(shape, kind) for shape, kind in outs],
        in_specs=[vmem] * len(operands),
        out_specs=[vmem] * len(outs),
        compiler_params=pltpu.CompilerParams(vmem_limit_bytes=32 * 1024 * 1024),
    )(*operands)


def add_over_pairs(sums):
    sums = sums + lax.ppermute(sums, "chan", [(at, at ^ 1) for at in range(GROUP)])
    return sums + lax.ppermute(sums, "chan", [(at, at ^ 2) for at in range(GROUP)])


def add_over_mirror(sums):
    mirror = [(at, (CHIPS - 1 - at // 2) * 2 + at % 2) for at in range(GROUP)]
    return sums + lax.ppermute(sums, "chan", mirror)


def on_device(gate_feat, key_feat, value_feat, filter_taps, skip_bias, norm_gain, cotangent):
    steps, turn = (jnp.asarray(table) for table in tables())
    skip_row, gain_row = skip_bias[None, :], norm_gain[None, :]
    natural = ((BLOCK, WIDTH), bf16)
    turned = ((WIDTH, BLOCK), bf16)
    pieces = ((PARTS, PIECE, BLOCK), bf16)
    spectra = ((4, ROWS, BLOCK), f32)

    mixed = (key_feat.astype(f32) * value_feat.astype(f32)).astype(bf16)
    taps = jnp.where(key_feat == key_feat, filter_taps, mixed)
    (packed,) = call(pack_kernel, "pack", [((PARTS, 2 * PIECE, BLOCK), bf16)], mixed, taps)
    arrived = lax.all_to_all(packed, "seq", 0, 0, tiled=True)
    conv, gate_t, cot_t = call(
        forward_kernel,
        "forward",
        [pieces, turned, turned],
        arrived,
        steps,
        turn,
        gate_feat,
        cotangent,
    )
    conv = lax.all_to_all(conv, "seq", 0, 0, tiled=True)
    sides = (conv, packed, gate_t, cot_t, skip_row, gain_row)
    (sums,) = call(sums_kernel, "sums", [((2, BLOCK), f32)], *sides)
    sums = add_over_pairs(sums)
    spec, full, push, hold = call(
        between_kernel,
        "between",
        [spectra, ((BLOCK, WIDTH), f32), ((WIDTH, BLOCK), f32), ((WIDTH, BLOCK), f32)],
        arrived,
        steps,
        turn,
        key_feat,
        value_feat,
        *sides,
        sums,
    )
    sums = add_over_mirror(sums)
    (grad,) = call(grad_kernel, "grad", [pieces], sums, push, hold)
    grad_arrived = lax.all_to_all(grad, "seq", 0, 0, tiled=True)
    result, grad_conv, normed, gate = call(
        backward_kernel,
        "backward",
        [((PARTS, 4 * PIECE + TAIL, 128), bf16), natural, natural, natural],
        grad_arrived,
        arrived,
        spec,
        steps,
        turn,
        sums,
        full,
        gate_feat,
        cotangent,
        gain_row,
    )
    result = lax.all_to_all(result, "seq", 0, 0, tiled=True)
    grad_key, grad_value, grad_filter, grad_bias, normed_out, grad_gate = call(
        last_kernel,
        "last",
        [natural] * 3 + [((1, WIDTH), f32)] + [natural] * 2,
        result,
        grad_conv,
        key_feat,
        value_feat,
        skip_row,
        normed,
        gate,
    )
    return normed_out, grad_gate, grad_key, grad_value, grad_filter, grad_bias[0]


def solution(mesh):
    wide, row = P("seq", "chan"), P("chan")
    return jax.shard_map(
        on_device,
        mesh=mesh,
        in_specs=(wide, wide, wide, wide, row, row, wide),
        out_specs=(wide, wide, wide, wide, wide, row),
        check_vma=False,
    )
```

```python
import jax
import jax.numpy as jnp
import numpy as np
from jax import lax
from jax.experimental import pallas as pl
from jax.experimental.pallas import tpu as pltpu
from jax.sharding import PartitionSpec as P

D = 4096
LENGTH = 8192
epsilon = 1e-05

f32, bf16 = jnp.float32, jnp.bfloat16

PARTS = 32
GROUP = 8
BLOCK = LENGTH // PARTS
WIDTH = D // GROUP
PIECE = WIDTH // PARTS
HALF = PIECE // 2
NEAR = BLOCK // 2
FULL = 2 * LENGTH
SPAN = 2 * PARTS
BINS = PARTS + 1
ROWS = BINS * PIECE
TAIL = 8
CHIPS = GROUP // 2


def tables():
    low = np.array(list(range(1, PARTS)) + [0, PARTS])
    block, inside, near = np.arange(PARTS), np.arange(BLOCK), np.arange(NEAR)
    outer = 2 * np.pi * (low[:, None] * block[None, :] % SPAN) / SPAN
    cosine, sine = np.cos(outer), np.sin(outer)
    eye = np.eye(HALF)
    enter = np.kron(np.concatenate([cosine, -sine[: PARTS - 1]], 0), eye)
    weight = np.where((low == 0) | (low == PARTS), 1.0, 2.0)[:, None] / 4
    leave = np.kron(np.concatenate([cosine * weight, (sine * weight)[: PARTS - 1]], 0).T, eye)
    into, back = [], []
    for odd in range(2):
        inner = 2 * np.pi * (near[:, None] * (2 * near[None, :] + odd) % BLOCK) / BLOCK
        cosine, sine = np.cos(inner) / 16, -np.sin(inner) / 16
        into.append(np.block([[cosine, sine], [-sine, cosine]]))
        back.append(np.block([[cosine.T, sine.T], [sine.T, -cosine.T]]))
    half = SPAN * HALF // 2
    steps = np.concatenate([*into, *back, leave, enter[:half], enter[half:]], 1)
    turn = 2 * np.pi * (low[:, None] * inside[None, :] % FULL) / FULL
    turn = np.stack([np.cos(turn), -np.sin(turn)])
    return steps.astype(np.float32).astype(bf16), turn.astype(np.float32)


def open_tables(steps_ref, turn_ref):
    blocks = [steps_ref[:, at * BLOCK : (at + 1) * BLOCK] for at in range(8)]
    turn = [
        jnp.broadcast_to(turn_ref[part][:, None, :], (BINS, HALF, BLOCK)).reshape(BINS * HALF, BLOCK)
        for part in range(2)
    ]
    enter, leave = jnp.concatenate(blocks[6:], 0), jnp.concatenate(blocks[4:6], 1)
    return enter, leave, blocks[:2], blocks[2:4], turn


def dot(first, second):
    return jnp.dot(first, second, preferred_element_type=f32)


def rotate(real, imag, turn):
    cosine, sine = turn
    own = imag.shape[0]
    turned_re = real[:own] * cosine[:own] - imag * sine[:own]
    turned_im = real[:own] * sine[:own] + imag * cosine[:own]
    turned_re = jnp.concatenate([turned_re, real[own:] * cosine[own:]], 0)
    turned_im = jnp.concatenate([turned_im, real[own:] * sine[own:]], 0)
    return turned_re, turned_im


def join(halves):
    parts = [half.reshape(BINS, HALF, NEAR) for half in halves]
    return jnp.concatenate(parts, 1).reshape(ROWS, NEAR).astype(bf16)


def enter_blocks(signal, enter):
    wide = signal.astype(f32)
    halves = [wide[:, half * HALF : (half + 1) * HALF].reshape(PARTS * HALF, BLOCK) for half in range(2)]
    return [dot(enter, half.astype(bf16)) for half in halves]


def finish_spectrum(halves, into, turn):
    pieces = ([], [], [], [])
    for mixed in halves:
        real, imag = rotate(mixed[: BINS * HALF], mixed[BINS * HALF :], turn)
        pieces[0].append(real[:, :NEAR] + real[:, NEAR:])
        pieces[1].append(imag[:, :NEAR] + imag[:, NEAR:])
        pieces[2].append(real[:, :NEAR] - real[:, NEAR:])
        pieces[3].append(imag[:, :NEAR] - imag[:, NEAR:])
    pieces = [join(piece) for piece in pieces]
    return [dot(jnp.concatenate(pieces[2 * odd : 2 * odd + 2], 1), into[odd]) for odd in range(2)]


def invert_inner(products, back):
    return [
        dot(jnp.concatenate([real.astype(bf16), imag.astype(bf16)], 1), matrix).reshape(BINS, PIECE, BLOCK)
        for (real, imag), matrix in zip(products, back, strict=True)
    ]


def finish_inverse(parts, leave, turn):
    outs = []
    for half in range(2):
        rows = slice(half * HALF, (half + 1) * HALF)
        even, odd = [part[:, rows].reshape(BINS * HALF, BLOCK) for part in parts]
        total, rest = even + odd, even - odd
        real = jnp.concatenate([total[:, :NEAR], rest[:, :NEAR]], 1)
        imag = jnp.concatenate([total[:, NEAR:], rest[:, NEAR:]], 1)
        own = (BINS - 2) * HALF
        turned_re = real * turn[0] - imag * turn[1]
        turned_im = real[:own] * turn[1][:own] + imag[:own] * turn[0][:own]
        turned = jnp.concatenate([turned_re, turned_im], 0).astype(bf16)
        outs.append(dot(leave, turned).reshape(PARTS, HALF, BLOCK))
    return jnp.concatenate(outs, 1)


def parts_of(values):
    return values[:, :NEAR], values[:, NEAR:]


def flat(pieces):
    return pieces.reshape(WIDTH, BLOCK)


def cut(rows):
    return rows.reshape(PARTS, PIECE, BLOCK)


def early_kernel(out_ref):
    out_ref[...] = jnp.zeros_like(out_ref)


def pack_kernel(key_ref, value_ref, taps_ref, after_ref, out_ref):
    mixed = (key_ref[...].astype(f32) * value_ref[...].astype(f32)).astype(bf16)
    out_ref[:, :PIECE, :] = cut(mixed.T)
    out_ref[:, PIECE:, :] = cut(taps_ref[...].T)


def forward_kernel(in_ref, steps_ref, turn_ref, gate_ref, cot_ref, out_ref, gate_out, cot_out):
    gate_out[...] = gate_ref[...].T
    cot_out[...] = cot_ref[...].T
    enter, leave, into, back, turn = open_tables(steps_ref, turn_ref)
    first = enter_blocks(in_ref[:, :PIECE, :], enter)
    second = enter_blocks(in_ref[:, PIECE:, :], enter)
    first, second = [finish_spectrum(halves, into, turn) for halves in (first, second)]
    products = []
    for one, other in zip(first, second, strict=True):
        one_re, one_im = parts_of(one)
        other_re, other_im = parts_of(other)
        products.append((one_re * other_re - one_im * other_im, one_re * other_im + one_im * other_re))
    out_ref[...] = finish_inverse(invert_inner(products, back), leave, turn).astype(bf16)


def between_kernel(
    in_ref, steps_ref, turn_ref, key_ref, value_ref, conv_ref, pack_ref, gate_ref, cot_ref, skip_ref, gain_ref,
    after_ref, spec_ref, full_ref, push_ref, hold_ref,
):
    _, gate, gated = gate_parts(conv_ref, pack_ref, gate_ref, skip_ref)
    push_ref[...] = cot_ref[...].astype(f32) * column(gain_ref) * gate
    hold_ref[...] = gated * gate
    enter, _, into, _, turn = open_tables(steps_ref, turn_ref)
    for place in range(2):
        signal = in_ref[:, place * PIECE : (place + 1) * PIECE, :]
        even, odd = finish_spectrum(enter_blocks(signal, enter), into, turn)
        spec_ref[2 * place] = even
        spec_ref[2 * place + 1] = odd
    mixed = (key_ref[...].astype(f32) * value_ref[...].astype(f32)).astype(bf16)
    full_ref[...] = flat(conv_ref[...]).T.astype(f32) + skip_ref[...] * mixed.astype(f32)


def column(row_ref):
    turned = jnp.broadcast_to(row_ref[...], (128, WIDTH)).T
    return jnp.concatenate([turned, turned], 1)


def gate_parts(conv_ref, pack_ref, gate_ref, skip_ref):
    mixed = flat(pack_ref[:, :PIECE, :]).astype(f32)
    full = flat(conv_ref[...]).astype(f32) + column(skip_ref) * mixed
    gate = gate_ref[...].astype(f32)
    return full, gate, gate * full


def sums_kernel(conv_ref, pack_ref, gate_ref, cot_ref, skip_ref, gain_ref, out_ref):
    _, _, gated = gate_parts(conv_ref, pack_ref, gate_ref, skip_ref)
    scaled = cot_ref[...].astype(f32) * column(gain_ref)
    squares = jnp.sum(gated * gated, axis=0, keepdims=True)
    inner = jnp.sum(scaled * gated, axis=0, keepdims=True)
    out_ref[...] = jnp.concatenate([squares, inner], 0)


def norm_parts(sums_ref):
    sums = sums_ref[...]
    inv_rms = lax.rsqrt(sums[0:1] / D + epsilon)
    return inv_rms, inv_rms * inv_rms * inv_rms * sums[1:2] / D


def grad_kernel(sums_ref, push_ref, hold_ref, out_ref):
    inv_rms, pull = norm_parts(sums_ref)
    out_ref[...] = cut((inv_rms * push_ref[...] - pull * hold_ref[...]).astype(bf16))


def wide_column(row):
    turned = jnp.broadcast_to(row, (128, BLOCK)).T
    return jnp.concatenate([turned] * (WIDTH // 128), 1)


def backward_kernel(
    in_ref, pack_ref, spec_ref, steps_ref, turn_ref, sums_ref, full_ref, gate_ref, cot_ref, gain_ref,
    out_ref, grad_out, normed_out, gate_out,
):
    inv_rms, pull = (wide_column(row) for row in norm_parts(sums_ref))
    full, gate, gain = full_ref[...], gate_ref[...].astype(f32), gain_ref[...]
    gated = gate * full
    normed_out[...] = (gated * inv_rms * gain).astype(bf16)
    grad_gated = inv_rms * (cot_ref[...].astype(f32) * gain) - gated * pull
    gate_out[...] = (grad_gated * full).astype(bf16)
    grad_out[...] = (grad_gated * gate).astype(bf16)
    enter, leave, into, back, turn = open_tables(steps_ref, turn_ref)
    grad = in_ref[...]
    bias = jnp.sum(grad.astype(f32) * pack_ref[:, :PIECE, :].astype(f32), axis=0)
    bias = jnp.sum(bias, axis=1, keepdims=True)
    high = bias.astype(bf16).astype(f32)
    lane = lax.broadcasted_iota(jnp.int32, (TAIL, 128), 1)
    tail = jnp.zeros((TAIL, 128), f32)
    for at, part in enumerate((high[:HALF], (bias - high)[:HALF], high[HALF:], (bias - high)[HALF:])):
        tail = jnp.where(lane == at, part, tail)
    out_ref[:, 4 * PIECE :, :] = jnp.broadcast_to(tail.astype(bf16)[None], (PARTS, TAIL, 128))
    spectra = finish_spectrum(enter_blocks(grad, enter), into, turn)
    inverses = []
    for other in (1, 0):
        products = []
        for parity, mine in enumerate(spectra):
            real, imag = parts_of(spec_ref[2 * other + parity])
            mine_re, mine_im = parts_of(mine)
            products.append((real * mine_re + imag * mine_im, real * mine_im - imag * mine_re))
        inverses.append(invert_inner(products, back))
    for place, parts in enumerate(inverses):
        result = finish_inverse(parts, leave, turn).astype(bf16)
        out_ref[:, 2 * place * PIECE : (2 * place + 1) * PIECE, :] = result[:, :, :128]
        out_ref[:, (2 * place + 1) * PIECE : (2 * place + 2) * PIECE, :] = result[:, :, 128:]


def last_kernel(
    in_ref, grad_ref, key_ref, value_ref, skip_ref, normed_ref, gate_ref,
    key_hbm, value_hbm, taps_hbm, bias_hbm, normed_hbm, gate_hbm,
    key_out, value_out, taps_out, bias_out, sems,
):
    copies = []

    def send(source, target):
        copies.append(pltpu.make_async_copy(source, target, sems.at[len(copies)]))
        copies[-1].start()

    def whole(place):
        at = 2 * place * PIECE
        left, right = in_ref[:, at : at + PIECE, :], in_ref[:, at + PIECE : at + 2 * PIECE, :]
        return jnp.concatenate([left.reshape(WIDTH, 128).T, right.reshape(WIDTH, 128).T], 0)

    send(normed_ref, normed_hbm)
    send(gate_ref, gate_hbm)
    tail = in_ref[:, 4 * PIECE :, :].astype(f32)
    tail = jnp.concatenate([tail, pltpu.roll(tail, 126, 2)], 1).reshape(WIDTH, 128).T
    bias_out[...] = tail[0:1] + tail[1:2]
    taps_out[...] = whole(1)
    grad_mixed = whole(0).astype(f32) + skip_ref[...] * grad_ref[...].astype(f32)
    key_out[...] = (grad_mixed * value_ref[...].astype(f32)).astype(bf16)
    value_out[...] = (grad_mixed * key_ref[...].astype(f32)).astype(bf16)
    for source, target in ((bias_out, bias_hbm), (taps_out, taps_hbm), (key_out, key_hbm), (value_out, value_hbm)):
        send(source, target)
    for copy in copies:
        copy.wait()


def call(kernel, name, outs, *operands, cost=None, out_space=pltpu.VMEM, scratch=()):
    vmem = pl.BlockSpec(memory_space=pltpu.VMEM)
    return pl.pallas_call(
        kernel,
        name=name,
        out_shape=[jax.ShapeDtypeStruct(shape, kind) for shape, kind in outs],
        in_specs=[vmem] * len(operands),
        out_specs=[pl.BlockSpec(memory_space=out_space)] * len(outs),
        scratch_shapes=list(scratch),
        cost_estimate=cost,
        compiler_params=pltpu.CompilerParams(vmem_limit_bytes=32 * 1024 * 1024),
    )(*operands)


def add_over_pairs(sums):
    sums = sums + lax.ppermute(sums, "chan", [(at, at ^ 1) for at in range(GROUP)])
    return sums + lax.ppermute(sums, "chan", [(at, at ^ 2) for at in range(GROUP)])


def add_over_mirror(sums):
    mirror = [(at, (CHIPS - 1 - at // 2) * 2 + at % 2) for at in range(GROUP)]
    return sums + lax.ppermute(sums, "chan", mirror)


def on_device(gate_feat, key_feat, value_feat, filter_taps, skip_bias, norm_gain, cotangent):
    steps, turn = (jnp.asarray(table) for table in tables())
    skip_row, gain_row = skip_bias[None, :], norm_gain[None, :]
    natural = ((BLOCK, WIDTH), bf16)
    turned = ((WIDTH, BLOCK), bf16)
    pieces = ((PARTS, PIECE, BLOCK), bf16)
    spectra = ((4, ROWS, BLOCK), f32)

    (token,) = call(
        early_kernel,
        "early",
        [((8, 128), f32)],
        cost=pl.CostEstimate(flops=2_000_000_000, bytes_accessed=4096, transcendentals=0),
    )
    (packed,) = call(
        pack_kernel, "pack", [((PARTS, 2 * PIECE, BLOCK), bf16)], key_feat, value_feat, filter_taps, token
    )
    arrived = lax.all_to_all(packed, "seq", 0, 0, tiled=True)
    conv, gate_t, cot_t = call(
        forward_kernel,
        "forward",
        [pieces, turned, turned],
        arrived,
        steps,
        turn,
        gate_feat,
        cotangent,
    )
    conv = lax.all_to_all(conv, "seq", 0, 0, tiled=True)
    sides = (conv, packed, gate_t, cot_t, skip_row, gain_row)
    (sums,) = call(sums_kernel, "sums", [((2, BLOCK), f32)], *sides)
    sums = add_over_pairs(sums)
    spec, full, push, hold = call(
        between_kernel,
        "between",
        [spectra, ((BLOCK, WIDTH), f32), ((WIDTH, BLOCK), f32), ((WIDTH, BLOCK), f32)],
        arrived,
        steps,
        turn,
        key_feat,
        value_feat,
        *sides,
        sums,
    )
    sums = add_over_mirror(sums)
    (grad,) = call(grad_kernel, "grad", [pieces], sums, push, hold)
    grad_arrived = lax.all_to_all(grad, "seq", 0, 0, tiled=True)
    result, grad_conv, normed, gate = call(
        backward_kernel,
        "backward",
        [((PARTS, 4 * PIECE + TAIL, 128), bf16), natural, natural, natural],
        grad_arrived,
        arrived,
        spec,
        steps,
        turn,
        sums,
        full,
        gate_feat,
        cotangent,
        gain_row,
    )
    result = lax.all_to_all(result, "seq", 0, 0, tiled=True)
    grad_key, grad_value, grad_filter, grad_bias, normed_out, grad_gate = call(
        last_kernel,
        "last",
        [natural] * 3 + [((1, WIDTH), f32)] + [natural] * 2,
        result,
        grad_conv,
        key_feat,
        value_feat,
        skip_row,
        normed,
        gate,
        out_space=pltpu.HBM,
        scratch=[pltpu.VMEM(*natural)] * 3 + [pltpu.VMEM((1, WIDTH), f32), pltpu.SemaphoreType.DMA((6,))],
    )
    return normed_out, grad_gate, grad_key, grad_value, grad_filter, grad_bias[0]


def solution(mesh):
    wide, row = P("seq", "chan"), P("chan")
    return jax.shard_map(
        on_device,
        mesh=mesh,
        in_specs=(wide, wide, wide, wide, row, row, wide),
        out_specs=(wide, wide, wide, wide, wide, row),
        check_vma=False,
    )
```

```python
import jax
import jax.numpy as jnp
import numpy as np
from jax import lax
from jax.experimental import pallas as pl
from jax.experimental.pallas import tpu as pltpu
from jax.sharding import PartitionSpec as P

D = 4096
LENGTH = 8192
epsilon = 1e-05

f32, bf16 = jnp.float32, jnp.bfloat16

PARTS = 32
GROUP = 8
BLOCK = LENGTH // PARTS
WIDTH = D // GROUP
PIECE = WIDTH // PARTS
HALF = PIECE // 2
NEAR = BLOCK // 2
FULL = 2 * LENGTH
SPAN = 2 * PARTS
BINS = PARTS + 1
ROWS = BINS * PIECE
TAIL = 8
CHIPS = GROUP // 2


def tables():
    low = np.array(list(range(1, PARTS)) + [0, PARTS])
    block, inside, near = np.arange(PARTS), np.arange(BLOCK), np.arange(NEAR)
    outer = 2 * np.pi * (low[:, None] * block[None, :] % SPAN) / SPAN
    cosine, sine = np.cos(outer), np.sin(outer)
    eye = np.eye(HALF)
    enter = np.kron(np.concatenate([cosine, -sine[: PARTS - 1]], 0), eye)
    weight = np.where((low == 0) | (low == PARTS), 1.0, 2.0)[:, None] / 4
    leave = np.kron(np.concatenate([cosine * weight, (sine * weight)[: PARTS - 1]], 0).T, eye)
    into, back = [], []
    for odd in range(2):
        inner = 2 * np.pi * (near[:, None] * (2 * near[None, :] + odd) % BLOCK) / BLOCK
        cosine, sine = np.cos(inner) / 16, -np.sin(inner) / 16
        into.append(np.block([[cosine, sine], [-sine, cosine]]))
        back.append(np.block([[cosine.T, sine.T], [sine.T, -cosine.T]]))
    half = SPAN * HALF // 2
    steps = np.concatenate([*into, *back, leave, enter[:half], enter[half:]], 1)
    turn = 2 * np.pi * (low[:, None] * inside[None, :] % FULL) / FULL
    turn = np.stack([np.cos(turn), -np.sin(turn)])
    return steps.astype(np.float32).astype(bf16), turn.astype(np.float32)


def open_tables(steps_ref, turn_ref):
    blocks = [steps_ref[:, at * BLOCK : (at + 1) * BLOCK] for at in range(8)]
    turn = [
        jnp.broadcast_to(turn_ref[part][:, None, :], (BINS, HALF, BLOCK)).reshape(BINS * HALF, BLOCK)
        for part in range(2)
    ]
    enter, leave = jnp.concatenate(blocks[6:], 0), jnp.concatenate(blocks[4:6], 1)
    return enter, leave, blocks[:2], blocks[2:4], turn


def dot(first, second):
    return jnp.dot(first, second, preferred_element_type=f32)


def rotate(real, imag, turn):
    cosine, sine = turn
    own = imag.shape[0]
    turned_re = real[:own] * cosine[:own] - imag * sine[:own]
    turned_im = real[:own] * sine[:own] + imag * cosine[:own]
    turned_re = jnp.concatenate([turned_re, real[own:] * cosine[own:]], 0)
    turned_im = jnp.concatenate([turned_im, real[own:] * sine[own:]], 0)
    return turned_re, turned_im


def join(halves):
    parts = [half.reshape(BINS, HALF, NEAR) for half in halves]
    return jnp.concatenate(parts, 1).reshape(ROWS, NEAR).astype(bf16)


def enter_blocks(signal, enter):
    wide = signal.astype(f32)
    halves = [wide[:, half * HALF : (half + 1) * HALF].reshape(PARTS * HALF, BLOCK) for half in range(2)]
    return [dot(enter, half.astype(bf16)) for half in halves]


def finish_spectrum(halves, into, turn):
    pieces = ([], [], [], [])
    for mixed in halves:
        real, imag = rotate(mixed[: BINS * HALF], mixed[BINS * HALF :], turn)
        pieces[0].append(real[:, :NEAR] + real[:, NEAR:])
        pieces[1].append(imag[:, :NEAR] + imag[:, NEAR:])
        pieces[2].append(real[:, :NEAR] - real[:, NEAR:])
        pieces[3].append(imag[:, :NEAR] - imag[:, NEAR:])
    pieces = [join(piece) for piece in pieces]
    return [dot(jnp.concatenate(pieces[2 * odd : 2 * odd + 2], 1), into[odd]) for odd in range(2)]


def invert_inner(products, back):
    return [
        dot(jnp.concatenate([real.astype(bf16), imag.astype(bf16)], 1), matrix).reshape(BINS, PIECE, BLOCK)
        for (real, imag), matrix in zip(products, back, strict=True)
    ]


def finish_inverse(parts, leave, turn):
    outs = []
    for half in range(2):
        rows = slice(half * HALF, (half + 1) * HALF)
        even, odd = [part[:, rows].reshape(BINS * HALF, BLOCK) for part in parts]
        total, rest = even + odd, even - odd
        real = jnp.concatenate([total[:, :NEAR], rest[:, :NEAR]], 1)
        imag = jnp.concatenate([total[:, NEAR:], rest[:, NEAR:]], 1)
        own = (BINS - 2) * HALF
        turned_re = real * turn[0] - imag * turn[1]
        turned_im = real[:own] * turn[1][:own] + imag[:own] * turn[0][:own]
        turned = jnp.concatenate([turned_re, turned_im], 0).astype(bf16)
        outs.append(dot(leave, turned).reshape(PARTS, HALF, BLOCK))
    return jnp.concatenate(outs, 1)


def parts_of(values):
    return values[:, :NEAR], values[:, NEAR:]


def flat(pieces):
    return pieces.reshape(WIDTH, BLOCK)


def cut(rows):
    return rows.reshape(PARTS, PIECE, BLOCK)


def early_kernel(out_ref):
    out_ref[...] = jnp.zeros_like(out_ref)


def pack_kernel(key_ref, value_ref, taps_ref, after_ref, out_ref):
    mixed = (key_ref[...].astype(f32) * value_ref[...].astype(f32)).astype(bf16)
    out_ref[:, :PIECE, :] = cut(mixed.T)
    out_ref[:, PIECE:, :] = cut(taps_ref[...].T)


def forward_kernel(
    in_ref, steps_ref, turn_ref, gate_ref, cot_ref, pack_ref, skip_ref, gain_ref,
    out_ref, gate_out, scaled_out, skipped_out,
):
    gate = gate_ref[...].T
    gate_out[...] = gate
    scaled_out[...] = cot_ref[...].T.astype(f32) * column(gain_ref)
    skipped_out[...] = flat(pack_ref[:, :PIECE, :]).astype(f32) * column(skip_ref) * gate.astype(f32)
    enter, leave, into, back, turn = open_tables(steps_ref, turn_ref)
    first = enter_blocks(in_ref[:, :PIECE, :], enter)
    second = enter_blocks(in_ref[:, PIECE:, :], enter)
    first, second = [finish_spectrum(halves, into, turn) for halves in (first, second)]
    products = []
    for one, other in zip(first, second, strict=True):
        one_re, one_im = parts_of(one)
        other_re, other_im = parts_of(other)
        products.append((one_re * other_re - one_im * other_im, one_re * other_im + one_im * other_re))
    out_ref[...] = finish_inverse(invert_inner(products, back), leave, turn).astype(bf16)


def between_kernel(
    in_ref, steps_ref, turn_ref, key_ref, value_ref, skip_ref, conv_ref, gate_ref, scaled_ref, skipped_ref,
    after_ref, spec_ref, full_ref, push_ref, hold_ref,
):
    gate, gated = gate_parts(conv_ref, gate_ref, skipped_ref)
    push_ref[...] = scaled_ref[...] * gate
    hold_ref[...] = gated * gate
    enter, _, into, _, turn = open_tables(steps_ref, turn_ref)
    for place in range(2):
        signal = in_ref[:, place * PIECE : (place + 1) * PIECE, :]
        even, odd = finish_spectrum(enter_blocks(signal, enter), into, turn)
        spec_ref[2 * place] = even
        spec_ref[2 * place + 1] = odd
    mixed = (key_ref[...].astype(f32) * value_ref[...].astype(f32)).astype(bf16)
    full_ref[...] = flat(conv_ref[...]).T.astype(f32) + skip_ref[...] * mixed.astype(f32)


def column(row_ref):
    turned = jnp.broadcast_to(row_ref[...], (128, WIDTH)).T
    return jnp.concatenate([turned, turned], 1)


def gate_parts(conv_ref, gate_ref, skipped_ref):
    gate = gate_ref[...].astype(f32)
    return gate, gate * flat(conv_ref[...]).astype(f32) + skipped_ref[...]


def sums_kernel(conv_ref, gate_ref, scaled_ref, skipped_ref, out_ref):
    _, gated = gate_parts(conv_ref, gate_ref, skipped_ref)
    squares = jnp.sum(gated * gated, axis=0, keepdims=True)
    inner = jnp.sum(scaled_ref[...] * gated, axis=0, keepdims=True)
    out_ref[...] = jnp.concatenate([squares, inner], 0)


def norm_parts(sums_ref):
    sums = sums_ref[...]
    inv_rms = lax.rsqrt(sums[0:1] / D + epsilon)
    return inv_rms, inv_rms * inv_rms * inv_rms * sums[1:2] / D


def grad_kernel(sums_ref, push_ref, hold_ref, out_ref):
    inv_rms, pull = norm_parts(sums_ref)
    out_ref[...] = cut((inv_rms * push_ref[...] - pull * hold_ref[...]).astype(bf16))


def wide_column(row):
    turned = jnp.broadcast_to(row, (128, BLOCK)).T
    return jnp.concatenate([turned] * (WIDTH // 128), 1)


def backward_kernel(
    in_ref, pack_ref, spec_ref, steps_ref, turn_ref, sums_ref, full_ref, gate_ref, cot_ref, gain_ref,
    out_ref, grad_out, normed_out, gate_out,
):
    inv_rms, pull = (wide_column(row) for row in norm_parts(sums_ref))
    full, gate, gain = full_ref[...], gate_ref[...].astype(f32), gain_ref[...]
    gated = gate * full
    normed_out[...] = (gated * inv_rms * gain).astype(bf16)
    grad_gated = inv_rms * (cot_ref[...].astype(f32) * gain) - gated * pull
    gate_out[...] = (grad_gated * full).astype(bf16)
    grad_out[...] = (grad_gated * gate).astype(bf16)
    enter, leave, into, back, turn = open_tables(steps_ref, turn_ref)
    grad = in_ref[...]
    bias = jnp.sum(grad.astype(f32) * pack_ref[:, :PIECE, :].astype(f32), axis=0)
    bias = jnp.sum(bias, axis=1, keepdims=True)
    high = bias.astype(bf16).astype(f32)
    lane = lax.broadcasted_iota(jnp.int32, (TAIL, 128), 1)
    tail = jnp.zeros((TAIL, 128), f32)
    for at, part in enumerate((high[:HALF], (bias - high)[:HALF], high[HALF:], (bias - high)[HALF:])):
        tail = jnp.where(lane == at, part, tail)
    out_ref[:, 4 * PIECE :, :] = jnp.broadcast_to(tail.astype(bf16)[None], (PARTS, TAIL, 128))
    spectra = finish_spectrum(enter_blocks(grad, enter), into, turn)
    inverses = []
    for other in (1, 0):
        products = []
        for parity, mine in enumerate(spectra):
            real, imag = parts_of(spec_ref[2 * other + parity])
            mine_re, mine_im = parts_of(mine)
            products.append((real * mine_re + imag * mine_im, real * mine_im - imag * mine_re))
        inverses.append(invert_inner(products, back))
    for place, parts in enumerate(inverses):
        result = finish_inverse(parts, leave, turn).astype(bf16)
        out_ref[:, 2 * place * PIECE : (2 * place + 1) * PIECE, :] = result[:, :, :128]
        out_ref[:, (2 * place + 1) * PIECE : (2 * place + 2) * PIECE, :] = result[:, :, 128:]


def last_kernel(
    in_ref, grad_ref, key_ref, value_ref, skip_ref, normed_ref, gate_ref,
    key_hbm, value_hbm, taps_hbm, bias_hbm, normed_hbm, gate_hbm,
    key_out, value_out, taps_out, bias_out, sems,
):
    copies = []

    def send(source, target):
        copies.append(pltpu.make_async_copy(source, target, sems.at[len(copies)]))
        copies[-1].start()

    def whole(place):
        at = 2 * place * PIECE
        left, right = in_ref[:, at : at + PIECE, :], in_ref[:, at + PIECE : at + 2 * PIECE, :]
        return jnp.concatenate([left.reshape(WIDTH, 128).T, right.reshape(WIDTH, 128).T], 0)

    send(normed_ref, normed_hbm)
    send(gate_ref, gate_hbm)
    tail = in_ref[:, 4 * PIECE :, :].astype(f32)
    tail = jnp.concatenate([tail, pltpu.roll(tail, 126, 2)], 1).reshape(WIDTH, 128).T
    bias_out[...] = tail[0:1] + tail[1:2]
    taps_out[...] = whole(1)
    grad_mixed = whole(0).astype(f32) + skip_ref[...] * grad_ref[...].astype(f32)
    key_out[...] = (grad_mixed * value_ref[...].astype(f32)).astype(bf16)
    value_out[...] = (grad_mixed * key_ref[...].astype(f32)).astype(bf16)
    for source, target in ((bias_out, bias_hbm), (taps_out, taps_hbm), (key_out, key_hbm), (value_out, value_hbm)):
        send(source, target)
    for copy in copies:
        copy.wait()


def call(kernel, name, outs, *operands, cost=None, out_space=pltpu.VMEM, scratch=()):
    vmem = pl.BlockSpec(memory_space=pltpu.VMEM)
    return pl.pallas_call(
        kernel,
        name=name,
        out_shape=[jax.ShapeDtypeStruct(shape, kind) for shape, kind in outs],
        in_specs=[vmem] * len(operands),
        out_specs=[pl.BlockSpec(memory_space=out_space)] * len(outs),
        scratch_shapes=list(scratch),
        cost_estimate=cost,
        compiler_params=pltpu.CompilerParams(vmem_limit_bytes=32 * 1024 * 1024),
    )(*operands)


def add_over_pairs(sums):
    sums = sums + lax.ppermute(sums, "chan", [(at, at ^ 1) for at in range(GROUP)])
    return sums + lax.ppermute(sums, "chan", [(at, at ^ 2) for at in range(GROUP)])


def add_over_mirror(sums):
    mirror = [(at, (CHIPS - 1 - at // 2) * 2 + at % 2) for at in range(GROUP)]
    return sums + lax.ppermute(sums, "chan", mirror)


def on_device(gate_feat, key_feat, value_feat, filter_taps, skip_bias, norm_gain, cotangent):
    steps, turn = (jnp.asarray(table) for table in tables())
    skip_row, gain_row = skip_bias[None, :], norm_gain[None, :]
    natural = ((BLOCK, WIDTH), bf16)
    pieces = ((PARTS, PIECE, BLOCK), bf16)
    spectra = ((4, ROWS, BLOCK), f32)

    (token,) = call(
        early_kernel,
        "early",
        [((8, 128), f32)],
        cost=pl.CostEstimate(flops=2_000_000_000, bytes_accessed=4096, transcendentals=0),
    )
    (packed,) = call(
        pack_kernel, "pack", [((PARTS, 2 * PIECE, BLOCK), bf16)], key_feat, value_feat, filter_taps, token
    )
    arrived = lax.all_to_all(packed, "seq", 0, 0, tiled=True)
    conv, gate_t, scaled_t, skipped_t = call(
        forward_kernel,
        "forward",
        [pieces, ((WIDTH, BLOCK), bf16), ((WIDTH, BLOCK), f32), ((WIDTH, BLOCK), f32)],
        arrived,
        steps,
        turn,
        gate_feat,
        cotangent,
        packed,
        skip_row,
        gain_row,
    )
    conv = lax.all_to_all(conv, "seq", 0, 0, tiled=True)
    sides = (conv, gate_t, scaled_t, skipped_t)
    (sums,) = call(sums_kernel, "sums", [((2, BLOCK), f32)], *sides)
    sums = add_over_pairs(sums)
    spec, full, push, hold = call(
        between_kernel,
        "between",
        [spectra, ((BLOCK, WIDTH), f32), ((WIDTH, BLOCK), f32), ((WIDTH, BLOCK), f32)],
        arrived,
        steps,
        turn,
        key_feat,
        value_feat,
        skip_row,
        *sides,
        sums,
    )
    sums = add_over_mirror(sums)
    (grad,) = call(grad_kernel, "grad", [pieces], sums, push, hold)
    grad_arrived = lax.all_to_all(grad, "seq", 0, 0, tiled=True)
    result, grad_conv, normed, gate = call(
        backward_kernel,
        "backward",
        [((PARTS, 4 * PIECE + TAIL, 128), bf16), natural, natural, natural],
        grad_arrived,
        arrived,
        spec,
        steps,
        turn,
        sums,
        full,
        gate_feat,
        cotangent,
        gain_row,
    )
    result = lax.all_to_all(result, "seq", 0, 0, tiled=True)
    grad_key, grad_value, grad_filter, grad_bias, normed_out, grad_gate = call(
        last_kernel,
        "last",
        [natural] * 3 + [((1, WIDTH), f32)] + [natural] * 2,
        result,
        grad_conv,
        key_feat,
        value_feat,
        skip_row,
        normed,
        gate,
        out_space=pltpu.HBM,
        scratch=[pltpu.VMEM(*natural)] * 3 + [pltpu.VMEM((1, WIDTH), f32), pltpu.SemaphoreType.DMA((6,))],
    )
    return normed_out, grad_gate, grad_key, grad_value, grad_filter, grad_bias[0]


def solution(mesh):
    wide, row = P("seq", "chan"), P("chan")
    return jax.shard_map(
        on_device,
        mesh=mesh,
        in_specs=(wide, wide, wide, wide, row, row, wide),
        out_specs=(wide, wide, wide, wide, wide, row),
        check_vma=False,
    )
```

```python
import jax
import jax.numpy as jnp
import numpy as np
from jax import lax
from jax.experimental import pallas as pl
from jax.experimental.pallas import tpu as pltpu
from jax.sharding import PartitionSpec as P

D = 4096
LENGTH = 8192
epsilon = 1e-05

f32, bf16 = jnp.float32, jnp.bfloat16

PARTS = 32
GROUP = 8
BLOCK = LENGTH // PARTS
WIDTH = D // GROUP
PIECE = WIDTH // PARTS
HALF = PIECE // 2
NEAR = BLOCK // 2
FULL = 2 * LENGTH
SPAN = 2 * PARTS
BINS = PARTS + 1
ROWS = BINS * PIECE
TAIL = 8
CHIPS = GROUP // 2


def tables():
    low = np.array(list(range(1, PARTS)) + [0, PARTS])
    block, inside, near = np.arange(PARTS), np.arange(BLOCK), np.arange(NEAR)
    outer = 2 * np.pi * (low[:, None] * block[None, :] % SPAN) / SPAN
    cosine, sine = np.cos(outer), np.sin(outer)
    eye = np.eye(HALF)
    enter = np.kron(np.concatenate([cosine, -sine[: PARTS - 1]], 0), eye)
    weight = np.where((low == 0) | (low == PARTS), 1.0, 2.0)[:, None] / 4
    leave = np.kron(np.concatenate([cosine * weight, (sine * weight)[: PARTS - 1]], 0).T, eye)
    into, back = [], []
    for odd in range(2):
        inner = 2 * np.pi * (near[:, None] * (2 * near[None, :] + odd) % BLOCK) / BLOCK
        cosine, sine = np.cos(inner) / 16, -np.sin(inner) / 16
        into.append(np.block([[cosine, sine], [-sine, cosine]]))
        back.append(np.block([[cosine.T, sine.T], [sine.T, -cosine.T]]))
    half = SPAN * HALF // 2
    steps = np.concatenate([*into, *back, leave, enter[:half], enter[half:]], 1)
    turn = 2 * np.pi * (low[:, None] * inside[None, :] % FULL) / FULL
    turn = np.stack([np.cos(turn), -np.sin(turn)])
    return steps.astype(np.float32).astype(bf16), turn.astype(np.float32)


def open_tables(steps_ref, turn_ref):
    blocks = [steps_ref[:, at * BLOCK : (at + 1) * BLOCK] for at in range(8)]
    turn = [
        jnp.broadcast_to(turn_ref[part][:, None, :], (BINS, HALF, BLOCK)).reshape(BINS * HALF, BLOCK)
        for part in range(2)
    ]
    enter, leave = jnp.concatenate(blocks[6:], 0), jnp.concatenate(blocks[4:6], 1)
    return enter, leave, blocks[:2], blocks[2:4], turn


def dot(first, second):
    return jnp.dot(first, second, preferred_element_type=f32)


def rotate(real, imag, turn):
    cosine, sine = turn
    own = imag.shape[0]
    turned_re = real[:own] * cosine[:own] - imag * sine[:own]
    turned_im = real[:own] * sine[:own] + imag * cosine[:own]
    turned_re = jnp.concatenate([turned_re, real[own:] * cosine[own:]], 0)
    turned_im = jnp.concatenate([turned_im, real[own:] * sine[own:]], 0)
    return turned_re, turned_im


def join(halves):
    parts = [half.reshape(BINS, HALF, NEAR) for half in halves]
    return jnp.concatenate(parts, 1).reshape(ROWS, NEAR).astype(bf16)


def enter_blocks(signal, enter):
    wide = signal.astype(f32)
    halves = [wide[:, half * HALF : (half + 1) * HALF].reshape(PARTS * HALF, BLOCK) for half in range(2)]
    return [dot(enter, half.astype(bf16)) for half in halves]


def finish_spectrum(halves, into, turn):
    pieces = ([], [], [], [])
    for mixed in halves:
        real, imag = rotate(mixed[: BINS * HALF], mixed[BINS * HALF :], turn)
        pieces[0].append(real[:, :NEAR] + real[:, NEAR:])
        pieces[1].append(imag[:, :NEAR] + imag[:, NEAR:])
        pieces[2].append(real[:, :NEAR] - real[:, NEAR:])
        pieces[3].append(imag[:, :NEAR] - imag[:, NEAR:])
    pieces = [join(piece) for piece in pieces]
    return [dot(jnp.concatenate(pieces[2 * odd : 2 * odd + 2], 1), into[odd]) for odd in range(2)]


def invert_inner(products, back):
    return [
        dot(jnp.concatenate([real.astype(bf16), imag.astype(bf16)], 1), matrix).reshape(BINS, PIECE, BLOCK)
        for (real, imag), matrix in zip(products, back, strict=True)
    ]


def finish_inverse(parts, leave, turn):
    outs = []
    for half in range(2):
        rows = slice(half * HALF, (half + 1) * HALF)
        even, odd = [part[:, rows].reshape(BINS * HALF, BLOCK) for part in parts]
        total, rest = even + odd, even - odd
        real = jnp.concatenate([total[:, :NEAR], rest[:, :NEAR]], 1)
        imag = jnp.concatenate([total[:, NEAR:], rest[:, NEAR:]], 1)
        own = (BINS - 2) * HALF
        turned_re = real * turn[0] - imag * turn[1]
        turned_im = real[:own] * turn[1][:own] + imag[:own] * turn[0][:own]
        turned = jnp.concatenate([turned_re, turned_im], 0).astype(bf16)
        outs.append(dot(leave, turned).reshape(PARTS, HALF, BLOCK))
    return jnp.concatenate(outs, 1)


def parts_of(values):
    return values[:, :NEAR], values[:, NEAR:]


def flat(pieces):
    return pieces.reshape(WIDTH, BLOCK)


def cut(rows):
    return rows.reshape(PARTS, PIECE, BLOCK)


def early_kernel(out_ref):
    out_ref[...] = jnp.zeros_like(out_ref)


def pack_kernel(key_ref, value_ref, taps_ref, after_ref, out_ref):
    mixed = (key_ref[...].astype(f32) * value_ref[...].astype(f32)).astype(bf16)
    out_ref[:, :PIECE, :] = cut(mixed.T)
    out_ref[:, PIECE:, :] = cut(taps_ref[...].T)


def forward_kernel(
    in_ref, steps_ref, turn_ref, gate_ref, cot_ref, pack_ref, skip_ref, gain_ref,
    out_ref, gate_out, scaled_out, skipped_out,
):
    gate = gate_ref[...].T
    gate_out[...] = gate
    scaled_out[...] = cot_ref[...].T.astype(f32) * column(gain_ref)
    skipped_out[...] = flat(pack_ref[:, :PIECE, :]).astype(f32) * column(skip_ref) * gate.astype(f32)
    enter, leave, into, back, turn = open_tables(steps_ref, turn_ref)
    first = enter_blocks(in_ref[:, :PIECE, :], enter)
    second = enter_blocks(in_ref[:, PIECE:, :], enter)
    first, second = [finish_spectrum(halves, into, turn) for halves in (first, second)]
    products = []
    for one, other in zip(first, second, strict=True):
        one_re, one_im = parts_of(one)
        other_re, other_im = parts_of(other)
        products.append((one_re * other_re - one_im * other_im, one_re * other_im + one_im * other_re))
    out_ref[...] = finish_inverse(invert_inner(products, back), leave, turn).astype(bf16)


def between_kernel(
    in_ref, steps_ref, turn_ref, key_ref, value_ref, skip_ref, conv_ref, gate_ref, scaled_ref, skipped_ref,
    gate_in, cot_in, gain_ref, after_ref, spec_ref, push_ref, hold_ref, norm_ref,
):
    gate, gated = gate_parts(conv_ref, gate_ref, skipped_ref)
    push_ref[...] = scaled_ref[...] * gate
    hold_ref[...] = gated * gate
    enter, _, into, _, turn = open_tables(steps_ref, turn_ref)
    for place in range(2):
        signal = in_ref[:, place * PIECE : (place + 1) * PIECE, :]
        even, odd = finish_spectrum(enter_blocks(signal, enter), into, turn)
        spec_ref[2 * place] = even
        spec_ref[2 * place + 1] = odd
    mixed = (key_ref[...].astype(f32) * value_ref[...].astype(f32)).astype(bf16)
    full = flat(conv_ref[...]).T.astype(f32) + skip_ref[...] * mixed.astype(f32)
    gate, scaled = gate_in[...].astype(f32), cot_in[...].astype(f32) * gain_ref[...]
    gated = gate * full
    for at, part in enumerate((gated * gain_ref[...], scaled * full, gated * full, scaled * gate, gated * gate)):
        norm_ref[at] = part


def column(row_ref):
    turned = jnp.broadcast_to(row_ref[...], (128, WIDTH)).T
    return jnp.concatenate([turned, turned], 1)


def gate_parts(conv_ref, gate_ref, skipped_ref):
    gate = gate_ref[...].astype(f32)
    return gate, gate * flat(conv_ref[...]).astype(f32) + skipped_ref[...]


def sums_kernel(conv_ref, gate_ref, scaled_ref, skipped_ref, out_ref):
    _, gated = gate_parts(conv_ref, gate_ref, skipped_ref)
    squares = jnp.sum(gated * gated, axis=0, keepdims=True)
    inner = jnp.sum(scaled_ref[...] * gated, axis=0, keepdims=True)
    out_ref[...] = jnp.concatenate([squares, inner], 0)


def norm_parts(sums_ref):
    sums = sums_ref[...]
    inv_rms = lax.rsqrt(sums[0:1] / D + epsilon)
    return inv_rms, inv_rms * inv_rms * inv_rms * sums[1:2] / D


def grad_kernel(sums_ref, push_ref, hold_ref, out_ref):
    inv_rms, pull = norm_parts(sums_ref)
    out_ref[...] = cut((inv_rms * push_ref[...] - pull * hold_ref[...]).astype(bf16))


def wide_column(row):
    turned = jnp.broadcast_to(row, (128, BLOCK)).T
    return jnp.concatenate([turned] * (WIDTH // 128), 1)


def backward_kernel(
    in_ref, pack_ref, spec_ref, steps_ref, turn_ref, sums_ref, norm_ref,
    out_ref, grad_out, normed_out, gate_out,
):
    inv_rms, pull = (wide_column(row) for row in norm_parts(sums_ref))
    normed_out[...] = (norm_ref[0] * inv_rms).astype(bf16)
    gate_out[...] = (norm_ref[1] * inv_rms - norm_ref[2] * pull).astype(bf16)
    grad_out[...] = (norm_ref[3] * inv_rms - norm_ref[4] * pull).astype(bf16)
    enter, leave, into, back, turn = open_tables(steps_ref, turn_ref)
    grad = in_ref[...]
    bias = jnp.sum(grad.astype(f32) * pack_ref[:, :PIECE, :].astype(f32), axis=0)
    bias = jnp.sum(bias, axis=1, keepdims=True)
    high = bias.astype(bf16).astype(f32)
    lane = lax.broadcasted_iota(jnp.int32, (TAIL, 128), 1)
    tail = jnp.zeros((TAIL, 128), f32)
    for at, part in enumerate((high[:HALF], (bias - high)[:HALF], high[HALF:], (bias - high)[HALF:])):
        tail = jnp.where(lane == at, part, tail)
    out_ref[:, 4 * PIECE :, :] = jnp.broadcast_to(tail.astype(bf16)[None], (PARTS, TAIL, 128))
    spectra = finish_spectrum(enter_blocks(grad, enter), into, turn)
    inverses = []
    for other in (1, 0):
        products = []
        for parity, mine in enumerate(spectra):
            real, imag = parts_of(spec_ref[2 * other + parity])
            mine_re, mine_im = parts_of(mine)
            products.append((real * mine_re + imag * mine_im, real * mine_im - imag * mine_re))
        inverses.append(invert_inner(products, back))
    for place, parts in enumerate(inverses):
        result = finish_inverse(parts, leave, turn).astype(bf16)
        out_ref[:, 2 * place * PIECE : (2 * place + 1) * PIECE, :] = result[:, :, :128]
        out_ref[:, (2 * place + 1) * PIECE : (2 * place + 2) * PIECE, :] = result[:, :, 128:]


def last_kernel(
    in_ref, grad_ref, key_ref, value_ref, skip_ref, normed_ref, gate_ref,
    key_hbm, value_hbm, taps_hbm, bias_hbm, normed_hbm, gate_hbm,
    key_out, value_out, taps_out, bias_out, sems,
):
    copies = []

    def send(source, target):
        copies.append(pltpu.make_async_copy(source, target, sems.at[len(copies)]))
        copies[-1].start()

    def whole(place):
        at = 2 * place * PIECE
        left, right = in_ref[:, at : at + PIECE, :], in_ref[:, at + PIECE : at + 2 * PIECE, :]
        return jnp.concatenate([left.reshape(WIDTH, 128).T, right.reshape(WIDTH, 128).T], 0)

    send(normed_ref, normed_hbm)
    send(gate_ref, gate_hbm)
    tail = in_ref[:, 4 * PIECE :, :].astype(f32)
    tail = jnp.concatenate([tail, pltpu.roll(tail, 126, 2)], 1).reshape(WIDTH, 128).T
    bias_out[...] = tail[0:1] + tail[1:2]
    taps_out[...] = whole(1)
    grad_mixed = whole(0).astype(f32) + skip_ref[...] * grad_ref[...].astype(f32)
    key_out[...] = (grad_mixed * value_ref[...].astype(f32)).astype(bf16)
    value_out[...] = (grad_mixed * key_ref[...].astype(f32)).astype(bf16)
    for source, target in ((bias_out, bias_hbm), (taps_out, taps_hbm), (key_out, key_hbm), (value_out, value_hbm)):
        send(source, target)
    for copy in copies:
        copy.wait()


def call(kernel, name, outs, *operands, cost=None, out_space=pltpu.VMEM, scratch=()):
    vmem = pl.BlockSpec(memory_space=pltpu.VMEM)
    return pl.pallas_call(
        kernel,
        name=name,
        out_shape=[jax.ShapeDtypeStruct(shape, kind) for shape, kind in outs],
        in_specs=[vmem] * len(operands),
        out_specs=[pl.BlockSpec(memory_space=out_space)] * len(outs),
        scratch_shapes=list(scratch),
        cost_estimate=cost,
        compiler_params=pltpu.CompilerParams(vmem_limit_bytes=32 * 1024 * 1024),
    )(*operands)


def add_over_pairs(sums):
    sums = sums + lax.ppermute(sums, "chan", [(at, at ^ 1) for at in range(GROUP)])
    return sums + lax.ppermute(sums, "chan", [(at, at ^ 2) for at in range(GROUP)])


def add_over_mirror(sums):
    mirror = [(at, (CHIPS - 1 - at // 2) * 2 + at % 2) for at in range(GROUP)]
    return sums + lax.ppermute(sums, "chan", mirror)


def on_device(gate_feat, key_feat, value_feat, filter_taps, skip_bias, norm_gain, cotangent):
    steps, turn = (jnp.asarray(table) for table in tables())
    skip_row, gain_row = skip_bias[None, :], norm_gain[None, :]
    natural = ((BLOCK, WIDTH), bf16)
    pieces = ((PARTS, PIECE, BLOCK), bf16)
    spectra = ((4, ROWS, BLOCK), f32)

    (token,) = call(
        early_kernel,
        "early",
        [((8, 128), f32)],
        cost=pl.CostEstimate(flops=2_000_000_000, bytes_accessed=4096, transcendentals=0),
    )
    (packed,) = call(
        pack_kernel, "pack", [((PARTS, 2 * PIECE, BLOCK), bf16)], key_feat, value_feat, filter_taps, token
    )
    arrived = lax.all_to_all(packed, "seq", 0, 0, tiled=True)
    conv, gate_t, scaled_t, skipped_t = call(
        forward_kernel,
        "forward",
        [pieces, ((WIDTH, BLOCK), bf16), ((WIDTH, BLOCK), f32), ((WIDTH, BLOCK), f32)],
        arrived,
        steps,
        turn,
        gate_feat,
        cotangent,
        packed,
        skip_row,
        gain_row,
    )
    conv = lax.all_to_all(conv, "seq", 0, 0, tiled=True)
    sides = (conv, gate_t, scaled_t, skipped_t)
    (sums,) = call(sums_kernel, "sums", [((2, BLOCK), f32)], *sides)
    sums = add_over_pairs(sums)
    spec, push, hold, norm = call(
        between_kernel,
        "between",
        [spectra, ((WIDTH, BLOCK), f32), ((WIDTH, BLOCK), f32), ((5, BLOCK, WIDTH), f32)],
        arrived,
        steps,
        turn,
        key_feat,
        value_feat,
        skip_row,
        *sides,
        gate_feat,
        cotangent,
        gain_row,
        sums,
    )
    sums = add_over_mirror(sums)
    (grad,) = call(grad_kernel, "grad", [pieces], sums, push, hold)
    grad_arrived = lax.all_to_all(grad, "seq", 0, 0, tiled=True)
    result, grad_conv, normed, gate = call(
        backward_kernel,
        "backward",
        [((PARTS, 4 * PIECE + TAIL, 128), bf16), natural, natural, natural],
        grad_arrived,
        arrived,
        spec,
        steps,
        turn,
        sums,
        norm,
    )
    result = lax.all_to_all(result, "seq", 0, 0, tiled=True)
    grad_key, grad_value, grad_filter, grad_bias, normed_out, grad_gate = call(
        last_kernel,
        "last",
        [natural] * 3 + [((1, WIDTH), f32)] + [natural] * 2,
        result,
        grad_conv,
        key_feat,
        value_feat,
        skip_row,
        normed,
        gate,
        out_space=pltpu.HBM,
        scratch=[pltpu.VMEM(*natural)] * 3 + [pltpu.VMEM((1, WIDTH), f32), pltpu.SemaphoreType.DMA((6,))],
    )
    return normed_out, grad_gate, grad_key, grad_value, grad_filter, grad_bias[0]


def solution(mesh):
    wide, row = P("seq", "chan"), P("chan")
    return jax.shard_map(
        on_device,
        mesh=mesh,
        in_specs=(wide, wide, wide, wide, row, row, wide),
        out_specs=(wide, wide, wide, wide, wide, row),
        check_vma=False,
    )
```

```python
import jax
import jax.numpy as jnp
import numpy as np
from jax import lax
from jax.experimental import pallas as pl
from jax.experimental.pallas import tpu as pltpu
from jax.sharding import PartitionSpec as P

D = 4096
LENGTH = 8192
epsilon = 1e-05

f32, bf16 = jnp.float32, jnp.bfloat16

PARTS = 32
GROUP = 8
BLOCK = LENGTH // PARTS
WIDTH = D // GROUP
PIECE = WIDTH // PARTS
HALF = PIECE // 2
NEAR = BLOCK // 2
FULL = 2 * LENGTH
SPAN = 2 * PARTS
BINS = PARTS + 1
ROWS = BINS * PIECE
TAIL = 8
CHIPS = GROUP // 2


def tables():
    low = np.array(list(range(1, PARTS)) + [0, PARTS])
    block, inside, near = np.arange(PARTS), np.arange(BLOCK), np.arange(NEAR)
    outer = 2 * np.pi * (low[:, None] * block[None, :] % SPAN) / SPAN
    cosine, sine = np.cos(outer), np.sin(outer)
    eye = np.eye(HALF)
    enter = np.kron(np.concatenate([cosine, -sine[: PARTS - 1]], 0), eye)
    weight = np.where((low == 0) | (low == PARTS), 1.0, 2.0)[:, None] / 4
    leave = np.kron(np.concatenate([cosine * weight, (sine * weight)[: PARTS - 1]], 0).T, eye)
    into, back = [], []
    for odd in range(2):
        inner = 2 * np.pi * (near[:, None] * (2 * near[None, :] + odd) % BLOCK) / BLOCK
        cosine, sine = np.cos(inner) / 16, -np.sin(inner) / 16
        into.append(np.block([[cosine, sine], [-sine, cosine]]))
        back.append(np.block([[cosine.T, sine.T], [sine.T, -cosine.T]]))
    half = SPAN * HALF // 2
    steps = np.concatenate([*into, *back, leave, enter[:half], enter[half:]], 1)
    turn = 2 * np.pi * (low[:, None] * inside[None, :] % FULL) / FULL
    turn = np.stack([np.cos(turn), -np.sin(turn)])
    return steps.astype(np.float32).astype(bf16), turn.astype(np.float32)


def open_tables(steps_ref, turn_ref):
    blocks = [steps_ref[:, at * BLOCK : (at + 1) * BLOCK] for at in range(8)]
    turn = [
        jnp.broadcast_to(turn_ref[part][:, None, :], (BINS, HALF, BLOCK)).reshape(BINS * HALF, BLOCK)
        for part in range(2)
    ]
    enter, leave = jnp.concatenate(blocks[6:], 0), jnp.concatenate(blocks[4:6], 1)
    return enter, leave, blocks[:2], blocks[2:4], turn


def dot(first, second):
    return jnp.dot(first, second, preferred_element_type=f32)


def rotate(real, imag, turn):
    cosine, sine = turn
    own = imag.shape[0]
    turned_re = real[:own] * cosine[:own] - imag * sine[:own]
    turned_im = real[:own] * sine[:own] + imag * cosine[:own]
    turned_re = jnp.concatenate([turned_re, real[own:] * cosine[own:]], 0)
    turned_im = jnp.concatenate([turned_im, real[own:] * sine[own:]], 0)
    return turned_re, turned_im


def join(halves):
    parts = [half.reshape(BINS, HALF, NEAR) for half in halves]
    return jnp.concatenate(parts, 1).reshape(ROWS, NEAR).astype(bf16)


def enter_blocks(signal, enter):
    wide = signal.astype(f32)
    halves = [wide[:, half * HALF : (half + 1) * HALF].reshape(PARTS * HALF, BLOCK) for half in range(2)]
    return [dot(enter, half.astype(bf16)) for half in halves]


def finish_spectrum(halves, into, turn):
    pieces = ([], [], [], [])
    for mixed in halves:
        real, imag = rotate(mixed[: BINS * HALF], mixed[BINS * HALF :], turn)
        pieces[0].append(real[:, :NEAR] + real[:, NEAR:])
        pieces[1].append(imag[:, :NEAR] + imag[:, NEAR:])
        pieces[2].append(real[:, :NEAR] - real[:, NEAR:])
        pieces[3].append(imag[:, :NEAR] - imag[:, NEAR:])
    pieces = [join(piece) for piece in pieces]
    return [dot(jnp.concatenate(pieces[2 * odd : 2 * odd + 2], 1), into[odd]) for odd in range(2)]


def invert_inner(products, back):
    return [
        dot(jnp.concatenate([real.astype(bf16), imag.astype(bf16)], 1), matrix).reshape(BINS, PIECE, BLOCK)
        for (real, imag), matrix in zip(products, back, strict=True)
    ]


def finish_inverse(parts, leave, turn):
    outs = []
    for half in range(2):
        rows = slice(half * HALF, (half + 1) * HALF)
        even, odd = [part[:, rows].reshape(BINS * HALF, BLOCK) for part in parts]
        total, rest = even + odd, even - odd
        real = jnp.concatenate([total[:, :NEAR], rest[:, :NEAR]], 1)
        imag = jnp.concatenate([total[:, NEAR:], rest[:, NEAR:]], 1)
        own = (BINS - 2) * HALF
        turned_re = real * turn[0] - imag * turn[1]
        turned_im = real[:own] * turn[1][:own] + imag[:own] * turn[0][:own]
        turned = jnp.concatenate([turned_re, turned_im], 0).astype(bf16)
        outs.append(dot(leave, turned).reshape(PARTS, HALF, BLOCK))
    return jnp.concatenate(outs, 1)


def parts_of(values):
    return values[:, :NEAR], values[:, NEAR:]


def flat(pieces):
    return pieces.reshape(WIDTH, BLOCK)


def cut(rows):
    return rows.reshape(PARTS, PIECE, BLOCK)


def early_kernel(out_ref):
    out_ref[...] = jnp.zeros_like(out_ref)


def pack_kernel(key_ref, value_ref, taps_ref, after_ref, out_ref):
    mixed = (key_ref[...].astype(f32) * value_ref[...].astype(f32)).astype(bf16)
    out_ref[:, :PIECE, :] = cut(mixed.T)
    out_ref[:, PIECE:, :] = cut(taps_ref[...].T)


def forward_kernel(
    in_ref, steps_ref, turn_ref, gate_ref, cot_ref, pack_ref, skip_ref, gain_ref,
    out_ref, gate_out, scaled_out, skipped_out,
):
    gate = gate_ref[...].T
    gate_out[...] = gate
    scaled_out[...] = cot_ref[...].T.astype(f32) * column(gain_ref)
    skipped_out[...] = flat(pack_ref[:, :PIECE, :]).astype(f32) * column(skip_ref) * gate.astype(f32)
    enter, leave, into, back, turn = open_tables(steps_ref, turn_ref)
    first = enter_blocks(in_ref[:, :PIECE, :], enter)
    second = enter_blocks(in_ref[:, PIECE:, :], enter)
    first, second = [finish_spectrum(halves, into, turn) for halves in (first, second)]
    products = []
    for one, other in zip(first, second, strict=True):
        one_re, one_im = parts_of(one)
        other_re, other_im = parts_of(other)
        products.append((one_re * other_re - one_im * other_im, one_re * other_im + one_im * other_re))
    out_ref[...] = finish_inverse(invert_inner(products, back), leave, turn).astype(bf16)


def between_kernel(
    in_ref, steps_ref, turn_ref, key_ref, value_ref, skip_ref, conv_ref, gate_ref, scaled_ref, skipped_ref,
    after_ref, spec_ref, full_ref, push_ref, hold_ref,
):
    gate, gated = gate_parts(conv_ref, gate_ref, skipped_ref)
    push_ref[...] = scaled_ref[...] * gate
    hold_ref[...] = gated * gate
    enter, _, into, _, turn = open_tables(steps_ref, turn_ref)
    for place in range(2):
        signal = in_ref[:, place * PIECE : (place + 1) * PIECE, :]
        even, odd = finish_spectrum(enter_blocks(signal, enter), into, turn)
        spec_ref[2 * place] = even
        spec_ref[2 * place + 1] = odd
    mixed = (key_ref[...].astype(f32) * value_ref[...].astype(f32)).astype(bf16)
    full_ref[...] = flat(conv_ref[...]).T.astype(f32) + skip_ref[...] * mixed.astype(f32)


def column(row_ref):
    turned = jnp.broadcast_to(row_ref[...], (128, WIDTH)).T
    return jnp.concatenate([turned, turned], 1)


def gate_parts(conv_ref, gate_ref, skipped_ref):
    gate = gate_ref[...].astype(f32)
    return gate, gate * flat(conv_ref[...]).astype(f32) + skipped_ref[...]


def sums_kernel(conv_ref, gate_ref, scaled_ref, skipped_ref, out_ref):
    _, gated = gate_parts(conv_ref, gate_ref, skipped_ref)
    squares = jnp.sum(gated * gated, axis=0, keepdims=True)
    inner = jnp.sum(scaled_ref[...] * gated, axis=0, keepdims=True)
    out_ref[...] = jnp.concatenate([squares, inner], 0)


def norm_parts(sums_ref):
    sums = sums_ref[...]
    inv_rms = lax.rsqrt(sums[0:1] / D + epsilon)
    return inv_rms, inv_rms * inv_rms * inv_rms * sums[1:2] / D


def grad_kernel(sums_ref, push_ref, hold_ref, out_ref):
    inv_rms, pull = norm_parts(sums_ref)
    out_ref[...] = cut((inv_rms * push_ref[...] - pull * hold_ref[...]).astype(bf16))


def wide_column(row):
    turned = jnp.broadcast_to(row, (128, BLOCK)).T
    return jnp.concatenate([turned] * (WIDTH // 128), 1)


def backward_kernel(
    in_ref, pack_ref, spec_ref, steps_ref, turn_ref, sums_ref, full_ref, gate_ref, cot_ref, gain_ref,
    out_ref, grad_out, normed_out, gate_out,
):
    inv_rms, pull = (wide_column(row) for row in norm_parts(sums_ref))
    full, gate, gain = full_ref[...], gate_ref[...].astype(f32), gain_ref[...]
    gated = gate * full
    normed_out[...] = (gated * inv_rms * gain).astype(bf16)
    grad_gated = inv_rms * (cot_ref[...].astype(f32) * gain) - gated * pull
    gate_out[...] = (grad_gated * full).astype(bf16)
    grad_out[...] = (grad_gated * gate).astype(bf16)
    enter, leave, into, back, turn = open_tables(steps_ref, turn_ref)
    grad = in_ref[...]
    bias = jnp.sum(grad.astype(f32) * pack_ref[:, :PIECE, :].astype(f32), axis=0)
    bias = jnp.sum(bias, axis=1, keepdims=True)
    high = bias.astype(bf16).astype(f32)
    lane = lax.broadcasted_iota(jnp.int32, (TAIL, 128), 1)
    tail = jnp.zeros((TAIL, 128), f32)
    for at, part in enumerate((high[:HALF], (bias - high)[:HALF], high[HALF:], (bias - high)[HALF:])):
        tail = jnp.where(lane == at, part, tail)
    out_ref[:, 4 * PIECE :, :] = jnp.broadcast_to(tail.astype(bf16)[None], (PARTS, TAIL, 128))
    spectra = finish_spectrum(enter_blocks(grad, enter), into, turn)
    inverses = []
    for other in (1, 0):
        products = []
        for parity, mine in enumerate(spectra):
            real, imag = parts_of(spec_ref[2 * other + parity])
            mine_re, mine_im = parts_of(mine)
            products.append((real * mine_re + imag * mine_im, real * mine_im - imag * mine_re))
        inverses.append(invert_inner(products, back))
    for place, parts in enumerate(inverses):
        result = finish_inverse(parts, leave, turn).astype(bf16)
        out_ref[:, 2 * place * PIECE : (2 * place + 1) * PIECE, :] = result[:, :, :128]
        out_ref[:, (2 * place + 1) * PIECE : (2 * place + 2) * PIECE, :] = result[:, :, 128:]


def last_kernel(
    in_ref, grad_ref, key_ref, value_ref, skip_ref, normed_ref, gate_ref,
    key_hbm, value_hbm, taps_hbm, bias_hbm, normed_hbm, gate_hbm,
    key_out, value_out, taps_out, bias_out, sems,
):
    copies = []

    def send(source, target):
        copies.append(pltpu.make_async_copy(source, target, sems.at[len(copies)]))
        copies[-1].start()

    def whole(place):
        at = 2 * place * PIECE
        left, right = in_ref[:, at : at + PIECE, :], in_ref[:, at + PIECE : at + 2 * PIECE, :]
        return jnp.concatenate([left.reshape(WIDTH, 128).T, right.reshape(WIDTH, 128).T], 0)

    send(normed_ref, normed_hbm)
    send(gate_ref, gate_hbm)
    tail = in_ref[:, 4 * PIECE :, :].astype(f32)
    tail = jnp.concatenate([tail, pltpu.roll(tail, 126, 2)], 1).reshape(WIDTH, 128).T
    bias_out[...] = tail[0:1] + tail[1:2]
    taps_out[...] = whole(1)
    grad_mixed = whole(0).astype(f32) + skip_ref[...] * grad_ref[...].astype(f32)
    key_out[...] = (grad_mixed * value_ref[...].astype(f32)).astype(bf16)
    value_out[...] = (grad_mixed * key_ref[...].astype(f32)).astype(bf16)
    for source, target in ((bias_out, bias_hbm), (taps_out, taps_hbm), (key_out, key_hbm), (value_out, value_hbm)):
        send(source, target)
    for copy in copies:
        copy.wait()


def call(kernel, name, outs, *operands, cost=None, out_space=pltpu.VMEM, scratch=()):
    vmem = pl.BlockSpec(memory_space=pltpu.VMEM)
    return pl.pallas_call(
        kernel,
        name=name,
        out_shape=[jax.ShapeDtypeStruct(shape, kind) for shape, kind in outs],
        in_specs=[vmem] * len(operands),
        out_specs=[pl.BlockSpec(memory_space=out_space)] * len(outs),
        scratch_shapes=list(scratch),
        cost_estimate=cost,
        compiler_params=pltpu.CompilerParams(vmem_limit_bytes=32 * 1024 * 1024),
    )(*operands)


def add_over_mirror(sums):
    sums = sums + lax.ppermute(sums, "chan", [(at, at ^ 1) for at in range(GROUP)])
    mirror = [(at, (CHIPS - 1 - at // 2) * 2 + at % 2) for at in range(GROUP)]
    return sums + lax.ppermute(sums, "chan", mirror)


def add_over_pairs(sums):
    return sums + lax.ppermute(sums, "chan", [(at, at ^ 2) for at in range(GROUP)])


def on_device(gate_feat, key_feat, value_feat, filter_taps, skip_bias, norm_gain, cotangent):
    steps, turn = (jnp.asarray(table) for table in tables())
    skip_row, gain_row = skip_bias[None, :], norm_gain[None, :]
    natural = ((BLOCK, WIDTH), bf16)
    pieces = ((PARTS, PIECE, BLOCK), bf16)
    spectra = ((4, ROWS, BLOCK), f32)

    (token,) = call(
        early_kernel,
        "early",
        [((8, 128), f32)],
        cost=pl.CostEstimate(flops=2_000_000_000, bytes_accessed=4096, transcendentals=0),
    )
    (packed,) = call(
        pack_kernel, "pack", [((PARTS, 2 * PIECE, BLOCK), bf16)], key_feat, value_feat, filter_taps, token
    )
    arrived = lax.all_to_all(packed, "seq", 0, 0, tiled=True)
    conv, gate_t, scaled_t, skipped_t = call(
        forward_kernel,
        "forward",
        [pieces, ((WIDTH, BLOCK), bf16), ((WIDTH, BLOCK), f32), ((WIDTH, BLOCK), f32)],
        arrived,
        steps,
        turn,
        gate_feat,
        cotangent,
        packed,
        skip_row,
        gain_row,
    )
    conv = lax.all_to_all(conv, "seq", 0, 0, tiled=True)
    sides = (conv, gate_t, scaled_t, skipped_t)
    (sums,) = call(sums_kernel, "sums", [((2, BLOCK), f32)], *sides)
    sums = add_over_mirror(sums)
    spec, full, push, hold = call(
        between_kernel,
        "between",
        [spectra, ((BLOCK, WIDTH), f32), ((WIDTH, BLOCK), f32), ((WIDTH, BLOCK), f32)],
        arrived,
        steps,
        turn,
        key_feat,
        value_feat,
        skip_row,
        *sides,
        sums,
    )
    sums = add_over_pairs(sums)
    (grad,) = call(grad_kernel, "grad", [pieces], sums, push, hold)
    grad_arrived = lax.all_to_all(grad, "seq", 0, 0, tiled=True)
    result, grad_conv, normed, gate = call(
        backward_kernel,
        "backward",
        [((PARTS, 4 * PIECE + TAIL, 128), bf16), natural, natural, natural],
        grad_arrived,
        arrived,
        spec,
        steps,
        turn,
        sums,
        full,
        gate_feat,
        cotangent,
        gain_row,
    )
    result = lax.all_to_all(result, "seq", 0, 0, tiled=True)
    grad_key, grad_value, grad_filter, grad_bias, normed_out, grad_gate = call(
        last_kernel,
        "last",
        [natural] * 3 + [((1, WIDTH), f32)] + [natural] * 2,
        result,
        grad_conv,
        key_feat,
        value_feat,
        skip_row,
        normed,
        gate,
        out_space=pltpu.HBM,
        scratch=[pltpu.VMEM(*natural)] * 3 + [pltpu.VMEM((1, WIDTH), f32), pltpu.SemaphoreType.DMA((6,))],
    )
    return normed_out, grad_gate, grad_key, grad_value, grad_filter, grad_bias[0]


def solution(mesh):
    wide, row = P("seq", "chan"), P("chan")
    return jax.shard_map(
        on_device,
        mesh=mesh,
        in_specs=(wide, wide, wide, wide, row, row, wide),
        out_specs=(wide, wide, wide, wide, wide, row),
        check_vma=False,
    )
```
